32 devices in a mesh: section: 4 (over x, core), ctx: 8 (over z, y).
Axes of the slice: x: 2, y: 2, z: 4, core: 2. Of those that a mesh axis runs over, the one named last changes fastest.
Arguments:
- handoff: bfloat16 [4, 2, 768, 4096], P('section', None, 'ctx'), may hold values from -500 to 500
- norm_gain: bfloat16 [4, 4096], P('section'), may hold values from 0.099609375 to 1.8984375
- kv_weight: bfloat16 [4, 4096, 1024], P('section', 'ctx'), may hold values from -0.09375 to 0.09375
- queries: bfloat16 [4, 2, 768, 4096], P('section', None, 'ctx'), may hold values from -120 to 120
- span_order: int32 [2, 16], replicated, may hold values from 0 to 15, each once within a row
Outputs:
- partial_out: bfloat16 [4, 2, 768, 4096], P('section', None, 'ctx')
- log_sum: float32 [4, 2, 32, 768], P('section', None, None, 'ctx')
The draws below stay inside these ranges and needn't reach their ends.
Inputs may be any that keep to these rules, and one draw needn't show every extreme that they name: Each row of span_order names every span of 0 to 15 once.
All inputs are finite; a program needn't handle non-finite values.
Results may differ from the reference program's by a relative error of at most 0.012.
The reference program's roundings to bfloat16 on the way count: a program that leaves them out, or rounds other values in their place, can miss the bound.
Values may be sent and summed in bfloat16 or wider, within the bound.
No kernel may reach another device: no remote copies, remote signals or barrier semaphores. Data moves between devices by JAX's collectives and lax.ppermute only.
A program may use at most 64 MiB of HBM per device.

```python
import math
import jax
import jax.numpy as jnp
from jax import lax

D = 4096
QH = 32
KVH = 4
HD = 128
TOK = 96
MB = 2
WINDOW = 4
SECTIONS = 4
SPAN = 48
SPANS = 16
SEQ = 768
N_CTX = 8


def draw_handoff(key, part):
    base_key = jax.random.fold_in(key, 11)
    noise_key, row_key, col_key = jax.random.split(base_key, 3)
    row_scale = jnp.exp(jax.random.uniform(row_key, (SECTIONS, MB, SEQ, 1), jnp.float32, 0.0, math.log(10.0)))
    col_scale = jnp.exp(jax.random.uniform(col_key, (SECTIONS, 1, 1, D), jnp.float32, 0.0, math.log(10.0)))
    noise_vals = jnp.clip(jax.random.normal(noise_key, (SECTIONS, MB, SEQ, D), jnp.float32), -5.0, 5.0)
    return (noise_vals * row_scale * col_scale).astype(jnp.bfloat16)


def draw_queries(key, part):
    base_key = jax.random.fold_in(key, 23)
    noise_key = jax.random.fold_in(base_key, 0)
    values = 3.0 * jnp.clip(jax.random.normal(noise_key, (SECTIONS, MB, SEQ, QH, HD), jnp.float32), -5.0, 5.0)
    return values.reshape(SECTIONS, MB, SEQ, QH * HD).astype(jnp.bfloat16)


def levels(key, extent, cuts, least, high):
    gain, own = 1.0, jax.random.fold_in(key, 6)
    for position, shards_of in cuts:
        steps = jnp.exp(jax.random.uniform(jax.random.fold_in(own, position), (shards_of,), jnp.float32, least / len(cuts), high / len(cuts)))
        gain = gain * jnp.repeat(steps, extent[position] // shards_of).reshape([-1 if axis == position else 1 for axis in range(len(extent))])
    return gain


def centred(own_key, dims, width, bound, pieces=(), kind=jnp.bfloat16):
    loudness = levels(own_key, dims, pieces, -0.22, 0.18) if pieces else 1.0
    values = jax.random.normal(own_key, dims, jnp.float32) * width * loudness
    return jnp.minimum(jnp.maximum(values, -bound), bound).astype(kind)


def setup_inputs(seed: int = 0) -> dict:
    seeds = jax.random.split(jax.random.key(seed), 6)
    return {
        "handoff": draw_handoff(jax.random.fold_in(seeds[5], 71), 0),
        "norm_gain": jnp.clip(1.0 + 0.18 * jax.random.normal(seeds[1], (SECTIONS, D), jnp.float32), 0.099609375, 1.8984375).astype(jnp.bfloat16),
        "kv_weight": centred(seeds[2], (SECTIONS, D, 2 * KVH * HD), D ** -0.5, 0.09375, ((0, 4), (1, 8))),
        "queries": draw_queries(jax.random.fold_in(seeds[5], 71), 0),
        "span_order": jax.vmap(lambda own: jax.random.permutation(own, SPANS))(jax.random.split(seeds[4], MB)).reshape((MB, SPANS)).astype(jnp.int32),
    }


rope_base = 500000.0

def rotate(key_vecs, positions):
    half_dim = key_vecs.shape[-1] // 2
    frequency = rope_base ** (-2.0 * jnp.arange(half_dim, dtype=jnp.float32) / key_vecs.shape[-1])
    angles = positions.astype(jnp.float32)[..., None, None] * frequency
    cosine = jnp.cos(angles)
    sine_part = jnp.sin(angles)
    first_half = key_vecs[..., :half_dim]
    second = key_vecs[..., half_dim:]
    return jnp.concatenate([first_half * cosine - second * sine_part, second * cosine + first_half * sine_part], axis=-1)

def reference(handoff, norm_gain, kv_weight, queries, span_order):
    layer_in = jnp.roll(handoff, 1, axis=0)
    offsets = (jnp.arange(SEQ) % SPAN).astype(jnp.int32)
    slots = (jnp.arange(SEQ) // SPAN).astype(jnp.int32)
    positions = (span_order[:, slots] * SPAN + offsets[None, :]).astype(jnp.int32)
    key_pos = positions.reshape(MB, N_CTX, TOK)
    window_pos = jnp.concatenate([jnp.roll(key_pos, step_num, axis=1) for step_num in range(WINDOW)], axis=2)
    group_size = QH // KVH

    def one_section(inputs):
        section_in, section_gain, weight, query_block = inputs
        activations = section_in.astype(jnp.float32)
        scale = lax.rsqrt(lax.optimization_barrier(jnp.mean(activations * activations, axis=-1, keepdims=True)) + 1e-05)
        normed = (activations * scale * section_gain.astype(jnp.float32)).astype(jnp.bfloat16)
        kv_rows = jnp.dot(normed.reshape(MB * SEQ, D), weight, preferred_element_type=jnp.float32)
        kv_rows = kv_rows.reshape(MB, SEQ, 2, KVH, HD)
        key_block = rotate(kv_rows[:, :, 0], positions).astype(jnp.bfloat16).reshape(MB, N_CTX, TOK, KVH, HD)
        value_block = kv_rows[:, :, 1].astype(jnp.bfloat16).reshape(MB, N_CTX, TOK, KVH, HD)
        window_keys = jnp.concatenate([jnp.roll(key_block, step_num, axis=1) for step_num in range(WINDOW)], axis=2)
        window_values = jnp.concatenate([jnp.roll(value_block, step_num, axis=1) for step_num in range(WINDOW)], axis=2)
        query_rows = query_block.reshape(MB, N_CTX, TOK, KVH, group_size, HD).astype(jnp.float32)
        scores = jnp.einsum('mctkgd,mcukd->mckgtu', query_rows, window_keys.astype(jnp.float32)) * HD ** (-0.5)
        visible = window_pos[:, :, None, None, None, :] <= key_pos[:, :, None, None, :, None]
        scores = jnp.where(visible, scores, -jnp.inf)
        row_max = lax.optimization_barrier(jnp.max(scores, axis=-1, keepdims=True))
        exps = jnp.exp(scores - row_max)
        running = lax.optimization_barrier(jnp.sum(exps, axis=-1, keepdims=True))
        log_sums = (row_max + jnp.log(running))[..., 0]
        weights_bf = lax.optimization_barrier(exps.astype(jnp.bfloat16))
        mixed = jnp.einsum('mckgtu,mcukd->mctkgd', weights_bf.astype(jnp.float32), window_values.astype(jnp.float32))
        denominator = jnp.moveaxis(running[..., 0], 4, 2)[..., None]
        result = (mixed / denominator).astype(jnp.bfloat16).reshape(MB, SEQ, QH * HD)
        log_result = jnp.transpose(log_sums, (0, 2, 3, 1, 4)).reshape(MB, QH, SEQ)
        return (result, log_result)
    partial_out, log_sum = lax.map(one_section, (layer_in, norm_gain, kv_weight, queries))
    return (partial_out, log_sum)
```

```python
import jax
import jax.numpy as jnp
from jax import lax
from jax.sharding import PartitionSpec as P

QH = 32
KVH = 4
HD = 128
WINDOW = 4
QUAD = 4


rope_base = 500000.0


def moved(block, axis, target):
    size = lax.axis_size(axis)
    return lax.ppermute(block, axis, [(i, target(i) % size) for i in range(size)])


def rope_tables(positions):
    half_dim = HD // 2
    frequency = rope_base ** (-2.0 * jnp.arange(half_dim, dtype=jnp.float32) / HD)
    angles = positions.astype(jnp.float32)[..., None, None] * frequency
    return jnp.cos(angles), jnp.sin(angles)


def rotate(key_vecs, tables):
    cosine, sine_part = tables
    half_dim = HD // 2
    first_half = key_vecs[..., :half_dim]
    second = key_vecs[..., half_dim:]
    return jnp.concatenate(
        [first_half * cosine - second * sine_part, second * cosine + first_half * sine_part],
        axis=-1,
    )


def on_device(handoff, norm_gain, kv_weight, queries, span_order):
    sections = lax.axis_size("section")
    cycle_size = lax.axis_size("ctx")
    own_index = lax.axis_index("ctx")
    quads = cycle_size // QUAD
    own_quad, own_place = own_index // QUAD, own_index % QUAD
    weight = kv_weight[0]
    shard_rows, kv_width = weight.shape[0], weight.shape[1] // 2
    _, micro_count, tok_rows, model_width = handoff.shape
    rows = micro_count * tok_rows

    def same_place_shards(part):
        return [part] + [
            moved(part, "ctx", lambda i, j=j: i + QUAD * j) for j in range(1, quads)
        ]

    key_shards = same_place_shards(weight[:, :kv_width])

    next_gain = moved(norm_gain, "section", lambda i: i - 1)
    activations = handoff[0].astype(jnp.float32)
    scale = lax.rsqrt(jnp.mean(activations * activations, axis=-1, keepdims=True) + 1e-05)
    normed = (activations * scale * next_gain[0].astype(jnp.float32)).astype(jnp.bfloat16)
    normed = normed.reshape(rows, model_width)

    def to_next_section(part, flip):
        route = [
            (s * cycle_size + i, (s + 1) % sections * cycle_size + (i ^ flip))
            for s in range(sections)
            for i in range(cycle_size)
        ]
        return lax.ppermute(part, ("section", "ctx"), route)

    arrived = []
    for flip in range(QUAD):
        pieces = [
            lax.dynamic_slice_in_dim(
                normed,
                ((own_quad - j) % quads * QUAD + (own_place ^ flip)) * shard_rows,
                shard_rows,
                1,
            )
            for j in range(quads)
        ]
        arrived.append(to_next_section(jnp.concatenate(pieces, axis=1), flip))
    flat_rows = jnp.concatenate(arrived, axis=0)

    def partial_product(shards):
        total = 0.0
        for j, shard in enumerate(shards):
            total = total + jnp.dot(
                flat_rows[:, j * shard_rows : (j + 1) * shard_rows],
                shard,
                preferred_element_type=jnp.float32,
            )
        return total

    def own_rows_total(product):
        total = product[:rows]
        for flip in range(1, QUAD):
            part = product[flip * rows : (flip + 1) * rows].astype(jnp.bfloat16)
            total = total + moved(part, "ctx", lambda i, flip=flip: i ^ flip).astype(jnp.float32)
        return total

    def window_of(block):
        two_back = moved(block, "ctx", lambda i: i + 2)
        beside = moved(two_back, "ctx", lambda i: i ^ 1)
        onward = jnp.where(own_index % 2 == 0, block, two_back)
        last = moved(onward, "ctx", lambda i: i + 1)
        return jnp.concatenate([block, two_back, beside, last], axis=1)

    odd = own_index % 2
    distances = [0, 2, 1 + 2 * odd, 3 - 2 * odd]
    span_len = tok_rows // 2

    def device_positions(device):
        span_ids = lax.dynamic_slice_in_dim(span_order, 2 * device, 2, 1)
        spread = (
            span_ids[:, :, None] * span_len + jnp.arange(span_len, dtype=jnp.int32)[None, None, :]
        )
        return spread.reshape(micro_count, tok_rows)

    own_pos = device_positions(own_index)
    window_pos = jnp.concatenate(
        [device_positions((own_index - d) % cycle_size) for d in distances], axis=1
    )
    tables = rope_tables(own_pos)

    key_total = own_rows_total(partial_product(key_shards))
    value_part, _ = lax.optimization_barrier((weight[:, kv_width:], key_shards[-1]))
    value_shards = same_place_shards(value_part)
    key_vecs = rotate(key_total.reshape(micro_count, tok_rows, KVH, HD), tables)
    key_block = key_vecs.reshape(micro_count, tok_rows, kv_width).astype(jnp.bfloat16)
    window_keys = window_of(key_block)

    group_size = QH // KVH
    query_block = queries[0].reshape(micro_count, tok_rows, KVH, group_size, HD)
    weights, sums, log_sums = [], [], []
    for micro_idx in range(micro_count):
        key_rows = window_keys[micro_idx].reshape(-1, KVH, HD)
        scores = jnp.einsum(
            "tkgd,ukd->kgtu", query_block[micro_idx], key_rows, preferred_element_type=jnp.float32
        ) * HD ** (-0.5)
        visible = (
            window_pos[micro_idx][None, None, None, :] <= own_pos[micro_idx][None, None, :, None]
        )
        scores = jnp.where(visible, scores, -jnp.inf)
        row_max = jnp.max(scores, axis=-1, keepdims=True)
        exps = jnp.exp(scores - row_max)
        running = jnp.sum(exps, axis=-1, keepdims=True)
        weights.append(exps.astype(jnp.bfloat16))
        sums.append(jnp.moveaxis(running[..., 0], 2, 0)[..., None])
        log_sums.append((row_max + jnp.log(running))[..., 0].reshape(QH, tok_rows))

    value_total = own_rows_total(partial_product(value_shards))
    value_block = value_total.astype(jnp.bfloat16).reshape(micro_count, tok_rows, kv_width)
    window_values = window_of(value_block)
    results = []
    for micro_idx in range(micro_count):
        value_rows = window_values[micro_idx].reshape(-1, KVH, HD)
        mixed = jnp.einsum(
            "kgtu,ukd->tkgd", weights[micro_idx], value_rows, preferred_element_type=jnp.float32
        )
        results.append((mixed / sums[micro_idx]).astype(jnp.bfloat16).reshape(tok_rows, QH * HD))
    return (jnp.stack(results)[None], jnp.stack(log_sums)[None])


def solution(mesh):
    placed = (
        P("section", None, "ctx", None),
        P("section", None),
        P("section", "ctx", None),
        P("section", None, "ctx", None),
        P(),
    )
    return jax.shard_map(
        on_device,
        mesh=mesh,
        in_specs=placed,
        out_specs=(P("section", None, "ctx", None), P("section", None, None, "ctx")),
        check_vma=False,
    )
```

```python
import jax
import jax.numpy as jnp
from jax import lax
from jax.experimental import pallas as pl
from jax.experimental.pallas import tpu as pltpu
from jax.sharding import PartitionSpec as P

QH = 32
KVH = 4
HD = 128
WINDOW = 4
QUAD = 4
GROUP = QH // KVH
LANES = 128
ROW_STEP = 16


rope_base = 500000.0


def moved(block, axis, target):
    size = lax.axis_size(axis)
    return lax.ppermute(block, axis, [(i, target(i) % size) for i in range(size)])


def params(mib):
    return pltpu.CompilerParams(vmem_limit_bytes=mib * 1024 * 1024)


def cost(flops, bytes_accessed):
    return pl.CostEstimate(flops=flops, bytes_accessed=bytes_accessed, transcendentals=0)


def norm_kernel(starts_ref, x_ref, gain_ref, *outs):
    rows, width = x_ref.shape[1], x_ref.shape[2]
    pieces = starts_ref.shape[1]
    piece_width = outs[0].shape[1] // pieces
    for r in range(0, rows, ROW_STEP):
        x = x_ref[0, r : r + ROW_STEP, :].astype(jnp.float32)
        scale = lax.rsqrt(jnp.sum(x * x, axis=-1, keepdims=True) / width + 1e-05)
        for flip, out in enumerate(outs):
            for j in range(pieces):
                start = pl.multiple_of(starts_ref[flip, j], LANES)
                xs = x_ref[0, r : r + ROW_STEP, pl.ds(start, piece_width)].astype(jnp.float32)
                gain = gain_ref[:, pl.ds(start, piece_width)]
                out[r : r + ROW_STEP, j * piece_width : (j + 1) * piece_width] = (
                    xs * scale * gain
                ).astype(jnp.bfloat16)


def normed_cuts(activations, gain, starts):
    micro_count, tok_rows, width = activations.shape
    rows = micro_count * tok_rows
    part = width // QUAD
    return pl.pallas_call(
        norm_kernel,
        grid=(micro_count,),
        in_specs=[
            pl.BlockSpec(memory_space=pltpu.SMEM),
            pl.BlockSpec((1, tok_rows, width), lambda m: (m, 0, 0)),
            pl.BlockSpec((1, width), lambda m: (0, 0)),
        ],
        out_specs=[pl.BlockSpec((tok_rows, part), lambda m: (m, 0))] * QUAD,
        out_shape=[jax.ShapeDtypeStruct((rows, part), jnp.bfloat16)] * QUAD,
        compiler_params=params(16),
        cost_estimate=cost(6 * rows * width, 4 * rows * width),
        name="norm_cuts",
    )(starts, activations, gain)


def product_kernel(quads, *refs):
    xs, shards, outs = refs[:QUAD], refs[QUAD : QUAD + quads], refs[QUAD + quads :]
    shard_rows = shards[0].shape[0]
    for x, out in zip(xs, outs):
        total = jnp.dot(x[:, :shard_rows], shards[0][...], preferred_element_type=jnp.float32)
        for j in range(1, quads):
            total = total + jnp.dot(
                x[:, j * shard_rows : (j + 1) * shard_rows],
                shards[j][...],
                preferred_element_type=jnp.float32,
            )
        out[...] = total.astype(out.dtype)


def partial_products(xs, shards):
    rows, part = xs[0].shape
    width = shards[0].shape[1]
    return pl.pallas_call(
        lambda *refs: product_kernel(len(shards), *refs),
        out_shape=[jax.ShapeDtypeStruct((rows, width), jnp.float32)]
        + [jax.ShapeDtypeStruct((rows, width), jnp.bfloat16)] * (QUAD - 1),
        compiler_params=params(24),
        cost_estimate=cost(2 * QUAD * rows * part * width, 2 * QUAD * rows * part + 2 * part * width),
        name="partial_products",
    )(*xs, *shards)


def added(own, one, two, three):
    return own + one.astype(jnp.float32) + two.astype(jnp.float32) + three.astype(jnp.float32)


def key_sum_kernel(own, one, two, three, cosine, sine_part, out):
    for h in range(out.shape[1] // HD):
        cols = slice(h * HD, (h + 1) * HD)
        total = added(own[:, cols], one[:, cols], two[:, cols], three[:, cols])
        turned = pltpu.roll(total, HD // 2, 1)
        out[:, cols] = (total * cosine[...] + turned * sine_part[...]).astype(jnp.bfloat16)


def value_sum_kernel(own, one, two, three, out):
    out[...] = added(own[...], one[...], two[...], three[...]).astype(jnp.bfloat16)


def block_sum(kernel, name, own, parts, *tables):
    return pl.pallas_call(
        kernel,
        out_shape=jax.ShapeDtypeStruct(own.shape, jnp.bfloat16),
        compiler_params=params(16),
        cost_estimate=cost(10 * own.size, 12 * own.size),
        name=name,
    )(own, *parts, *tables)


def stacked(refs, odd):
    own, two_back, three_back, beside, from_even = refs
    one_back = jnp.where(odd == 1, beside[...], from_even[...])
    return jnp.concatenate([own[...], one_back, two_back[...], three_back[...]], axis=0)


def score_kernel(odd_ref, q_ref, *refs):
    key_refs, (row_pos, col_pos, weights, sums, log_sums) = refs[:5], refs[5:]
    keys = stacked(key_refs, odd_ref[0])
    tok_rows = q_ref.shape[2]
    visible = col_pos[0] <= row_pos[0]
    lane = lax.broadcasted_iota(jnp.int32, (tok_rows, LANES), 1)
    all_sums = jnp.ones((tok_rows, LANES), jnp.float32)
    all_max = jnp.zeros((tok_rows, LANES), jnp.float32)
    for h in range(GROUP):
        scores = lax.dot_general(
            q_ref[0, 0, :, h * HD : (h + 1) * HD],
            keys,
            (((1,), (1,)), ((), ())),
            preferred_element_type=jnp.float32,
        ) * HD ** (-0.5)
        scores = jnp.where(visible, scores, -jnp.inf)
        row_max = jnp.max(scores, axis=-1, keepdims=True)
        exps = jnp.exp(scores - row_max)
        running = jnp.sum(exps, axis=-1, keepdims=True)
        weights[0, 0, h * tok_rows : (h + 1) * tok_rows, :] = exps.astype(jnp.bfloat16)
        all_sums = jnp.where(lane == h, running, all_sums)
        all_max = jnp.where(lane == h, row_max, all_max)
    sums[0, 0] = all_sums
    log_sums[0] = jnp.transpose(all_max + jnp.log(all_sums))[:GROUP]


def window_specs(tok_rows):
    return [pl.BlockSpec((tok_rows, HD), lambda m, k: (m, k))] * 5


def scored(odd, queries, window, row_pos, col_pos):
    _, micro_count, tok_rows, width = queries.shape
    keys = WINDOW * tok_rows
    return pl.pallas_call(
        score_kernel,
        grid=(micro_count, KVH),
        in_specs=[
            pl.BlockSpec(memory_space=pltpu.SMEM),
            pl.BlockSpec((1, 1, tok_rows, GROUP * HD), lambda m, k: (0, m, 0, k)),
            *window_specs(tok_rows),
            pl.BlockSpec((1, tok_rows, 1), lambda m, k: (m, 0, 0)),
            pl.BlockSpec((1, 1, keys), lambda m, k: (m, 0, 0)),
        ],
        out_specs=[
            pl.BlockSpec((1, 1, GROUP * tok_rows, keys), lambda m, k: (m, k, 0, 0)),
            pl.BlockSpec((1, 1, tok_rows, LANES), lambda m, k: (m, k, 0, 0)),
            pl.BlockSpec((1, GROUP, tok_rows), lambda m, k: (m, k, 0)),
        ],
        out_shape=[
            jax.ShapeDtypeStruct((micro_count, KVH, GROUP * tok_rows, keys), jnp.bfloat16),
            jax.ShapeDtypeStruct((micro_count, KVH, tok_rows, LANES), jnp.float32),
            jax.ShapeDtypeStruct((micro_count, QH, tok_rows), jnp.float32),
        ],
        compiler_params=params(24),
        cost_estimate=cost(2 * micro_count * QH * tok_rows * keys * HD, 8 * 2**20),
        name="scores",
    )(odd, queries, *window, row_pos, col_pos)


def mix_kernel(odd_ref, weights, sums, *refs):
    values = stacked(refs[:5], odd_ref[0])
    out = refs[5]
    tok_rows = out.shape[2]
    mixed = jnp.dot(weights[0, 0], values, preferred_element_type=jnp.float32)
    share = 1.0 / sums[0, 0]
    for h in range(GROUP):
        out[0, 0, :, h * HD : (h + 1) * HD] = (
            mixed[h * tok_rows : (h + 1) * tok_rows] * share[:, h : h + 1]
        ).astype(jnp.bfloat16)


def mixed_values(odd, weights, sums, window):
    micro_count, _, group_rows, keys = weights.shape
    tok_rows = group_rows // GROUP
    return pl.pallas_call(
        mix_kernel,
        grid=(micro_count, KVH),
        in_specs=[
            pl.BlockSpec(memory_space=pltpu.SMEM),
            pl.BlockSpec((1, 1, group_rows, keys), lambda m, k: (m, k, 0, 0)),
            pl.BlockSpec((1, 1, tok_rows, LANES), lambda m, k: (m, k, 0, 0)),
            *window_specs(tok_rows),
        ],
        out_specs=pl.BlockSpec((1, 1, tok_rows, GROUP * HD), lambda m, k: (0, m, 0, k)),
        out_shape=jax.ShapeDtypeStruct((1, micro_count, tok_rows, QH * HD), jnp.bfloat16),
        compiler_params=params(24),
        cost_estimate=cost(2 * micro_count * QH * tok_rows * keys * HD, 8 * 2**20),
        name="mixed_values",
    )(odd, weights, sums, *window)


def on_device(handoff, norm_gain, kv_weight, queries, span_order):
    sections = lax.axis_size("section")
    cycle_size = lax.axis_size("ctx")
    own_index = lax.axis_index("ctx")
    quads = cycle_size // QUAD
    own_quad, own_place = own_index // QUAD, own_index % QUAD
    weight = kv_weight[0]
    shard_rows, kv_width = weight.shape[0], weight.shape[1] // 2
    _, micro_count, tok_rows, _ = handoff.shape

    def same_place_shards(part):
        return [part] + [
            moved(part, "ctx", lambda i, j=j: i + QUAD * j) for j in range(1, quads)
        ]

    key_shards = same_place_shards(weight[:, :kv_width])
    value_part, _ = lax.optimization_barrier((weight[:, kv_width:], key_shards[-1]))
    value_shards = same_place_shards(value_part)

    next_gain = moved(norm_gain, "section", lambda i: i - 1).astype(jnp.float32)
    starts = jnp.stack(
        [
            jnp.stack(
                [
                    ((own_quad - j) % quads * QUAD + (own_place ^ flip)) * shard_rows
                    for j in range(quads)
                ]
            )
            for flip in range(QUAD)
        ]
    ).astype(jnp.int32)
    cuts = normed_cuts(handoff[0], next_gain, starts)

    def to_next_section(part, flip):
        route = [
            (s * cycle_size + i, (s + 1) % sections * cycle_size + (i ^ flip))
            for s in range(sections)
            for i in range(cycle_size)
        ]
        return lax.ppermute(part, ("section", "ctx"), route)

    arrived = [to_next_section(cuts[flip], flip) for flip in range(QUAD)]

    def swapped(parts):
        return [
            moved(part, "ctx", lambda i, flip=flip: i ^ flip)
            for flip, part in enumerate(parts, start=1)
        ]

    def window_of(block):
        two_back = moved(block, "ctx", lambda i: i + 2)
        beside = moved(block, "ctx", lambda i: i ^ 1)
        three_back = moved(two_back, "ctx", lambda i: i + 1)
        from_even = lax.ppermute(
            beside, "ctx", [(i, (i + 2) % cycle_size) for i in range(0, cycle_size, 2)]
        )
        return [block, two_back, three_back, beside, from_even]

    span_len = tok_rows // 2

    def device_positions(device):
        span_ids = lax.dynamic_slice_in_dim(span_order, 2 * device, 2, 1)
        spread = (
            span_ids[:, :, None] * span_len + jnp.arange(span_len, dtype=jnp.int32)[None, None, :]
        )
        return spread.reshape(micro_count, tok_rows)

    own_pos = device_positions(own_index)
    col_pos = jnp.concatenate(
        [device_positions((own_index - d) % cycle_size) for d in range(WINDOW)], axis=1
    )[:, None, :]
    half_dim = HD // 2
    frequency = rope_base ** (-2.0 * jnp.arange(half_dim, dtype=jnp.float32) / HD)
    angles = own_pos.reshape(-1, 1).astype(jnp.float32) * frequency
    cosine, sine_part = jnp.cos(angles), jnp.sin(angles)
    cosine = jnp.concatenate([cosine, cosine], axis=1)
    sine_part = jnp.concatenate([-sine_part, sine_part], axis=1)
    odd = (own_index % 2).astype(jnp.int32).reshape(1)

    own_keys, *key_parts = partial_products(arrived, key_shards)
    key_parts, value_shards = lax.optimization_barrier((swapped(key_parts), value_shards))
    key_block = block_sum(key_sum_kernel, "key_sum", own_keys, key_parts, cosine, sine_part)
    key_window = window_of(key_block)
    weights, sums, log_sums = scored(odd, queries, key_window, own_pos[:, :, None], col_pos)

    own_values, *value_parts = partial_products(arrived, value_shards)
    value_block = block_sum(value_sum_kernel, "value_sum", own_values, swapped(value_parts))
    out = mixed_values(odd, weights, sums, window_of(value_block))
    return (out, log_sums[None])


def solution(mesh):
    placed = (
        P("section", None, "ctx", None),
        P("section", None),
        P("section", "ctx", None),
        P("section", None, "ctx", None),
        P(),
    )
    return jax.shard_map(
        on_device,
        mesh=mesh,
        in_specs=placed,
        out_specs=(P("section", None, "ctx", None), P("section", None, None, "ctx")),
        check_vma=False,
    )
```

```python
import jax
import jax.numpy as jnp
from jax import lax
from jax.experimental import pallas as pl
from jax.experimental.pallas import tpu as pltpu
from jax.sharding import PartitionSpec as P

QH = 32
KVH = 4
HD = 128
WINDOW = 4
QUAD = 4
GROUP = QH // KVH
LANES = 128
ROW_STEP = 16


rope_base = 500000.0


def moved(block, axis, target):
    size = lax.axis_size(axis)
    return lax.ppermute(block, axis, [(i, target(i) % size) for i in range(size)])


def params(mib):
    return pltpu.CompilerParams(vmem_limit_bytes=mib * 1024 * 1024)


def cost(flops, bytes_accessed):
    return pl.CostEstimate(flops=flops, bytes_accessed=bytes_accessed, transcendentals=0)


def norm_kernel(starts_ref, x_ref, gain_ref, *outs):
    rows, width = x_ref.shape[1], x_ref.shape[2]
    piece_width = outs[0].shape[1]
    for r in range(0, rows, ROW_STEP):
        x = x_ref[0, r : r + ROW_STEP, :].astype(jnp.float32)
        scale = lax.rsqrt(jnp.sum(x * x, axis=-1, keepdims=True) / width + 1e-05)
        for j, out in enumerate(outs):
            start = pl.multiple_of(starts_ref[j], LANES)
            xs = x_ref[0, r : r + ROW_STEP, pl.ds(start, piece_width)].astype(jnp.float32)
            gain = gain_ref[:, pl.ds(start, piece_width)]
            out[r : r + ROW_STEP, :] = (xs * scale * gain).astype(jnp.bfloat16)


def normed_cuts(activations, gain, starts):
    micro_count, tok_rows, width = activations.shape
    rows = micro_count * tok_rows
    pieces = starts.shape[0]
    part = width // pieces
    return pl.pallas_call(
        norm_kernel,
        grid=(micro_count,),
        in_specs=[
            pl.BlockSpec(memory_space=pltpu.SMEM),
            pl.BlockSpec((1, tok_rows, width), lambda m: (m, 0, 0)),
            pl.BlockSpec((1, width), lambda m: (0, 0)),
        ],
        out_specs=[pl.BlockSpec((tok_rows, part), lambda m: (m, 0))] * pieces,
        out_shape=[jax.ShapeDtypeStruct((rows, part), jnp.bfloat16)] * pieces,
        compiler_params=params(16),
        cost_estimate=cost(6 * rows * width, 4 * rows * width),
        name="norm_cuts",
    )(starts, activations, gain)


def product_kernel(starts_ref, x, *refs):
    shards, out = refs[:QUAD], refs[QUAD]
    shard_rows = shards[0].shape[0]
    total = 0.0
    for i, shard in enumerate(shards):
        start = pl.multiple_of(starts_ref[i], LANES)
        total = total + jnp.dot(
            x[:, pl.ds(start, shard_rows)], shard[...], preferred_element_type=jnp.float32
        )
    out[...] = total.astype(out.dtype)


def product(starts, x, shards, dtype):
    rows, part = x.shape
    width = shards[0].shape[1]
    vmem = pl.BlockSpec(memory_space=pltpu.VMEM)
    return pl.pallas_call(
        product_kernel,
        in_specs=[pl.BlockSpec(memory_space=pltpu.SMEM)] + [vmem] * (1 + QUAD),
        out_shape=jax.ShapeDtypeStruct((rows, width), dtype),
        compiler_params=params(24),
        cost_estimate=cost(2 * rows * part * width, 2 * (rows * part + part * width)),
        name="product",
    )(starts, x, *shards)


def added(own, parts, cols):
    total = own[:, cols]
    for part in parts:
        total = total + part[:, cols].astype(jnp.float32)
    return total


def key_sum_kernel(cosine, sine_part, own, *refs):
    parts, out = refs[:-1], refs[-1]
    for h in range(out.shape[1] // HD):
        cols = slice(h * HD, (h + 1) * HD)
        total = added(own, parts, cols)
        turned = pltpu.roll(total, HD // 2, 1)
        out[:, cols] = (total * cosine[...] + turned * sine_part[...]).astype(jnp.bfloat16)


def value_sum_kernel(own, *refs):
    parts, out = refs[:-1], refs[-1]
    out[...] = added(own, parts, slice(None)).astype(jnp.bfloat16)


def block_sum(kernel, name, own, parts, *tables):
    return pl.pallas_call(
        kernel,
        out_shape=jax.ShapeDtypeStruct(own.shape, jnp.bfloat16),
        compiler_params=params(16),
        cost_estimate=cost(10 * own.size, 12 * own.size),
        name=name,
    )(*tables, own, *parts)


def stacked(refs, odd):
    own, two_back, three_back, beside, from_even = refs
    one_back = jnp.where(odd == 1, beside[...], from_even[...])
    return jnp.concatenate([own[...], one_back, two_back[...], three_back[...]], axis=0)


def score_kernel(odd_ref, q_ref, *refs):
    key_refs, (row_pos, col_pos, weights, sums, log_sums) = refs[:5], refs[5:]
    keys = stacked(key_refs, odd_ref[0])
    tok_rows = q_ref.shape[2]
    visible = col_pos[0] <= row_pos[0]
    lane = lax.broadcasted_iota(jnp.int32, (tok_rows, LANES), 1)
    all_sums = jnp.ones((tok_rows, LANES), jnp.float32)
    all_max = jnp.zeros((tok_rows, LANES), jnp.float32)
    for h in range(GROUP):
        scores = lax.dot_general(
            q_ref[0, 0, :, h * HD : (h + 1) * HD],
            keys,
            (((1,), (1,)), ((), ())),
            preferred_element_type=jnp.float32,
        ) * HD ** (-0.5)
        scores = jnp.where(visible, scores, -jnp.inf)
        row_max = jnp.max(scores, axis=-1, keepdims=True)
        exps = jnp.exp(scores - row_max)
        running = jnp.sum(exps, axis=-1, keepdims=True)
        weights[0, 0, h * tok_rows : (h + 1) * tok_rows, :] = exps.astype(jnp.bfloat16)
        all_sums = jnp.where(lane == h, running, all_sums)
        all_max = jnp.where(lane == h, row_max, all_max)
    sums[0, 0] = all_sums
    log_sums[0] = jnp.transpose(all_max + jnp.log(all_sums))[:GROUP]


def window_specs(tok_rows):
    return [pl.BlockSpec((tok_rows, HD), lambda m, k: (m, k))] * 5


def scored(odd, queries, window, row_pos, col_pos):
    _, micro_count, tok_rows, width = queries.shape
    keys = WINDOW * tok_rows
    return pl.pallas_call(
        score_kernel,
        grid=(micro_count, KVH),
        in_specs=[
            pl.BlockSpec(memory_space=pltpu.SMEM),
            pl.BlockSpec((1, 1, tok_rows, GROUP * HD), lambda m, k: (0, m, 0, k)),
            *window_specs(tok_rows),
            pl.BlockSpec((1, tok_rows, 1), lambda m, k: (m, 0, 0)),
            pl.BlockSpec((1, 1, keys), lambda m, k: (m, 0, 0)),
        ],
        out_specs=[
            pl.BlockSpec((1, 1, GROUP * tok_rows, keys), lambda m, k: (m, k, 0, 0)),
            pl.BlockSpec((1, 1, tok_rows, LANES), lambda m, k: (m, k, 0, 0)),
            pl.BlockSpec((1, GROUP, tok_rows), lambda m, k: (m, k, 0)),
        ],
        out_shape=[
            jax.ShapeDtypeStruct((micro_count, KVH, GROUP * tok_rows, keys), jnp.bfloat16),
            jax.ShapeDtypeStruct((micro_count, KVH, tok_rows, LANES), jnp.float32),
            jax.ShapeDtypeStruct((micro_count, QH, tok_rows), jnp.float32),
        ],
        compiler_params=params(24),
        cost_estimate=cost(2 * micro_count * QH * tok_rows * keys * HD, 8 * 2**20),
        name="scores",
    )(odd, queries, *window, row_pos, col_pos)


def mix_kernel(odd_ref, weights, sums, *refs):
    values = stacked(refs[:5], odd_ref[0])
    out = refs[5]
    tok_rows = out.shape[2]
    for k in range(KVH):
        mixed = jnp.dot(
            weights[0, k], values[:, k * HD : (k + 1) * HD], preferred_element_type=jnp.float32
        )
        share = 1.0 / sums[0, k]
        for h in range(GROUP):
            head = k * GROUP + h
            out[0, 0, :, head * HD : (head + 1) * HD] = (
                mixed[h * tok_rows : (h + 1) * tok_rows] * share[:, h : h + 1]
            ).astype(jnp.bfloat16)


def mixed_values(odd, weights, sums, window):
    micro_count, _, group_rows, keys = weights.shape
    tok_rows = group_rows // GROUP
    return pl.pallas_call(
        mix_kernel,
        grid=(micro_count,),
        in_specs=[
            pl.BlockSpec(memory_space=pltpu.SMEM),
            pl.BlockSpec((1, KVH, group_rows, keys), lambda m: (m, 0, 0, 0)),
            pl.BlockSpec((1, KVH, tok_rows, LANES), lambda m: (m, 0, 0, 0)),
            *[pl.BlockSpec((tok_rows, KVH * HD), lambda m: (m, 0))] * 5,
        ],
        out_specs=pl.BlockSpec((1, 1, tok_rows, QH * HD), lambda m: (0, m, 0, 0)),
        out_shape=jax.ShapeDtypeStruct((1, micro_count, tok_rows, QH * HD), jnp.bfloat16),
        compiler_params=params(32),
        cost_estimate=cost(2 * micro_count * QH * tok_rows * keys * HD, 8 * 2**20),
        name="mixed_values",
    )(odd, weights, sums, *window)


def on_device(handoff, norm_gain, kv_weight, queries, span_order):
    sections = lax.axis_size("section")
    cycle_size = lax.axis_size("ctx")
    own_index = lax.axis_index("ctx")
    quads = cycle_size // QUAD
    own_quad, own_place = own_index // QUAD, own_index % QUAD
    weight = kv_weight[0]
    shard_rows, kv_width = weight.shape[0], weight.shape[1] // 2
    _, micro_count, tok_rows, _ = handoff.shape

    def over_z(part):
        return moved(part, "ctx", lambda i: i ^ 2)

    def over_y(part):
        return moved(part, "ctx", lambda i: i ^ 1)

    places = own_place ^ jnp.array([0, 2, 1, 3], jnp.int32)
    starts = places * shard_rows
    key_part, value_part = weight[:, :kv_width], weight[:, kv_width:]
    key_z = over_z(key_part)
    key_shards = [key_part, key_z, over_y(key_part), over_y(key_z)]
    late_part, _ = lax.optimization_barrier((value_part, key_z))
    value_z = over_z(late_part)
    value_shards = [value_part, value_z, over_y(value_part), over_y(value_z)]

    next_gain = moved(norm_gain, "section", lambda i: i - 1).astype(jnp.float32)
    cut_starts = (own_quad + jnp.arange(quads, dtype=jnp.int32)) % quads * (QUAD * shard_rows)
    cuts = normed_cuts(handoff[0], next_gain, cut_starts)

    def to_next_section(part, j):
        route = [
            (s * cycle_size + i, (s + 1) % sections * cycle_size + (i + QUAD * j) % cycle_size)
            for s in range(sections)
            for i in range(cycle_size)
        ]
        return lax.ppermute(part, ("section", "ctx"), route)

    arrived = [to_next_section(cuts[j], j) for j in range(quads)]

    def sent_back(shards):
        return [
            moved(
                product(starts, arrived[j], shards, jnp.bfloat16),
                "ctx",
                lambda i, j=j: i - QUAD * j,
            )
            for j in range(1, quads)
        ]

    def window_of(block):
        two_back = moved(block, "ctx", lambda i: i + 2)
        beside = moved(block, "ctx", lambda i: i ^ 1)
        three_back = moved(two_back, "ctx", lambda i: i + 1)
        from_even = lax.ppermute(
            beside, "ctx", [(i, (i + 2) % cycle_size) for i in range(0, cycle_size, 2)]
        )
        return [block, two_back, three_back, beside, from_even]

    span_len = tok_rows // 2

    def device_positions(device):
        span_ids = lax.dynamic_slice_in_dim(span_order, 2 * device, 2, 1)
        spread = (
            span_ids[:, :, None] * span_len + jnp.arange(span_len, dtype=jnp.int32)[None, None, :]
        )
        return spread.reshape(micro_count, tok_rows)

    own_pos = device_positions(own_index)
    col_pos = jnp.concatenate(
        [device_positions((own_index - d) % cycle_size) for d in range(WINDOW)], axis=1
    )[:, None, :]
    half_dim = HD // 2
    frequency = rope_base ** (-2.0 * jnp.arange(half_dim, dtype=jnp.float32) / HD)
    angles = own_pos.reshape(-1, 1).astype(jnp.float32) * frequency
    cosine, sine_part = jnp.cos(angles), jnp.sin(angles)
    cosine = jnp.concatenate([cosine, cosine], axis=1)
    sine_part = jnp.concatenate([-sine_part, sine_part], axis=1)
    odd = (own_index % 2).astype(jnp.int32).reshape(1)

    key_parts = sent_back(key_shards)
    own_keys = product(starts, arrived[0], key_shards, jnp.float32)
    key_block = block_sum(key_sum_kernel, "key_sum", own_keys, key_parts, cosine, sine_part)
    weights, sums, log_sums = scored(
        odd, queries, window_of(key_block), own_pos[:, :, None], col_pos
    )

    value_parts = sent_back(value_shards)
    own_values = product(starts, arrived[0], value_shards, jnp.float32)
    value_block = block_sum(value_sum_kernel, "value_sum", own_values, value_parts)
    out = mixed_values(odd, weights, sums, window_of(value_block))
    return (out, log_sums[None])


def solution(mesh):
    placed = (
        P("section", None, "ctx", None),
        P("section", None),
        P("section", "ctx", None),
        P("section", None, "ctx", None),
        P(),
    )
    return jax.shard_map(
        on_device,
        mesh=mesh,
        in_specs=placed,
        out_specs=(P("section", None, "ctx", None), P("section", None, None, "ctx")),
        check_vma=False,
    )
```

```python
import jax
import jax.numpy as jnp
from jax import lax
from jax.experimental import pallas as pl
from jax.experimental.pallas import tpu as pltpu
from jax.sharding import PartitionSpec as P

QH = 32
KVH = 4
HD = 128
WINDOW = 4
QUAD = 4
GROUP = QH // KVH
LANES = 128
ROW_STEP = 16


rope_base = 500000.0


def moved(block, axis, target):
    size = lax.axis_size(axis)
    return lax.ppermute(block, axis, [(i, target(i) % size) for i in range(size)])


def params(mib):
    return pltpu.CompilerParams(vmem_limit_bytes=mib * 1024 * 1024)


def cost(flops, bytes_accessed):
    return pl.CostEstimate(flops=flops, bytes_accessed=bytes_accessed, transcendentals=0)


def norm_kernel(starts_ref, x_ref, gain_ref, *outs):
    rows, width = x_ref.shape[1], x_ref.shape[2]
    piece_width = outs[0].shape[1]
    for r in range(0, rows, ROW_STEP):
        x = x_ref[0, r : r + ROW_STEP, :].astype(jnp.float32)
        scale = lax.rsqrt(jnp.sum(x * x, axis=-1, keepdims=True) / width + 1e-05)
        for j, out in enumerate(outs):
            start = pl.multiple_of(starts_ref[j], LANES)
            xs = x_ref[0, r : r + ROW_STEP, pl.ds(start, piece_width)].astype(jnp.float32)
            gain = gain_ref[:, pl.ds(start, piece_width)]
            out[r : r + ROW_STEP, :] = (xs * scale * gain).astype(jnp.bfloat16)


def normed_cuts(activations, gain, starts):
    micro_count, tok_rows, width = activations.shape
    rows = micro_count * tok_rows
    pieces = starts.shape[0]
    part = width // pieces
    return pl.pallas_call(
        norm_kernel,
        grid=(micro_count,),
        in_specs=[
            pl.BlockSpec(memory_space=pltpu.SMEM),
            pl.BlockSpec((1, tok_rows, width), lambda m: (m, 0, 0)),
            pl.BlockSpec((1, width), lambda m: (0, 0)),
        ],
        out_specs=[pl.BlockSpec((tok_rows, part), lambda m: (m, 0))] * pieces,
        out_shape=[jax.ShapeDtypeStruct((rows, part), jnp.bfloat16)] * pieces,
        compiler_params=params(16),
        cost_estimate=cost(6 * rows * width, 4 * rows * width),
        name="norm_cuts",
    )(starts, activations, gain)


def product_kernel(starts_ref, x, *refs):
    shards, out = refs[:QUAD], refs[QUAD]
    shard_rows = shards[0].shape[0]
    total = 0.0
    for i, shard in enumerate(shards):
        start = pl.multiple_of(starts_ref[i], LANES)
        total = total + jnp.dot(
            x[:, pl.ds(start, shard_rows)], shard[...], preferred_element_type=jnp.float32
        )
    out[...] = total.astype(out.dtype)


def product(starts, x, shards, dtype):
    rows, part = x.shape
    width = shards[0].shape[1]
    vmem = pl.BlockSpec(memory_space=pltpu.VMEM)
    return pl.pallas_call(
        product_kernel,
        in_specs=[pl.BlockSpec(memory_space=pltpu.SMEM)] + [vmem] * (1 + QUAD),
        out_shape=jax.ShapeDtypeStruct((rows, width), dtype),
        compiler_params=params(24),
        cost_estimate=cost(2 * rows * part * width, 2 * (rows * part + part * width)),
        name="product",
    )(starts, x, *shards)


def added(own, parts, cols):
    total = own[:, cols]
    for part in parts:
        total = total + part[:, cols].astype(jnp.float32)
    return total


def key_sum_kernel(cosine, sine_part, own, *refs):
    parts, out = refs[:-1], refs[-1]
    for h in range(out.shape[1] // HD):
        cols = slice(h * HD, (h + 1) * HD)
        total = added(own, parts, cols)
        turned = pltpu.roll(total, HD // 2, 1)
        out[:, cols] = (total * cosine[...] + turned * sine_part[...]).astype(jnp.bfloat16)


def value_sum_kernel(own, *refs):
    parts, out = refs[:-1], refs[-1]
    out[...] = added(own, parts, slice(None)).astype(jnp.bfloat16)


def block_sum(kernel, name, own, parts, *tables):
    return pl.pallas_call(
        kernel,
        out_shape=jax.ShapeDtypeStruct(own.shape, jnp.bfloat16),
        compiler_params=params(16),
        cost_estimate=cost(10 * own.size, 12 * own.size),
        name=name,
    )(*tables, own, *parts)


def stacked(refs, odd):
    own, two_back, three_back, beside, from_even = refs
    one_back = jnp.where(odd == 1, beside[...], from_even[...])
    return jnp.concatenate([three_back[...], two_back[...], one_back, own[...]], axis=0)


def score_kernel(odd_ref, q_ref, *refs):
    key_refs, (row_pos, col_pos, weights, sums, log_sums) = refs[:5], refs[5:]
    keys = stacked(key_refs, odd_ref[0])
    tok_rows = q_ref.shape[2]
    visible = col_pos[0] <= row_pos[0]
    lane = lax.broadcasted_iota(jnp.int32, (tok_rows, LANES), 1)
    all_sums = jnp.ones((tok_rows, LANES), jnp.float32)
    all_max = jnp.zeros((tok_rows, LANES), jnp.float32)
    for h in range(GROUP):
        scores = lax.dot_general(
            q_ref[0, 0, :, h * HD : (h + 1) * HD],
            keys,
            (((1,), (1,)), ((), ())),
            preferred_element_type=jnp.float32,
        ) * HD ** (-0.5)
        scores = jnp.where(visible, scores, -jnp.inf)
        row_max = jnp.max(scores, axis=-1, keepdims=True)
        exps = jnp.exp(scores - row_max)
        running = jnp.sum(exps, axis=-1, keepdims=True)
        weights[0, 0, h * tok_rows : (h + 1) * tok_rows, :] = exps.astype(jnp.bfloat16)
        all_sums = jnp.where(lane == h, running, all_sums)
        all_max = jnp.where(lane == h, row_max, all_max)
    sums[0, 0] = all_sums
    log_sums[0] = jnp.transpose(all_max + jnp.log(all_sums))[:GROUP]


def window_specs(tok_rows):
    return [pl.BlockSpec((tok_rows, HD), lambda m, k: (m, k))] * 5


def scored(odd, queries, window, row_pos, col_pos):
    _, micro_count, tok_rows, _ = queries.shape
    keys = WINDOW * tok_rows
    return pl.pallas_call(
        score_kernel,
        grid=(micro_count, KVH),
        in_specs=[
            pl.BlockSpec(memory_space=pltpu.SMEM),
            pl.BlockSpec((1, 1, tok_rows, GROUP * HD), lambda m, k: (0, m, 0, k)),
            *window_specs(tok_rows),
            pl.BlockSpec((1, tok_rows, 1), lambda m, k: (m, 0, 0)),
            pl.BlockSpec((1, 1, keys), lambda m, k: (m, 0, 0)),
        ],
        out_specs=[
            pl.BlockSpec((1, 1, GROUP * tok_rows, keys), lambda m, k: (m, k, 0, 0)),
            pl.BlockSpec((1, 1, tok_rows, LANES), lambda m, k: (m, k, 0, 0)),
            pl.BlockSpec((1, GROUP, tok_rows), lambda m, k: (m, k, 0)),
        ],
        out_shape=[
            jax.ShapeDtypeStruct((micro_count, KVH, GROUP * tok_rows, keys), jnp.bfloat16),
            jax.ShapeDtypeStruct((micro_count, KVH, tok_rows, LANES), jnp.float32),
            jax.ShapeDtypeStruct((micro_count, QH, tok_rows), jnp.float32),
        ],
        compiler_params=params(24),
        cost_estimate=cost(2 * micro_count * QH * tok_rows * keys * HD, 8 * 2**20),
        name="scores",
    )(odd, queries, *window, row_pos, col_pos)


def mix_kernel(odd_ref, weights, sums, *refs):
    values = stacked(refs[:5], odd_ref[0])
    out = refs[5]
    tok_rows = out.shape[2]
    for k in range(KVH):
        mixed = jnp.dot(
            weights[0, k], values[:, k * HD : (k + 1) * HD], preferred_element_type=jnp.float32
        )
        share = 1.0 / sums[0, k]
        for h in range(GROUP):
            head = k * GROUP + h
            out[0, 0, :, head * HD : (head + 1) * HD] = (
                mixed[h * tok_rows : (h + 1) * tok_rows] * share[:, h : h + 1]
            ).astype(jnp.bfloat16)


def mixed_values(odd, weights, sums, window):
    micro_count, _, group_rows, keys = weights.shape
    tok_rows = group_rows // GROUP
    return pl.pallas_call(
        mix_kernel,
        grid=(micro_count,),
        in_specs=[
            pl.BlockSpec(memory_space=pltpu.SMEM),
            pl.BlockSpec((1, KVH, group_rows, keys), lambda m: (m, 0, 0, 0)),
            pl.BlockSpec((1, KVH, tok_rows, LANES), lambda m: (m, 0, 0, 0)),
            *[pl.BlockSpec((tok_rows, KVH * HD), lambda m: (m, 0))] * 5,
        ],
        out_specs=pl.BlockSpec((1, 1, tok_rows, QH * HD), lambda m: (0, m, 0, 0)),
        out_shape=jax.ShapeDtypeStruct((1, micro_count, tok_rows, QH * HD), jnp.bfloat16),
        compiler_params=params(32),
        cost_estimate=cost(2 * micro_count * QH * tok_rows * keys * HD, 8 * 2**20),
        name="mixed_values",
    )(odd, weights, sums, *window)


def on_device(handoff, norm_gain, kv_weight, queries, span_order):
    sections = lax.axis_size("section")
    cycle_size = lax.axis_size("ctx")
    own_index = lax.axis_index("ctx")
    quads = cycle_size // QUAD
    own_quad, own_place = own_index // QUAD, own_index % QUAD
    weight = kv_weight[0]
    shard_rows, kv_width = weight.shape[0], weight.shape[1] // 2
    _, micro_count, tok_rows, _ = handoff.shape

    next_gain = moved(norm_gain, "section", lambda i: i - 1).astype(jnp.float32)
    cut_starts = (own_quad + jnp.arange(quads, dtype=jnp.int32)) % quads * (QUAD * shard_rows)
    cuts = normed_cuts(handoff[0], next_gain, cut_starts)

    def over_z(part):
        return moved(part, "ctx", lambda i: i ^ 2)

    def over_y(part):
        return moved(part, "ctx", lambda i: i ^ 1)

    places = own_place ^ jnp.array([0, 2, 1, 3], jnp.int32)
    starts = places * shard_rows
    key_part, value_part, cuts = lax.optimization_barrier(
        (weight[:, :kv_width], weight[:, kv_width:], cuts)
    )
    key_z = over_z(key_part)
    key_shards = [key_part, key_z, over_y(key_part), over_y(key_z)]
    late_part, _ = lax.optimization_barrier((value_part, key_z))
    value_z = over_z(late_part)
    value_shards = [value_part, value_z, over_y(value_part), over_y(value_z)]

    def to_next_section(part, j):
        route = [
            (s * cycle_size + i, (s + 1) % sections * cycle_size + (i + QUAD * j) % cycle_size)
            for s in range(sections)
            for i in range(cycle_size)
        ]
        return lax.ppermute(part, ("section", "ctx"), route)

    arrived = [to_next_section(cuts[j], j) for j in range(quads)]

    def partials(shards):
        return [product(starts, arrived[j], shards, jnp.bfloat16) for j in range(1, quads)]

    def sent_back(parts):
        return [
            moved(part, "ctx", lambda i, j=j: i - QUAD * j) for j, part in enumerate(parts, start=1)
        ]

    def near_blocks(block):
        return [moved(block, "ctx", lambda i: i + 2), moved(block, "ctx", lambda i: i ^ 1)]

    def window_of(block, two_back, beside):
        three_back = moved(two_back, "ctx", lambda i: i + 1)
        from_even = lax.ppermute(
            beside, "ctx", [(i, (i + 2) % cycle_size) for i in range(0, cycle_size, 2)]
        )
        return [block, two_back, three_back, beside, from_even]

    span_len = tok_rows // 2
    places_of = span_order[:, :, None] * span_len + jnp.arange(span_len, dtype=jnp.int32)
    all_pos = places_of.reshape(micro_count, cycle_size * tok_rows)
    col_pos = lax.dynamic_slice_in_dim(
        jnp.concatenate([all_pos[:, -(WINDOW - 1) * tok_rows :], all_pos], axis=1),
        own_index * tok_rows,
        WINDOW * tok_rows,
        1,
    )
    own_pos = col_pos[:, -tok_rows:]
    half_dim = HD // 2
    frequency = rope_base ** (-2.0 * jnp.arange(half_dim, dtype=jnp.float32) / HD)
    angles = own_pos.reshape(-1, 1).astype(jnp.float32) * frequency
    cosine, sine_part = jnp.cos(angles), jnp.sin(angles)
    cosine = jnp.concatenate([cosine, cosine], axis=1)
    sine_part = jnp.concatenate([-sine_part, sine_part], axis=1)
    odd = (own_index % 2).astype(jnp.int32).reshape(1)

    key_parts = sent_back(partials(key_shards))
    own_keys = product(starts, arrived[0], key_shards, jnp.float32)
    own_values = product(starts, arrived[0], value_shards, jnp.float32)
    value_partials, key_parts, own_values = lax.optimization_barrier(
        (partials(value_shards), key_parts, own_values)
    )
    value_parts = sent_back(value_partials)
    key_block = block_sum(key_sum_kernel, "key_sum", own_keys, key_parts, cosine, sine_part)
    key_near, value_parts = lax.optimization_barrier((near_blocks(key_block), value_parts))
    key_window = window_of(key_block, *key_near)
    weights, sums, log_sums = scored(
        odd, queries, key_window, own_pos[:, :, None], col_pos[:, None, :]
    )
    value_block = block_sum(value_sum_kernel, "value_sum", own_values, value_parts)
    value_window = window_of(value_block, *near_blocks(value_block))
    out = mixed_values(odd, weights, sums, value_window)
    return (out, log_sums[None])


def solution(mesh):
    placed = (
        P("section", None, "ctx", None),
        P("section", None),
        P("section", "ctx", None),
        P("section", None, "ctx", None),
        P(),
    )
    return jax.shard_map(
        on_device,
        mesh=mesh,
        in_specs=placed,
        out_specs=(P("section", None, "ctx", None), P("section", None, None, "ctx")),
        check_vma=False,
    )
```

```python
import jax
import jax.numpy as jnp
from jax import lax
from jax.experimental import pallas as pl
from jax.experimental.pallas import tpu as pltpu
from jax.sharding import PartitionSpec as P

QH = 32
KVH = 4
HD = 128
WINDOW = 4
QUAD = 4
GROUP = QH // KVH
LANES = 128
ROW_STEP = 16


rope_base = 500000.0


def moved(block, axis, target):
    size = lax.axis_size(axis)
    return lax.ppermute(block, axis, [(i, target(i) % size) for i in range(size)])


def params(mib):
    return pltpu.CompilerParams(vmem_limit_bytes=mib * 1024 * 1024)


def cost(flops, bytes_accessed):
    return pl.CostEstimate(flops=flops, bytes_accessed=bytes_accessed, transcendentals=0)


def norm_kernel(starts_ref, x_ref, gain_ref, *outs):
    rows, width = x_ref.shape[1], x_ref.shape[2]
    piece_width = outs[0].shape[1]
    for r in range(0, rows, ROW_STEP):
        x = x_ref[0, r : r + ROW_STEP, :].astype(jnp.float32)
        scale = lax.rsqrt(jnp.sum(x * x, axis=-1, keepdims=True) / width + 1e-05)
        for j, out in enumerate(outs):
            start = pl.multiple_of(starts_ref[j], LANES)
            xs = x_ref[0, r : r + ROW_STEP, pl.ds(start, piece_width)].astype(jnp.float32)
            gain = gain_ref[:, pl.ds(start, piece_width)]
            out[r : r + ROW_STEP, :] = (xs * scale * gain).astype(jnp.bfloat16)


def normed_cuts(activations, gain, starts):
    micro_count, tok_rows, width = activations.shape
    rows = micro_count * tok_rows
    pieces = starts.shape[0]
    part = width // pieces
    return pl.pallas_call(
        norm_kernel,
        grid=(micro_count,),
        in_specs=[
            pl.BlockSpec(memory_space=pltpu.SMEM),
            pl.BlockSpec((1, tok_rows, width), lambda m: (m, 0, 0)),
            pl.BlockSpec((1, width), lambda m: (0, 0)),
        ],
        out_specs=[pl.BlockSpec((tok_rows, part), lambda m: (m, 0))] * pieces,
        out_shape=[jax.ShapeDtypeStruct((rows, part), jnp.bfloat16)] * pieces,
        compiler_params=params(16),
        cost_estimate=cost(6 * rows * width, 4 * rows * width),
        name="norm_cuts",
    )(starts, activations, gain)


def product_kernel(starts_ref, x, *refs):
    shards, out = refs[:QUAD], refs[QUAD]
    shard_rows = shards[0].shape[0]
    total = 0.0
    for i, shard in enumerate(shards):
        start = pl.multiple_of(starts_ref[i], LANES)
        total = total + jnp.dot(
            x[:, pl.ds(start, shard_rows)], shard[...], preferred_element_type=jnp.float32
        )
    out[...] = total.astype(out.dtype)


def product(starts, x, shards, dtype):
    rows, part = x.shape
    width = shards[0].shape[1]
    vmem = pl.BlockSpec(memory_space=pltpu.VMEM)
    return pl.pallas_call(
        product_kernel,
        in_specs=[pl.BlockSpec(memory_space=pltpu.SMEM)] + [vmem] * (1 + QUAD),
        out_shape=jax.ShapeDtypeStruct((rows, width), dtype),
        compiler_params=params(24),
        cost_estimate=cost(8 * rows * part * width, 8 * (rows * part + part * width)),
        name="product",
    )(starts, x, *shards)


def added(own, parts, cols):
    total = own[:, cols]
    for part in parts:
        total = total + part[:, cols].astype(jnp.float32)
    return total


def key_sum_kernel(cosine, sine_part, own, *refs):
    parts, out = refs[:-1], refs[-1]
    for h in range(out.shape[1] // HD):
        cols = slice(h * HD, (h + 1) * HD)
        total = added(own, parts, cols)
        turned = pltpu.roll(total, HD // 2, 1)
        out[:, cols] = (total * cosine[...] + turned * sine_part[...]).astype(jnp.bfloat16)


def value_sum_kernel(own, *refs):
    parts, out = refs[:-1], refs[-1]
    out[...] = added(own, parts, slice(None)).astype(jnp.bfloat16)


def block_sum(kernel, name, own, parts, *tables):
    return pl.pallas_call(
        kernel,
        out_shape=jax.ShapeDtypeStruct(own.shape, jnp.bfloat16),
        compiler_params=params(16),
        cost_estimate=cost(10 * own.size, 12 * own.size),
        name=name,
    )(*tables, own, *parts)


def stacked(refs, odd):
    own, two_back, three_back, beside, from_even = refs
    one_back = jnp.where(odd == 1, beside[...], from_even[...])
    return jnp.concatenate([three_back[...], two_back[...], one_back, own[...]], axis=0)


def score_kernel(odd_ref, q_ref, *refs):
    key_refs, (row_pos, col_pos, weights, sums, log_sums) = refs[:5], refs[5:]
    keys = stacked(key_refs, odd_ref[0])
    tok_rows = q_ref.shape[2]
    visible = col_pos[0] <= row_pos[0]
    lane = lax.broadcasted_iota(jnp.int32, (tok_rows, LANES), 1)
    all_sums = jnp.ones((tok_rows, LANES), jnp.float32)
    all_max = jnp.zeros((tok_rows, LANES), jnp.float32)
    for h in range(GROUP):
        scores = lax.dot_general(
            q_ref[0, 0, :, h * HD : (h + 1) * HD],
            keys,
            (((1,), (1,)), ((), ())),
            preferred_element_type=jnp.float32,
        ) * HD ** (-0.5)
        scores = jnp.where(visible, scores, -jnp.inf)
        row_max = jnp.max(scores, axis=-1, keepdims=True)
        exps = jnp.exp(scores - row_max)
        running = jnp.sum(exps, axis=-1, keepdims=True)
        weights[0, 0, h * tok_rows : (h + 1) * tok_rows, :] = exps.astype(jnp.bfloat16)
        all_sums = jnp.where(lane == h, running, all_sums)
        all_max = jnp.where(lane == h, row_max, all_max)
    sums[0, 0] = all_sums
    log_sums[0] = jnp.transpose(all_max + jnp.log(all_sums))[:GROUP]


def window_specs(tok_rows):
    return [pl.BlockSpec((tok_rows, HD), lambda m, k: (m, k))] * 5


def scored(odd, queries, window, row_pos, col_pos):
    _, micro_count, tok_rows, _ = queries.shape
    keys = WINDOW * tok_rows
    return pl.pallas_call(
        score_kernel,
        grid=(micro_count, KVH),
        in_specs=[
            pl.BlockSpec(memory_space=pltpu.SMEM),
            pl.BlockSpec((1, 1, tok_rows, GROUP * HD), lambda m, k: (0, m, 0, k)),
            *window_specs(tok_rows),
            pl.BlockSpec((1, tok_rows, 1), lambda m, k: (m, 0, 0)),
            pl.BlockSpec((1, 1, keys), lambda m, k: (m, 0, 0)),
        ],
        out_specs=[
            pl.BlockSpec((1, 1, GROUP * tok_rows, keys), lambda m, k: (m, k, 0, 0)),
            pl.BlockSpec((1, 1, tok_rows, LANES), lambda m, k: (m, k, 0, 0)),
            pl.BlockSpec((1, GROUP, tok_rows), lambda m, k: (m, k, 0)),
        ],
        out_shape=[
            jax.ShapeDtypeStruct((micro_count, KVH, GROUP * tok_rows, keys), jnp.bfloat16),
            jax.ShapeDtypeStruct((micro_count, KVH, tok_rows, LANES), jnp.float32),
            jax.ShapeDtypeStruct((micro_count, QH, tok_rows), jnp.float32),
        ],
        compiler_params=params(24),
        cost_estimate=cost(2 * micro_count * QH * tok_rows * keys * HD, 8 * 2**20),
        name="scores",
    )(odd, queries, *window, row_pos, col_pos)


def mix_kernel(odd_ref, weights, sums, *refs):
    values = stacked(refs[:5], odd_ref[0])
    out = refs[5]
    tok_rows = out.shape[2]
    for k in range(KVH):
        mixed = jnp.dot(
            weights[0, k], values[:, k * HD : (k + 1) * HD], preferred_element_type=jnp.float32
        )
        share = 1.0 / sums[0, k]
        for h in range(GROUP):
            head = k * GROUP + h
            out[0, 0, :, head * HD : (head + 1) * HD] = (
                mixed[h * tok_rows : (h + 1) * tok_rows] * share[:, h : h + 1]
            ).astype(jnp.bfloat16)


def mixed_values(odd, weights, sums, window):
    micro_count, _, group_rows, keys = weights.shape
    tok_rows = group_rows // GROUP
    return pl.pallas_call(
        mix_kernel,
        grid=(micro_count,),
        in_specs=[
            pl.BlockSpec(memory_space=pltpu.SMEM),
            pl.BlockSpec((1, KVH, group_rows, keys), lambda m: (m, 0, 0, 0)),
            pl.BlockSpec((1, KVH, tok_rows, LANES), lambda m: (m, 0, 0, 0)),
            *[pl.BlockSpec((tok_rows, KVH * HD), lambda m: (m, 0))] * 5,
        ],
        out_specs=pl.BlockSpec((1, 1, tok_rows, QH * HD), lambda m: (0, m, 0, 0)),
        out_shape=jax.ShapeDtypeStruct((1, micro_count, tok_rows, QH * HD), jnp.bfloat16),
        compiler_params=params(32),
        cost_estimate=cost(2 * micro_count * QH * tok_rows * keys * HD, 8 * 2**20),
        name="mixed_values",
    )(odd, weights, sums, *window)


def on_device(handoff, norm_gain, kv_weight, queries, span_order):
    sections = lax.axis_size("section")
    cycle_size = lax.axis_size("ctx")
    own_index = lax.axis_index("ctx")
    quads = cycle_size // QUAD
    own_quad, own_place = own_index // QUAD, own_index % QUAD
    weight = kv_weight[0]
    shard_rows, kv_width = weight.shape[0], weight.shape[1] // 2
    _, micro_count, tok_rows, _ = handoff.shape

    next_gain = moved(norm_gain, "section", lambda i: i - 1).astype(jnp.float32)
    cut_starts = (own_quad + jnp.arange(quads, dtype=jnp.int32)) % quads * (QUAD * shard_rows)
    cuts = normed_cuts(handoff[0], next_gain, cut_starts)

    def over_z(part):
        return moved(part, "ctx", lambda i: i ^ 2)

    def over_y(part):
        return moved(part, "ctx", lambda i: i ^ 1)

    places = own_place ^ jnp.array([0, 2, 1, 3], jnp.int32)
    starts = places * shard_rows
    key_part, value_part, cuts = lax.optimization_barrier(
        (weight[:, :kv_width], weight[:, kv_width:], cuts)
    )
    key_z = over_z(key_part)
    key_shards = [key_part, key_z, over_y(key_part), over_y(key_z)]
    late_part, _ = lax.optimization_barrier((value_part, key_z))
    value_z = over_z(late_part)
    value_shards = [value_part, value_z, over_y(value_part), over_y(value_z)]

    def to_next_section(part, j):
        route = [
            (s * cycle_size + i, (s + 1) % sections * cycle_size + (i + QUAD * j) % cycle_size)
            for s in range(sections)
            for i in range(cycle_size)
        ]
        return lax.ppermute(part, ("section", "ctx"), route)

    arrived = [to_next_section(cuts[j], j) for j in range(quads)]

    def partials(shards):
        return [product(starts, arrived[j], shards, jnp.bfloat16) for j in range(1, quads)]

    def sent_back(parts):
        return [
            moved(part, "ctx", lambda i, j=j: i - QUAD * j) for j, part in enumerate(parts, start=1)
        ]

    def near_blocks(block):
        return [moved(block, "ctx", lambda i: i + 2), moved(block, "ctx", lambda i: i ^ 1)]

    def window_of(block, two_back, beside):
        three_back = moved(two_back, "ctx", lambda i: i + 1)
        from_even = lax.ppermute(
            beside, "ctx", [(i, (i + 2) % cycle_size) for i in range(0, cycle_size, 2)]
        )
        return [block, two_back, three_back, beside, from_even]

    span_len = tok_rows // 2
    places_of = span_order[:, :, None] * span_len + jnp.arange(span_len, dtype=jnp.int32)
    all_pos = places_of.reshape(micro_count, cycle_size * tok_rows)
    col_pos = lax.dynamic_slice_in_dim(
        jnp.concatenate([all_pos[:, -(WINDOW - 1) * tok_rows :], all_pos], axis=1),
        own_index * tok_rows,
        WINDOW * tok_rows,
        1,
    )
    own_pos = col_pos[:, -tok_rows:]
    half_dim = HD // 2
    frequency = rope_base ** (-2.0 * jnp.arange(half_dim, dtype=jnp.float32) / HD)
    angles = own_pos.reshape(-1, 1).astype(jnp.float32) * frequency
    cosine, sine_part = jnp.cos(angles), jnp.sin(angles)
    cosine = jnp.concatenate([cosine, cosine], axis=1)
    sine_part = jnp.concatenate([-sine_part, sine_part], axis=1)
    odd = (own_index % 2).astype(jnp.int32).reshape(1)

    key_parts = sent_back(partials(key_shards))
    own_keys = product(starts, arrived[0], key_shards, jnp.float32)
    own_values = product(starts, arrived[0], value_shards, jnp.float32)
    value_partials, key_parts, own_values = lax.optimization_barrier(
        (partials(value_shards), key_parts, own_values)
    )
    value_parts = sent_back(value_partials)
    key_block = block_sum(key_sum_kernel, "key_sum", own_keys, key_parts, cosine, sine_part)
    key_near, value_parts = lax.optimization_barrier((near_blocks(key_block), value_parts))
    key_window = window_of(key_block, *key_near)
    weights, sums, log_sums = scored(
        odd, queries, key_window, own_pos[:, :, None], col_pos[:, None, :]
    )
    value_block = block_sum(value_sum_kernel, "value_sum", own_values, value_parts)
    value_window = window_of(value_block, *near_blocks(value_block))
    out = mixed_values(odd, weights, sums, value_window)
    return (out, log_sums[None])


def solution(mesh):
    placed = (
        P("section", None, "ctx", None),
        P("section", None),
        P("section", "ctx", None),
        P("section", None, "ctx", None),
        P(),
    )
    return jax.shard_map(
        on_device,
        mesh=mesh,
        in_specs=placed,
        out_specs=(P("section", None, "ctx", None), P("section", None, None, "ctx")),
        check_vma=False,
    )
```

```python
import jax
import jax.numpy as jnp
from jax import lax
from jax.experimental import pallas as pl
from jax.experimental.pallas import tpu as pltpu
from jax.sharding import PartitionSpec as P

QH = 32
KVH = 4
HD = 128
WINDOW = 4
QUAD = 4
GROUP = QH // KVH
LANES = 128
ROW_STEP = 16


rope_base = 500000.0


def moved(block, axis, target):
    size = lax.axis_size(axis)
    return lax.ppermute(block, axis, [(i, target(i) % size) for i in range(size)])


def params(mib):
    return pltpu.CompilerParams(vmem_limit_bytes=mib * 1024 * 1024)


def cost(flops, bytes_accessed):
    return pl.CostEstimate(flops=flops, bytes_accessed=bytes_accessed, transcendentals=0)


def norm_kernel(starts_ref, x_ref, gain_ref, *outs):
    rows, width = x_ref.shape[1], x_ref.shape[2]
    pieces = starts_ref.shape[1]
    piece_width = outs[0].shape[1] // pieces
    for r in range(0, rows, ROW_STEP):
        x = x_ref[0, r : r + ROW_STEP, :].astype(jnp.float32)
        scale = lax.rsqrt(jnp.sum(x * x, axis=-1, keepdims=True) / width + 1e-05)
        for i, out in enumerate(outs):
            for j in range(pieces):
                start = pl.multiple_of(starts_ref[i, j], LANES)
                xs = x_ref[0, r : r + ROW_STEP, pl.ds(start, piece_width)].astype(jnp.float32)
                gain = gain_ref[:, pl.ds(start, piece_width)]
                out[r : r + ROW_STEP, j * piece_width : (j + 1) * piece_width] = (
                    xs * scale * gain
                ).astype(jnp.bfloat16)


def normed_cuts(activations, gain, starts):
    micro_count, tok_rows, width = activations.shape
    rows = micro_count * tok_rows
    cuts = starts.shape[0]
    part = width // cuts
    return pl.pallas_call(
        norm_kernel,
        grid=(micro_count,),
        in_specs=[
            pl.BlockSpec(memory_space=pltpu.SMEM),
            pl.BlockSpec((1, tok_rows, width), lambda m: (m, 0, 0)),
            pl.BlockSpec((1, width), lambda m: (0, 0)),
        ],
        out_specs=[pl.BlockSpec((tok_rows, part), lambda m: (m, 0))] * cuts,
        out_shape=[jax.ShapeDtypeStruct((rows, part), jnp.bfloat16)] * cuts,
        compiler_params=params(16),
        cost_estimate=cost(6 * rows * width, 4 * rows * width),
        name="norm_cuts",
    )(starts, activations, gain)


def product_kernel(starts_ref, x, *refs):
    shards, out = refs[:-1], refs[-1]
    total = 0.0
    for i, shard in enumerate(shards):
        start = pl.multiple_of(starts_ref[i], LANES)
        total = total + jnp.dot(
            x[:, pl.ds(start, shard.shape[0])], shard[...], preferred_element_type=jnp.float32
        )
    out[...] = total.astype(out.dtype)


def product(starts, x, shards, dtype):
    rows, part = x.shape
    width = shards[0].shape[1]
    vmem = pl.BlockSpec(memory_space=pltpu.VMEM)
    return pl.pallas_call(
        product_kernel,
        in_specs=[pl.BlockSpec(memory_space=pltpu.SMEM)] + [vmem] * (1 + len(shards)),
        out_shape=jax.ShapeDtypeStruct((rows, width), dtype),
        compiler_params=params(24),
        cost_estimate=cost(8 * rows * part * width, 8 * (rows * part + part * width)),
        name="product",
    )(starts, x, *shards)


def added(own, parts, cols):
    total = own[:, cols]
    for part in parts:
        total = total + part[:, cols].astype(jnp.float32)
    return total


def key_sum_kernel(cosine, sine_part, own, *refs):
    parts, out = refs[:-1], refs[-1]
    for h in range(out.shape[1] // HD):
        cols = slice(h * HD, (h + 1) * HD)
        total = added(own, parts, cols)
        turned = pltpu.roll(total, HD // 2, 1)
        out[:, cols] = (total * cosine[...] + turned * sine_part[...]).astype(jnp.bfloat16)


def value_sum_kernel(own, *refs):
    parts, out = refs[:-1], refs[-1]
    out[...] = added(own, parts, slice(None)).astype(jnp.bfloat16)


def block_sum(kernel, name, own, parts, *tables):
    return pl.pallas_call(
        kernel,
        out_shape=jax.ShapeDtypeStruct(own.shape, jnp.bfloat16),
        compiler_params=params(16),
        cost_estimate=cost(10 * own.size, 12 * own.size),
        name=name,
    )(*tables, own, *parts)


def stacked(refs, odd):
    own, two_back, three_back, beside, from_even = refs
    one_back = jnp.where(odd == 1, beside[...], from_even[...])
    return jnp.concatenate([three_back[...], two_back[...], one_back, own[...]], axis=0)


def score_kernel(odd_ref, q_ref, *refs):
    key_refs, (row_pos, col_pos, weights, sums, log_sums) = refs[:5], refs[5:]
    keys = stacked(key_refs, odd_ref[0])
    tok_rows = q_ref.shape[2]
    visible = col_pos[0] <= row_pos[0]
    lane = lax.broadcasted_iota(jnp.int32, (tok_rows, LANES), 1)
    all_sums = jnp.ones((tok_rows, LANES), jnp.float32)
    all_max = jnp.zeros((tok_rows, LANES), jnp.float32)
    for h in range(GROUP):
        scores = lax.dot_general(
            q_ref[0, 0, :, h * HD : (h + 1) * HD],
            keys,
            (((1,), (1,)), ((), ())),
            preferred_element_type=jnp.float32,
        ) * HD ** (-0.5)
        scores = jnp.where(visible, scores, -jnp.inf)
        row_max = jnp.max(scores, axis=-1, keepdims=True)
        exps = jnp.exp(scores - row_max)
        running = jnp.sum(exps, axis=-1, keepdims=True)
        weights[0, 0, h * tok_rows : (h + 1) * tok_rows, :] = exps.astype(jnp.bfloat16)
        all_sums = jnp.where(lane == h, running, all_sums)
        all_max = jnp.where(lane == h, row_max, all_max)
    sums[0, 0] = all_sums
    log_sums[0] = jnp.transpose(all_max + jnp.log(all_sums))[:GROUP]


def window_specs(tok_rows):
    return [pl.BlockSpec((tok_rows, HD), lambda m, k: (m, k))] * 5


def scored(odd, queries, window, row_pos, col_pos):
    _, micro_count, tok_rows, _ = queries.shape
    keys = WINDOW * tok_rows
    return pl.pallas_call(
        score_kernel,
        grid=(micro_count, KVH),
        in_specs=[
            pl.BlockSpec(memory_space=pltpu.SMEM),
            pl.BlockSpec((1, 1, tok_rows, GROUP * HD), lambda m, k: (0, m, 0, k)),
            *window_specs(tok_rows),
            pl.BlockSpec((1, tok_rows, 1), lambda m, k: (m, 0, 0)),
            pl.BlockSpec((1, 1, keys), lambda m, k: (m, 0, 0)),
        ],
        out_specs=[
            pl.BlockSpec((1, 1, GROUP * tok_rows, keys), lambda m, k: (m, k, 0, 0)),
            pl.BlockSpec((1, 1, tok_rows, LANES), lambda m, k: (m, k, 0, 0)),
            pl.BlockSpec((1, GROUP, tok_rows), lambda m, k: (m, k, 0)),
        ],
        out_shape=[
            jax.ShapeDtypeStruct((micro_count, KVH, GROUP * tok_rows, keys), jnp.bfloat16),
            jax.ShapeDtypeStruct((micro_count, KVH, tok_rows, LANES), jnp.float32),
            jax.ShapeDtypeStruct((micro_count, QH, tok_rows), jnp.float32),
        ],
        compiler_params=params(24),
        cost_estimate=cost(2 * micro_count * QH * tok_rows * keys * HD, 8 * 2**20),
        name="scores",
    )(odd, queries, *window, row_pos, col_pos)


def mix_kernel(odd_ref, weights, sums, *refs):
    values = stacked(refs[:5], odd_ref[0])
    out = refs[5]
    tok_rows = out.shape[2]
    for k in range(KVH):
        mixed = jnp.dot(
            weights[0, k], values[:, k * HD : (k + 1) * HD], preferred_element_type=jnp.float32
        )
        share = 1.0 / sums[0, k]
        for h in range(GROUP):
            head = k * GROUP + h
            out[0, 0, :, head * HD : (head + 1) * HD] = (
                mixed[h * tok_rows : (h + 1) * tok_rows] * share[:, h : h + 1]
            ).astype(jnp.bfloat16)


def mixed_values(odd, weights, sums, window):
    micro_count, _, group_rows, keys = weights.shape
    tok_rows = group_rows // GROUP
    return pl.pallas_call(
        mix_kernel,
        grid=(micro_count,),
        in_specs=[
            pl.BlockSpec(memory_space=pltpu.SMEM),
            pl.BlockSpec((1, KVH, group_rows, keys), lambda m: (m, 0, 0, 0)),
            pl.BlockSpec((1, KVH, tok_rows, LANES), lambda m: (m, 0, 0, 0)),
            *[pl.BlockSpec((tok_rows, KVH * HD), lambda m: (m, 0))] * 5,
        ],
        out_specs=pl.BlockSpec((1, 1, tok_rows, QH * HD), lambda m: (0, m, 0, 0)),
        out_shape=jax.ShapeDtypeStruct((1, micro_count, tok_rows, QH * HD), jnp.bfloat16),
        compiler_params=params(32),
        cost_estimate=cost(2 * micro_count * QH * tok_rows * keys * HD, 8 * 2**20),
        name="mixed_values",
    )(odd, weights, sums, *window)


def on_device(handoff, norm_gain, kv_weight, queries, span_order):
    sections = lax.axis_size("section")
    cycle_size = lax.axis_size("ctx")
    own_index = lax.axis_index("ctx")
    quads = cycle_size // QUAD
    own_quad, own_place = own_index // QUAD, own_index % QUAD
    weight = kv_weight[0]
    shard_rows, kv_width = weight.shape[0], weight.shape[1] // 2
    _, micro_count, tok_rows, _ = handoff.shape

    next_gain = moved(norm_gain, "section", lambda i: i - 1).astype(jnp.float32)
    parity, own_y = own_place // 2, own_place % 2
    quad_ids = jnp.arange(quads, dtype=jnp.int32)
    cut_starts = jnp.stack(
        [(quad_ids * QUAD + 2 * p) * shard_rows for p in (parity, 1 - parity)]
    )
    cuts = normed_cuts(handoff[0], next_gain, cut_starts)

    def to_next_section(part, flip):
        route = [
            (s * cycle_size + i, (s + 1) % sections * cycle_size + (i ^ flip))
            for s in range(sections)
            for i in range(cycle_size)
        ]
        return lax.ppermute(part, ("section", "ctx"), route)

    own_rows, next_rows = to_next_section(cuts[0], 0), to_next_section(cuts[1], 2)

    def along_z(part):
        return [moved(part, "ctx", lambda i, j=j: i + QUAD * j) for j in range(1, quads)]

    def over_y(part):
        return moved(part, "ctx", lambda i: i ^ 1)

    key_part, value_part, _ = lax.optimization_barrier(
        (weight[:, :kv_width], weight[:, kv_width:], cuts)
    )
    key_line = along_z(key_part)
    late_part, _ = lax.optimization_barrier((value_part, key_line[-1]))
    value_line = along_z(late_part)
    key_y, value_y = over_y(key_part), over_y(value_part)
    passed_on, _ = lax.optimization_barrier((key_line, value_y))
    key_shards = [key_part, *key_line, key_y, *map(over_y, passed_on)]
    value_shards = [value_part, *value_line, value_y]
    line = (own_quad - quad_ids) % quads * 2
    starts = jnp.concatenate([line + own_y, line + 1 - own_y]) * shard_rows

    def partial(shards):
        return product(starts, next_rows, shards, jnp.bfloat16)

    def sent_back(part):
        return [moved(part, "ctx", lambda i: i ^ 2)]

    def near_blocks(block):
        return [moved(block, "ctx", lambda i: i + 2), moved(block, "ctx", lambda i: i ^ 1)]

    def window_of(block, two_back, beside):
        three_back = moved(two_back, "ctx", lambda i: i + 1)
        from_even = lax.ppermute(
            beside, "ctx", [(i, (i + 2) % cycle_size) for i in range(0, cycle_size, 2)]
        )
        return [block, two_back, three_back, beside, from_even]

    span_len = tok_rows // 2
    places_of = span_order[:, :, None] * span_len + jnp.arange(span_len, dtype=jnp.int32)
    all_pos = places_of.reshape(micro_count, cycle_size * tok_rows)
    col_pos = lax.dynamic_slice_in_dim(
        jnp.concatenate([all_pos[:, -(WINDOW - 1) * tok_rows :], all_pos], axis=1),
        own_index * tok_rows,
        WINDOW * tok_rows,
        1,
    )
    own_pos = col_pos[:, -tok_rows:]
    half_dim = HD // 2
    frequency = rope_base ** (-2.0 * jnp.arange(half_dim, dtype=jnp.float32) / HD)
    angles = own_pos.reshape(-1, 1).astype(jnp.float32) * frequency
    cosine, sine_part = jnp.cos(angles), jnp.sin(angles)
    cosine = jnp.concatenate([cosine, cosine], axis=1)
    sine_part = jnp.concatenate([-sine_part, sine_part], axis=1)
    odd = (own_index % 2).astype(jnp.int32).reshape(1)

    key_parts = sent_back(partial(key_shards))
    own_keys = product(starts, own_rows, key_shards, jnp.float32)
    key_block = block_sum(key_sum_kernel, "key_sum", own_keys, key_parts, cosine, sine_part)
    value_line, _ = lax.optimization_barrier((value_line, key_parts))
    value_shards += map(over_y, value_line)
    value_shards, _ = lax.optimization_barrier((value_shards, key_block))
    value_parts = sent_back(partial(value_shards))
    own_values = product(starts, own_rows, value_shards, jnp.float32)
    key_near = near_blocks(key_block)
    value_parts, _ = lax.optimization_barrier((value_parts, key_near))
    key_window = window_of(key_block, *key_near)
    weights, sums, log_sums = scored(
        odd, queries, key_window, own_pos[:, :, None], col_pos[:, None, :]
    )
    value_block = block_sum(value_sum_kernel, "value_sum", own_values, value_parts)
    value_window = window_of(value_block, *near_blocks(value_block))
    out = mixed_values(odd, weights, sums, value_window)
    return (out, log_sums[None])


def solution(mesh):
    placed = (
        P("section", None, "ctx", None),
        P("section", None),
        P("section", "ctx", None),
        P("section", None, "ctx", None),
        P(),
    )
    return jax.shard_map(
        on_device,
        mesh=mesh,
        in_specs=placed,
        out_specs=(P("section", None, "ctx", None), P("section", None, None, "ctx")),
        check_vma=False,
    )
```

```python
import jax
import jax.numpy as jnp
from jax import lax
from jax.experimental import pallas as pl
from jax.experimental.pallas import tpu as pltpu
from jax.sharding import PartitionSpec as P

QH = 32
KVH = 4
HD = 128
WINDOW = 4
QUAD = 4
GROUP = QH // KVH
LANES = 128
ROW_STEP = 16


rope_base = 500000.0


def moved(block, axis, target):
    size = lax.axis_size(axis)
    return lax.ppermute(block, axis, [(i, target(i) % size) for i in range(size)])


def params(mib):
    return pltpu.CompilerParams(vmem_limit_bytes=mib * 1024 * 1024)


def cost(flops, bytes_accessed):
    return pl.CostEstimate(flops=flops, bytes_accessed=bytes_accessed, transcendentals=0)


def norm_kernel(starts_ref, x_ref, gain_ref, *outs):
    rows, width = x_ref.shape[1], x_ref.shape[2]
    pieces = starts_ref.shape[1]
    piece_width = outs[0].shape[1] // pieces
    for r in range(0, rows, ROW_STEP):
        x = x_ref[0, r : r + ROW_STEP, :].astype(jnp.float32)
        scale = lax.rsqrt(jnp.sum(x * x, axis=-1, keepdims=True) / width + 1e-05)
        for i, out in enumerate(outs):
            for j in range(pieces):
                start = pl.multiple_of(starts_ref[i, j], LANES)
                xs = x_ref[0, r : r + ROW_STEP, pl.ds(start, piece_width)].astype(jnp.float32)
                gain = gain_ref[:, pl.ds(start, piece_width)]
                out[r : r + ROW_STEP, j * piece_width : (j + 1) * piece_width] = (
                    xs * scale * gain
                ).astype(jnp.bfloat16)


def normed_cuts(activations, gain, starts):
    micro_count, tok_rows, width = activations.shape
    rows = micro_count * tok_rows
    cuts = starts.shape[0]
    part = width // cuts
    return pl.pallas_call(
        norm_kernel,
        grid=(micro_count,),
        in_specs=[
            pl.BlockSpec(memory_space=pltpu.SMEM),
            pl.BlockSpec((1, tok_rows, width), lambda m: (m, 0, 0)),
            pl.BlockSpec((1, width), lambda m: (0, 0)),
        ],
        out_specs=[pl.BlockSpec((tok_rows, part), lambda m: (m, 0))] * cuts,
        out_shape=[jax.ShapeDtypeStruct((rows, part), jnp.bfloat16)] * cuts,
        compiler_params=params(16),
        cost_estimate=cost(6 * rows * width, 4 * rows * width),
        name="norm_cuts",
    )(starts, activations, gain)


def product_kernel(blocks, *refs):
    xs, shards, outs = refs[:blocks], refs[blocks:-blocks], refs[-blocks:]
    shard_rows = shards[0].shape[0]
    for x, out in zip(xs, outs):
        total = 0.0
        for j, shard in enumerate(shards):
            total = total + jnp.dot(
                x[:, j * shard_rows : (j + 1) * shard_rows],
                shard[...],
                preferred_element_type=jnp.float32,
            )
        out[...] = total.astype(out.dtype)


def products(xs, shards, dtype):
    rows, part = xs[0].shape
    width = shards[0].shape[1]
    blocks = len(xs)
    size = 8 * blocks * rows * part
    return pl.pallas_call(
        lambda *refs: product_kernel(blocks, *refs),
        out_shape=[jax.ShapeDtypeStruct((rows, width), dtype)] * blocks,
        compiler_params=params(24),
        cost_estimate=cost(size * width, size),
        name="products",
    )(*xs, *shards)


def added(own, parts, cols):
    total = own[:, cols]
    for part in parts:
        total = total + part[:, cols].astype(jnp.float32)
    return total


def key_sum_kernel(cosine, sine_part, own, *refs):
    parts, out = refs[:-1], refs[-1]
    for h in range(out.shape[1] // HD):
        cols = slice(h * HD, (h + 1) * HD)
        total = added(own, parts, cols)
        turned = pltpu.roll(total, HD // 2, 1)
        out[:, cols] = (total * cosine[...] + turned * sine_part[...]).astype(jnp.bfloat16)


def value_sum_kernel(own, *refs):
    parts, out = refs[:-1], refs[-1]
    out[...] = added(own, parts, slice(None)).astype(jnp.bfloat16)


def block_sum(kernel, name, own, parts, *tables):
    return pl.pallas_call(
        kernel,
        out_shape=jax.ShapeDtypeStruct(own.shape, jnp.bfloat16),
        compiler_params=params(16),
        cost_estimate=cost(10 * own.size, 12 * own.size),
        name=name,
    )(*tables, own, *parts)


def stacked(refs, odd):
    own, two_back, three_back, beside, from_even = refs
    one_back = jnp.where(odd == 1, beside[...], from_even[...])
    return jnp.concatenate([three_back[...], two_back[...], one_back, own[...]], axis=0)


def score_kernel(odd_ref, q_ref, *refs):
    key_refs, (row_pos, col_pos, weights, sums, log_sums) = refs[:5], refs[5:]
    keys = stacked(key_refs, odd_ref[0])
    tok_rows = q_ref.shape[2]
    visible = col_pos[0] <= row_pos[0]
    lane = lax.broadcasted_iota(jnp.int32, (tok_rows, LANES), 1)
    all_sums = jnp.ones((tok_rows, LANES), jnp.float32)
    all_max = jnp.zeros((tok_rows, LANES), jnp.float32)
    for h in range(GROUP):
        scores = lax.dot_general(
            q_ref[0, 0, :, h * HD : (h + 1) * HD],
            keys,
            (((1,), (1,)), ((), ())),
            preferred_element_type=jnp.float32,
        ) * HD ** (-0.5)
        scores = jnp.where(visible, scores, -jnp.inf)
        row_max = jnp.max(scores, axis=-1, keepdims=True)
        exps = jnp.exp(scores - row_max)
        running = jnp.sum(exps, axis=-1, keepdims=True)
        weights[0, 0, h * tok_rows : (h + 1) * tok_rows, :] = exps.astype(jnp.bfloat16)
        all_sums = jnp.where(lane == h, running, all_sums)
        all_max = jnp.where(lane == h, row_max, all_max)
    sums[0, 0] = all_sums
    log_sums[0] = jnp.transpose(all_max + jnp.log(all_sums))[:GROUP]


def window_specs(tok_rows):
    return [pl.BlockSpec((tok_rows, HD), lambda m, k: (m, k))] * 5


def scored(odd, queries, window, row_pos, col_pos):
    _, micro_count, tok_rows, _ = queries.shape
    keys = WINDOW * tok_rows
    return pl.pallas_call(
        score_kernel,
        grid=(micro_count, KVH),
        in_specs=[
            pl.BlockSpec(memory_space=pltpu.SMEM),
            pl.BlockSpec((1, 1, tok_rows, GROUP * HD), lambda m, k: (0, m, 0, k)),
            *window_specs(tok_rows),
            pl.BlockSpec((1, tok_rows, 1), lambda m, k: (m, 0, 0)),
            pl.BlockSpec((1, 1, keys), lambda m, k: (m, 0, 0)),
        ],
        out_specs=[
            pl.BlockSpec((1, 1, GROUP * tok_rows, keys), lambda m, k: (m, k, 0, 0)),
            pl.BlockSpec((1, 1, tok_rows, LANES), lambda m, k: (m, k, 0, 0)),
            pl.BlockSpec((1, GROUP, tok_rows), lambda m, k: (m, k, 0)),
        ],
        out_shape=[
            jax.ShapeDtypeStruct((micro_count, KVH, GROUP * tok_rows, keys), jnp.bfloat16),
            jax.ShapeDtypeStruct((micro_count, KVH, tok_rows, LANES), jnp.float32),
            jax.ShapeDtypeStruct((micro_count, QH, tok_rows), jnp.float32),
        ],
        compiler_params=params(24),
        cost_estimate=cost(2 * micro_count * QH * tok_rows * keys * HD, 8 * 2**20),
        name="scores",
    )(odd, queries, *window, row_pos, col_pos)


def mix_kernel(odd_ref, weights, sums, *refs):
    values = stacked(refs[:5], odd_ref[0])
    out = refs[5]
    tok_rows = out.shape[2]
    for k in range(KVH):
        mixed = jnp.dot(
            weights[0, k], values[:, k * HD : (k + 1) * HD], preferred_element_type=jnp.float32
        )
        share = 1.0 / sums[0, k]
        for h in range(GROUP):
            head = k * GROUP + h
            out[0, 0, :, head * HD : (head + 1) * HD] = (
                mixed[h * tok_rows : (h + 1) * tok_rows] * share[:, h : h + 1]
            ).astype(jnp.bfloat16)


def mixed_values(odd, weights, sums, window):
    micro_count, _, group_rows, keys = weights.shape
    tok_rows = group_rows // GROUP
    return pl.pallas_call(
        mix_kernel,
        grid=(micro_count,),
        in_specs=[
            pl.BlockSpec(memory_space=pltpu.SMEM),
            pl.BlockSpec((1, KVH, group_rows, keys), lambda m: (m, 0, 0, 0)),
            pl.BlockSpec((1, KVH, tok_rows, LANES), lambda m: (m, 0, 0, 0)),
            *[pl.BlockSpec((tok_rows, KVH * HD), lambda m: (m, 0))] * 5,
        ],
        out_specs=pl.BlockSpec((1, 1, tok_rows, QH * HD), lambda m: (0, m, 0, 0)),
        out_shape=jax.ShapeDtypeStruct((1, micro_count, tok_rows, QH * HD), jnp.bfloat16),
        compiler_params=params(32),
        cost_estimate=cost(2 * micro_count * QH * tok_rows * keys * HD, 8 * 2**20),
        name="mixed_values",
    )(odd, weights, sums, *window)


def on_device(handoff, norm_gain, kv_weight, queries, span_order):
    sections = lax.axis_size("section")
    cycle_size = lax.axis_size("ctx")
    own_index = lax.axis_index("ctx")
    quads = cycle_size // QUAD
    own_quad, own_place = own_index // QUAD, own_index % QUAD
    weight = kv_weight[0]
    shard_rows, kv_width = weight.shape[0], weight.shape[1] // 2
    _, micro_count, tok_rows, _ = handoff.shape

    next_gain = moved(norm_gain, "section", lambda i: i - 1).astype(jnp.float32)
    quad_order = (own_quad - jnp.arange(quads, dtype=jnp.int32)) % quads * QUAD
    flips = jnp.arange(QUAD, dtype=jnp.int32)
    cut_starts = (quad_order[None, :] + (own_place ^ flips)[:, None]) * shard_rows
    cuts = normed_cuts(handoff[0], next_gain, cut_starts)

    def to_next_section(part, flip):
        route = [
            (s * cycle_size + i, (s + 1) % sections * cycle_size + (i ^ flip))
            for s in range(sections)
            for i in range(cycle_size)
        ]
        return lax.ppermute(part, ("section", "ctx"), route)

    arrived = [to_next_section(cuts[flip], flip) for flip in range(QUAD)]

    def same_place(part):
        return [part] + [
            moved(part, "ctx", lambda i, j=j: i + QUAD * j) for j in range(1, quads)
        ]

    key_shards = same_place(weight[:, :kv_width])
    late_part, _ = lax.optimization_barrier((weight[:, kv_width:], key_shards[-1]))
    value_shards = same_place(late_part)

    def sent_back(parts):
        return [
            moved(part, "ctx", lambda i, flip=flip: i ^ flip)
            for flip, part in enumerate(parts, start=1)
        ]

    def near_blocks(block):
        return [moved(block, "ctx", lambda i: i + 2), moved(block, "ctx", lambda i: i ^ 1)]

    def window_of(block, two_back, beside):
        three_back = moved(two_back, "ctx", lambda i: i + 1)
        from_even = lax.ppermute(
            beside, "ctx", [(i, (i + 2) % cycle_size) for i in range(0, cycle_size, 2)]
        )
        return [block, two_back, three_back, beside, from_even]

    span_len = tok_rows // 2
    places_of = span_order[:, :, None] * span_len + jnp.arange(span_len, dtype=jnp.int32)
    all_pos = places_of.reshape(micro_count, cycle_size * tok_rows)
    col_pos = lax.dynamic_slice_in_dim(
        jnp.concatenate([all_pos[:, -(WINDOW - 1) * tok_rows :], all_pos], axis=1),
        own_index * tok_rows,
        WINDOW * tok_rows,
        1,
    )
    own_pos = col_pos[:, -tok_rows:]
    half_dim = HD // 2
    frequency = rope_base ** (-2.0 * jnp.arange(half_dim, dtype=jnp.float32) / HD)
    angles = own_pos.reshape(-1, 1).astype(jnp.float32) * frequency
    cosine, sine_part = jnp.cos(angles), jnp.sin(angles)
    cosine = jnp.concatenate([cosine, cosine], axis=1)
    sine_part = jnp.concatenate([-sine_part, sine_part], axis=1)
    odd = (own_index % 2).astype(jnp.int32).reshape(1)

    key_parts = sent_back(products(arrived[1:], key_shards, jnp.bfloat16))
    (own_keys,) = products(arrived[:1], key_shards, jnp.float32)
    value_products = products(arrived[1:], value_shards, jnp.bfloat16)
    key_parts, value_products = lax.optimization_barrier((key_parts, value_products))
    key_block = block_sum(key_sum_kernel, "key_sum", own_keys, key_parts, cosine, sine_part)
    value_products, _ = lax.optimization_barrier((value_products, key_block))
    value_parts = sent_back(value_products)
    (own_values,) = products(arrived[:1], value_shards, jnp.float32)
    key_near = near_blocks(key_block)
    value_parts, _ = lax.optimization_barrier((value_parts, key_near))
    key_window = window_of(key_block, *key_near)
    weights, sums, log_sums = scored(
        odd, queries, key_window, own_pos[:, :, None], col_pos[:, None, :]
    )
    value_block = block_sum(value_sum_kernel, "value_sum", own_values, value_parts)
    value_near, weights = lax.optimization_barrier((near_blocks(value_block), weights))
    value_window = window_of(value_block, *value_near)
    out = mixed_values(odd, weights, sums, value_window)
    return (out, log_sums[None])


def solution(mesh):
    placed = (
        P("section", None, "ctx", None),
        P("section", None),
        P("section", "ctx", None),
        P("section", None, "ctx", None),
        P(),
    )
    return jax.shard_map(
        on_device,
        mesh=mesh,
        in_specs=placed,
        out_specs=(P("section", None, "ctx", None), P("section", None, None, "ctx")),
        check_vma=False,
    )
```

```python
import jax
import jax.numpy as jnp
from jax import lax
from jax.experimental import pallas as pl
from jax.experimental.pallas import tpu as pltpu
from jax.sharding import PartitionSpec as P

QH = 32
KVH = 4
HD = 128
WINDOW = 4
QUAD = 4
GROUP = QH // KVH
SCALE = HD**-0.5
LOG2_E = 1.4426950408889634
LANES = 128
ROW_STEP = 16


rope_base = 500000.0


def moved(block, axis, target):
    size = lax.axis_size(axis)
    return lax.ppermute(block, axis, [(i, target(i) % size) for i in range(size)])


def params(mib):
    return pltpu.CompilerParams(vmem_limit_bytes=mib * 1024 * 1024)


def cost(flops, bytes_accessed):
    return pl.CostEstimate(flops=flops, bytes_accessed=bytes_accessed, transcendentals=0)


def norm_kernel(starts_ref, x_ref, gain_ref, *outs):
    rows, width = x_ref.shape[1], x_ref.shape[2]
    pieces = starts_ref.shape[1]
    piece_width = outs[0].shape[1] // pieces
    for r in range(0, rows, ROW_STEP):
        x = x_ref[0, r : r + ROW_STEP, :].astype(jnp.float32)
        scale = lax.rsqrt(jnp.sum(x * x, axis=-1, keepdims=True) / width + 1e-05)
        for i, out in enumerate(outs):
            for j in range(pieces):
                start = pl.multiple_of(starts_ref[i, j], LANES)
                xs = x_ref[0, r : r + ROW_STEP, pl.ds(start, piece_width)].astype(jnp.float32)
                gain = gain_ref[:, pl.ds(start, piece_width)]
                out[r : r + ROW_STEP, j * piece_width : (j + 1) * piece_width] = (
                    xs * scale * gain
                ).astype(jnp.bfloat16)


def normed_cuts(activations, gain, starts):
    micro_count, tok_rows, width = activations.shape
    rows = micro_count * tok_rows
    cuts = starts.shape[0]
    part = width // cuts
    return pl.pallas_call(
        norm_kernel,
        grid=(micro_count,),
        in_specs=[
            pl.BlockSpec(memory_space=pltpu.SMEM),
            pl.BlockSpec((1, tok_rows, width), lambda m: (m, 0, 0)),
            pl.BlockSpec((1, width), lambda m: (0, 0)),
        ],
        out_specs=[pl.BlockSpec((tok_rows, part), lambda m: (m, 0))] * cuts,
        out_shape=[jax.ShapeDtypeStruct((rows, part), jnp.bfloat16)] * cuts,
        compiler_params=params(16),
        cost_estimate=cost(6 * rows * width, 4 * rows * width),
        name="norm_cuts",
    )(starts, activations, gain)


def product_kernel(blocks, *refs):
    xs, shards, outs = refs[:blocks], refs[blocks:-blocks], refs[-blocks:]
    shard_rows = shards[0].shape[0]
    for x, out in zip(xs, outs):
        total = 0.0
        for j, shard in enumerate(shards):
            total = total + jnp.dot(
                x[:, j * shard_rows : (j + 1) * shard_rows],
                shard[...],
                preferred_element_type=jnp.float32,
            )
        out[...] = total.astype(out.dtype)


def products(xs, shards, dtype):
    rows, part = xs[0].shape
    width = shards[0].shape[1]
    blocks = len(xs)
    size = 8 * blocks * rows * part
    return pl.pallas_call(
        lambda *refs: product_kernel(blocks, *refs),
        out_shape=[jax.ShapeDtypeStruct((rows, width), dtype)] * blocks,
        compiler_params=params(24),
        cost_estimate=cost(size * width, size),
        name="products",
    )(*xs, *shards)


def added(own, parts, cols):
    total = own[:, cols]
    for part in parts:
        total = total + part[:, cols].astype(jnp.float32)
    return total


def key_sum_kernel(cosine, sine_part, own, *refs):
    parts, out = refs[:-1], refs[-1]
    for h in range(out.shape[1] // HD):
        cols = slice(h * HD, (h + 1) * HD)
        total = added(own, parts, cols)
        turned = pltpu.roll(total, HD // 2, 1)
        out[:, cols] = (total * cosine[...] + turned * sine_part[...]).astype(jnp.bfloat16)


def value_sum_kernel(own, *refs):
    parts, out = refs[:-1], refs[-1]
    out[...] = added(own, parts, slice(None)).astype(jnp.bfloat16)


def block_sum(kernel, name, own, parts, *tables):
    return pl.pallas_call(
        kernel,
        out_shape=jax.ShapeDtypeStruct(own.shape, jnp.bfloat16),
        compiler_params=params(16),
        cost_estimate=cost(10 * own.size, 12 * own.size),
        name=name,
    )(*tables, own, *parts)


def score_kernel(q_ref, *refs):
    key_refs, (row_pos, col_pos, weights, sums, log_sums) = refs[:WINDOW], refs[WINDOW:]
    keys = jnp.concatenate([ref[...] for ref in key_refs], axis=0)
    tok_rows = q_ref.shape[2]
    visible = col_pos[0] <= row_pos[0]
    lane = lax.broadcasted_iota(jnp.int32, (tok_rows, LANES), 1)
    all_sums = jnp.ones((tok_rows, LANES), jnp.float32)
    all_max = jnp.zeros((tok_rows, LANES), jnp.float32)
    for h in range(GROUP):
        dots = lax.dot_general(
            q_ref[0, 0, :, h * HD : (h + 1) * HD],
            keys,
            (((1,), (1,)), ((), ())),
            preferred_element_type=jnp.float32,
        )
        dots = jnp.where(visible, dots, -jnp.inf)
        row_max = jnp.max(dots, axis=-1, keepdims=True)
        exps = jnp.exp2((dots - row_max) * (SCALE * LOG2_E))
        running = jnp.sum(exps, axis=-1, keepdims=True)
        weights[0, 0, h * tok_rows : (h + 1) * tok_rows, :] = exps.astype(jnp.bfloat16)
        all_sums = jnp.where(lane == h, running, all_sums)
        all_max = jnp.where(lane == h, row_max, all_max)
    sums[0, 0] = all_sums
    log_sums[0] = jnp.transpose(all_max * SCALE + jnp.log(all_sums))[:GROUP]


def window_specs(tok_rows):
    return [pl.BlockSpec((tok_rows, HD), lambda m, k: (m, k))] * WINDOW


def scored(queries, window, row_pos, col_pos):
    _, micro_count, tok_rows, _ = queries.shape
    keys = WINDOW * tok_rows
    return pl.pallas_call(
        score_kernel,
        grid=(micro_count, KVH),
        in_specs=[
            pl.BlockSpec((1, 1, tok_rows, GROUP * HD), lambda m, k: (0, m, 0, k)),
            *window_specs(tok_rows),
            pl.BlockSpec((1, tok_rows, 1), lambda m, k: (m, 0, 0)),
            pl.BlockSpec((1, 1, keys), lambda m, k: (m, 0, 0)),
        ],
        out_specs=[
            pl.BlockSpec((1, 1, GROUP * tok_rows, keys), lambda m, k: (m, k, 0, 0)),
            pl.BlockSpec((1, 1, tok_rows, LANES), lambda m, k: (m, k, 0, 0)),
            pl.BlockSpec((1, GROUP, tok_rows), lambda m, k: (m, k, 0)),
        ],
        out_shape=[
            jax.ShapeDtypeStruct((micro_count, KVH, GROUP * tok_rows, keys), jnp.bfloat16),
            jax.ShapeDtypeStruct((micro_count, KVH, tok_rows, LANES), jnp.float32),
            jax.ShapeDtypeStruct((micro_count, QH, tok_rows), jnp.float32),
        ],
        compiler_params=params(24),
        cost_estimate=cost(2 * micro_count * QH * tok_rows * keys * HD, 8 * 2**20),
        name="scores",
    )(queries, *window, row_pos, col_pos)


def mix_kernel(weights, sums, *refs):
    values = jnp.concatenate([ref[...] for ref in refs[:WINDOW]], axis=0)
    out = refs[WINDOW]
    tok_rows = out.shape[2]
    for k in range(KVH):
        mixed = jnp.dot(
            weights[0, k], values[:, k * HD : (k + 1) * HD], preferred_element_type=jnp.float32
        )
        share = 1.0 / sums[0, k]
        for h in range(GROUP):
            head = k * GROUP + h
            out[0, 0, :, head * HD : (head + 1) * HD] = (
                mixed[h * tok_rows : (h + 1) * tok_rows] * share[:, h : h + 1]
            ).astype(jnp.bfloat16)


def mixed_values(weights, sums, window):
    micro_count, _, group_rows, keys = weights.shape
    tok_rows = group_rows // GROUP
    return pl.pallas_call(
        mix_kernel,
        grid=(micro_count,),
        in_specs=[
            pl.BlockSpec((1, KVH, group_rows, keys), lambda m: (m, 0, 0, 0)),
            pl.BlockSpec((1, KVH, tok_rows, LANES), lambda m: (m, 0, 0, 0)),
            *[pl.BlockSpec((tok_rows, KVH * HD), lambda m: (m, 0))] * WINDOW,
        ],
        out_specs=pl.BlockSpec((1, 1, tok_rows, QH * HD), lambda m: (0, m, 0, 0)),
        out_shape=jax.ShapeDtypeStruct((1, micro_count, tok_rows, QH * HD), jnp.bfloat16),
        compiler_params=params(32),
        cost_estimate=cost(2 * micro_count * QH * tok_rows * keys * HD, 8 * 2**20),
        name="mixed_values",
    )(weights, sums, *window)


def on_device(handoff, norm_gain, kv_weight, queries, span_order):
    sections = lax.axis_size("section")
    cycle_size = lax.axis_size("ctx")
    own_index = lax.axis_index("ctx")
    quads = cycle_size // QUAD
    own_quad, own_place = own_index // QUAD, own_index % QUAD
    weight = kv_weight[0]
    shard_rows, kv_width = weight.shape[0], weight.shape[1] // 2
    _, micro_count, tok_rows, _ = handoff.shape

    next_gain = moved(norm_gain, "section", lambda i: i - 1).astype(jnp.float32)
    quad_order = (own_quad - jnp.arange(quads, dtype=jnp.int32)) % quads * QUAD
    flips = jnp.arange(QUAD, dtype=jnp.int32)
    cut_starts = (quad_order[None, :] + (own_place ^ flips)[:, None]) * shard_rows
    cuts = normed_cuts(handoff[0], next_gain, cut_starts)

    def to_next_section(part, flip):
        route = [
            (s * cycle_size + i, (s + 1) % sections * cycle_size + (i ^ flip))
            for s in range(sections)
            for i in range(cycle_size)
        ]
        return lax.ppermute(part, ("section", "ctx"), route)

    arrived = [to_next_section(cuts[flip], flip) for flip in range(QUAD)]

    def same_place(part):
        return [part] + [
            moved(part, "ctx", lambda i, j=j: i + QUAD * j) for j in range(1, quads)
        ]

    key_shards = same_place(weight[:, :kv_width])
    late_part, _ = lax.optimization_barrier((weight[:, kv_width:], (key_shards[-1], arrived)))
    value_shards = same_place(late_part)

    def sent_back(parts):
        return [
            moved(part, "ctx", lambda i, flip=flip: i ^ flip)
            for flip, part in enumerate(parts, start=1)
        ]

    def near_blocks(block):
        return [moved(block, "ctx", lambda i, d=d: i + d) for d in (1, 2)]

    def window_of(block, one_back, two_back):
        return [moved(one_back, "ctx", lambda i: i + 2), two_back, one_back, block]

    span_len = tok_rows // 2
    places_of = span_order[:, :, None] * span_len + jnp.arange(span_len, dtype=jnp.int32)
    all_pos = places_of.reshape(micro_count, cycle_size * tok_rows)
    col_pos = lax.dynamic_slice_in_dim(
        jnp.concatenate([all_pos[:, -(WINDOW - 1) * tok_rows :], all_pos], axis=1),
        own_index * tok_rows,
        WINDOW * tok_rows,
        1,
    )
    own_pos = col_pos[:, -tok_rows:]
    half_dim = HD // 2
    frequency = rope_base ** (-2.0 * jnp.arange(half_dim, dtype=jnp.float32) / HD)
    angles = own_pos.reshape(-1, 1).astype(jnp.float32) * frequency
    cosine, sine_part = jnp.cos(angles), jnp.sin(angles)
    cosine = jnp.concatenate([cosine, cosine], axis=1)
    sine_part = jnp.concatenate([-sine_part, sine_part], axis=1)

    key_parts = sent_back(products(arrived[1:], key_shards, jnp.bfloat16))
    (own_keys,) = products(arrived[:1], key_shards, jnp.float32)
    key_block = block_sum(key_sum_kernel, "key_sum", own_keys, key_parts, cosine, sine_part)
    value_shards, _ = lax.optimization_barrier((value_shards, key_block))
    value_parts = sent_back(products(arrived[1:], value_shards, jnp.bfloat16))
    (own_values,) = products(arrived[:1], value_shards, jnp.float32)
    key_near = near_blocks(key_block)
    value_parts, _ = lax.optimization_barrier((value_parts, key_near))
    key_window = window_of(key_block, *key_near)
    weights, sums, log_sums = scored(
        queries, key_window, own_pos[:, :, None], col_pos[:, None, :]
    )
    value_block = block_sum(value_sum_kernel, "value_sum", own_values, value_parts)
    value_near, weights = lax.optimization_barrier((near_blocks(value_block), weights))
    value_window = window_of(value_block, *value_near)
    out = mixed_values(weights, sums, value_window)
    return (out, log_sums[None])


def solution(mesh):
    placed = (
        P("section", None, "ctx", None),
        P("section", None),
        P("section", "ctx", None),
        P("section", None, "ctx", None),
        P(),
    )
    return jax.shard_map(
        on_device,
        mesh=mesh,
        in_specs=placed,
        out_specs=(P("section", None, "ctx", None), P("section", None, None, "ctx")),
        check_vma=False,
    )
```

```python
import jax
import jax.numpy as jnp
from jax import lax
from jax.experimental import pallas as pl
from jax.experimental.pallas import tpu as pltpu
from jax.sharding import PartitionSpec as P

QH = 32
KVH = 4
HD = 128
WINDOW = 4
QUAD = 4
GROUP = QH // KVH
SCALE = HD**-0.5
LOG2_E = 1.4426950408889634
LANES = 128
ROW_STEP = 16


rope_base = 500000.0


def moved(block, axis, target):
    size = lax.axis_size(axis)
    return lax.ppermute(block, axis, [(i, target(i) % size) for i in range(size)])


def params(mib):
    return pltpu.CompilerParams(vmem_limit_bytes=mib * 1024 * 1024)


def cost(flops, bytes_accessed):
    return pl.CostEstimate(flops=flops, bytes_accessed=bytes_accessed, transcendentals=0)


def norm_kernel(starts_ref, x_ref, gain_ref, *outs):
    rows, width = x_ref.shape[1], x_ref.shape[2]
    pieces = starts_ref.shape[1]
    piece_width = outs[0].shape[1] // pieces
    for r in range(0, rows, ROW_STEP):
        x = x_ref[0, r : r + ROW_STEP, :].astype(jnp.float32)
        scale = lax.rsqrt(jnp.sum(x * x, axis=-1, keepdims=True) / width + 1e-05)
        for i, out in enumerate(outs):
            for j in range(pieces):
                start = pl.multiple_of(starts_ref[i, j], LANES)
                xs = x_ref[0, r : r + ROW_STEP, pl.ds(start, piece_width)].astype(jnp.float32)
                gain = gain_ref[:, pl.ds(start, piece_width)]
                out[r : r + ROW_STEP, j * piece_width : (j + 1) * piece_width] = (
                    xs * scale * gain
                ).astype(jnp.bfloat16)


def normed_cuts(activations, gain, starts):
    micro_count, tok_rows, width = activations.shape
    rows = micro_count * tok_rows
    cuts = starts.shape[0]
    part = width // cuts
    return pl.pallas_call(
        norm_kernel,
        grid=(micro_count,),
        in_specs=[
            pl.BlockSpec(memory_space=pltpu.SMEM),
            pl.BlockSpec((1, tok_rows, width), lambda m: (m, 0, 0)),
            pl.BlockSpec((1, width), lambda m: (0, 0)),
        ],
        out_specs=[pl.BlockSpec((tok_rows, part), lambda m: (m, 0))] * cuts,
        out_shape=[jax.ShapeDtypeStruct((rows, part), jnp.bfloat16)] * cuts,
        compiler_params=params(16),
        cost_estimate=cost(6 * rows * width, 4 * rows * width),
        name="norm_cuts",
    )(starts, activations, gain)


def product_kernel(blocks, *refs):
    xs, shards, out = refs[:blocks], refs[blocks:-1], refs[-1]
    rows, shard_rows = xs[0].shape[0], shards[0].shape[0]
    for i, x in enumerate(xs):
        total = 0.0
        for j, shard in enumerate(shards):
            total = total + jnp.dot(
                x[:, j * shard_rows : (j + 1) * shard_rows],
                shard[...],
                preferred_element_type=jnp.float32,
            )
        out[i * rows : (i + 1) * rows, :] = total.astype(out.dtype)


def products(xs, shards, dtype):
    rows, part = xs[0].shape
    width = shards[0].shape[1]
    blocks = len(xs)
    size = 8 * blocks * rows * part
    return pl.pallas_call(
        lambda *refs: product_kernel(blocks, *refs),
        out_shape=jax.ShapeDtypeStruct((blocks * rows, width), dtype),
        compiler_params=params(24),
        cost_estimate=cost(size * width, size),
        name="products",
    )(*xs, *shards)


def half_sum_kernel(held, arrived, own, onward):
    rows = own.shape[0]
    own[...] = held[:rows, :] + arrived[:rows, :].astype(jnp.float32)
    onward[...] = (held[rows:, :] + arrived[rows:, :].astype(jnp.float32)).astype(jnp.bfloat16)


def half_sum(held, arrived):
    rows, width = held.shape[0] // 2, held.shape[1]
    return pl.pallas_call(
        half_sum_kernel,
        out_shape=[
            jax.ShapeDtypeStruct((rows, width), jnp.float32),
            jax.ShapeDtypeStruct((rows, width), jnp.bfloat16),
        ],
        compiler_params=params(16),
        cost_estimate=cost(2 * held.size, 9 * held.size),
        name="half_sum",
    )(held, arrived)


def added(own, parts, cols):
    total = own[:, cols]
    for part in parts:
        total = total + part[:, cols].astype(jnp.float32)
    return total


def key_sum_kernel(cosine, sine_part, own, *refs):
    parts, out = refs[:-1], refs[-1]
    for h in range(out.shape[1] // HD):
        cols = slice(h * HD, (h + 1) * HD)
        total = added(own, parts, cols)
        turned = pltpu.roll(total, HD // 2, 1)
        out[:, cols] = (total * cosine[...] + turned * sine_part[...]).astype(jnp.bfloat16)


def value_sum_kernel(own, *refs):
    parts, out = refs[:-1], refs[-1]
    out[...] = added(own, parts, slice(None)).astype(jnp.bfloat16)


def block_sum(kernel, name, own, parts, *tables):
    return pl.pallas_call(
        kernel,
        out_shape=jax.ShapeDtypeStruct(own.shape, jnp.bfloat16),
        compiler_params=params(16),
        cost_estimate=cost(10 * own.size, 12 * own.size),
        name=name,
    )(*tables, own, *parts)


def score_kernel(q_ref, *refs):
    key_refs, (row_pos, col_pos, weights, sums, log_sums) = refs[:WINDOW], refs[WINDOW:]
    keys = jnp.concatenate([ref[...] for ref in key_refs], axis=0)
    tok_rows = q_ref.shape[2]
    visible = col_pos[0] <= row_pos[0]
    lane = lax.broadcasted_iota(jnp.int32, (tok_rows, LANES), 1)
    all_sums = jnp.ones((tok_rows, LANES), jnp.float32)
    all_max = jnp.zeros((tok_rows, LANES), jnp.float32)
    for h in range(GROUP):
        dots = lax.dot_general(
            q_ref[0, 0, :, h * HD : (h + 1) * HD],
            keys,
            (((1,), (1,)), ((), ())),
            preferred_element_type=jnp.float32,
        )
        dots = jnp.where(visible, dots, -jnp.inf)
        row_max = jnp.max(dots, axis=-1, keepdims=True)
        exps = jnp.exp2((dots - row_max) * (SCALE * LOG2_E))
        running = jnp.sum(exps, axis=-1, keepdims=True)
        weights[0, 0, h * tok_rows : (h + 1) * tok_rows, :] = exps.astype(jnp.bfloat16)
        all_sums = jnp.where(lane == h, running, all_sums)
        all_max = jnp.where(lane == h, row_max, all_max)
    sums[0, 0] = all_sums
    log_sums[0] = jnp.transpose(all_max * SCALE + jnp.log(all_sums))[:GROUP]


def window_specs(tok_rows):
    return [pl.BlockSpec((tok_rows, HD), lambda m, k: (m, k))] * WINDOW


def scored(queries, window, row_pos, col_pos):
    _, micro_count, tok_rows, _ = queries.shape
    keys = WINDOW * tok_rows
    return pl.pallas_call(
        score_kernel,
        grid=(micro_count, KVH),
        in_specs=[
            pl.BlockSpec((1, 1, tok_rows, GROUP * HD), lambda m, k: (0, m, 0, k)),
            *window_specs(tok_rows),
            pl.BlockSpec((1, tok_rows, 1), lambda m, k: (m, 0, 0)),
            pl.BlockSpec((1, 1, keys), lambda m, k: (m, 0, 0)),
        ],
        out_specs=[
            pl.BlockSpec((1, 1, GROUP * tok_rows, keys), lambda m, k: (m, k, 0, 0)),
            pl.BlockSpec((1, 1, tok_rows, LANES), lambda m, k: (m, k, 0, 0)),
            pl.BlockSpec((1, GROUP, tok_rows), lambda m, k: (m, k, 0)),
        ],
        out_shape=[
            jax.ShapeDtypeStruct((micro_count, KVH, GROUP * tok_rows, keys), jnp.bfloat16),
            jax.ShapeDtypeStruct((micro_count, KVH, tok_rows, LANES), jnp.float32),
            jax.ShapeDtypeStruct((micro_count, QH, tok_rows), jnp.float32),
        ],
        compiler_params=params(24),
        cost_estimate=cost(2 * micro_count * QH * tok_rows * keys * HD, 8 * 2**20),
        name="scores",
    )(queries, *window, row_pos, col_pos)


def mix_kernel(weights, sums, *refs):
    values = jnp.concatenate([ref[...] for ref in refs[:WINDOW]], axis=0)
    out = refs[WINDOW]
    tok_rows = out.shape[2]
    for k in range(KVH):
        mixed = jnp.dot(
            weights[0, k], values[:, k * HD : (k + 1) * HD], preferred_element_type=jnp.float32
        )
        share = 1.0 / sums[0, k]
        for h in range(GROUP):
            head = k * GROUP + h
            out[0, 0, :, head * HD : (head + 1) * HD] = (
                mixed[h * tok_rows : (h + 1) * tok_rows] * share[:, h : h + 1]
            ).astype(jnp.bfloat16)


def mixed_values(weights, sums, window):
    micro_count, _, group_rows, keys = weights.shape
    tok_rows = group_rows // GROUP
    return pl.pallas_call(
        mix_kernel,
        grid=(micro_count,),
        in_specs=[
            pl.BlockSpec((1, KVH, group_rows, keys), lambda m: (m, 0, 0, 0)),
            pl.BlockSpec((1, KVH, tok_rows, LANES), lambda m: (m, 0, 0, 0)),
            *[pl.BlockSpec((tok_rows, KVH * HD), lambda m: (m, 0))] * WINDOW,
        ],
        out_specs=pl.BlockSpec((1, 1, tok_rows, QH * HD), lambda m: (0, m, 0, 0)),
        out_shape=jax.ShapeDtypeStruct((1, micro_count, tok_rows, QH * HD), jnp.bfloat16),
        compiler_params=params(32),
        cost_estimate=cost(2 * micro_count * QH * tok_rows * keys * HD, 8 * 2**20),
        name="mixed_values",
    )(weights, sums, *window)


def on_device(handoff, norm_gain, kv_weight, queries, span_order):
    sections = lax.axis_size("section")
    cycle_size = lax.axis_size("ctx")
    own_index = lax.axis_index("ctx")
    quads = cycle_size // QUAD
    own_quad, own_place = own_index // QUAD, own_index % QUAD
    weight = kv_weight[0]
    shard_rows, kv_width = weight.shape[0], weight.shape[1] // 2
    _, micro_count, tok_rows, _ = handoff.shape

    next_gain = moved(norm_gain, "section", lambda i: i - 1).astype(jnp.float32)
    quad_order = (own_quad - jnp.arange(quads, dtype=jnp.int32)) % quads * QUAD
    flips = jnp.arange(QUAD, dtype=jnp.int32)
    cut_starts = (quad_order[None, :] + (own_place ^ flips)[:, None]) * shard_rows
    cuts = normed_cuts(handoff[0], next_gain, cut_starts)

    def to_next_section(part, flip):
        route = [
            (s * cycle_size + i, (s + 1) % sections * cycle_size + (i ^ flip))
            for s in range(sections)
            for i in range(cycle_size)
        ]
        return lax.ppermute(part, ("section", "ctx"), route)

    arrived = [to_next_section(cuts[flip], flip) for flip in range(QUAD)]

    def same_place(part):
        return [part] + [
            moved(part, "ctx", lambda i, j=j: i + QUAD * j) for j in range(1, quads)
        ]

    key_shards = same_place(weight[:, :kv_width])
    late_part, _ = lax.optimization_barrier((weight[:, kv_width:], key_shards[-1]))
    value_shards = same_place(late_part)

    def over_y(part):
        return moved(part, "ctx", lambda i: i ^ 1)

    def over_z(part):
        return moved(part, "ctx", lambda i: i ^ 2)

    def for_others(shards):
        return products([arrived[1], arrived[3]], shards, jnp.bfloat16)

    def held_here(shards):
        return products([arrived[0], arrived[2]], shards, jnp.float32)

    def near_blocks(block):
        return [moved(block, "ctx", lambda i, d=d: i + d) for d in (1, 2)]

    def window_of(block, one_back, two_back):
        return [moved(one_back, "ctx", lambda i: i + 2), two_back, one_back, block]

    span_len = tok_rows // 2
    places_of = span_order[:, :, None] * span_len + jnp.arange(span_len, dtype=jnp.int32)
    all_pos = places_of.reshape(micro_count, cycle_size * tok_rows)
    col_pos = lax.dynamic_slice_in_dim(
        jnp.concatenate([all_pos[:, -(WINDOW - 1) * tok_rows :], all_pos], axis=1),
        own_index * tok_rows,
        WINDOW * tok_rows,
        1,
    )
    own_pos = col_pos[:, -tok_rows:]
    half_dim = HD // 2
    frequency = rope_base ** (-2.0 * jnp.arange(half_dim, dtype=jnp.float32) / HD)
    angles = own_pos.reshape(-1, 1).astype(jnp.float32) * frequency
    cosine, sine_part = jnp.cos(angles), jnp.sin(angles)
    cosine = jnp.concatenate([cosine, cosine], axis=1)
    sine_part = jnp.concatenate([-sine_part, sine_part], axis=1)

    key_y = over_y(for_others(key_shards))
    key_held = held_here(key_shards)
    value_products, key_y = lax.optimization_barrier((for_others(value_shards), key_y))
    own_keys, onward_keys = half_sum(key_held, key_y)
    key_z = over_z(onward_keys)
    value_y = over_y(value_products)
    value_held = held_here(value_shards)
    key_block = block_sum(key_sum_kernel, "key_sum", own_keys, [key_z], cosine, sine_part)
    key_near = near_blocks(key_block)
    own_values, onward_values = half_sum(value_held, value_y)
    value_z = over_z(onward_values)
    key_window = window_of(key_block, *key_near)
    weights, sums, log_sums = scored(
        queries, key_window, own_pos[:, :, None], col_pos[:, None, :]
    )
    value_block = block_sum(value_sum_kernel, "value_sum", own_values, [value_z])
    value_window = window_of(value_block, *near_blocks(value_block))
    out = mixed_values(weights, sums, value_window)
    return (out, log_sums[None])


def solution(mesh):
    placed = (
        P("section", None, "ctx", None),
        P("section", None),
        P("section", "ctx", None),
        P("section", None, "ctx", None),
        P(),
    )
    return jax.shard_map(
        on_device,
        mesh=mesh,
        in_specs=placed,
        out_specs=(P("section", None, "ctx", None), P("section", None, None, "ctx")),
        check_vma=False,
    )
```

```python
import jax
import jax.numpy as jnp
from jax import lax
from jax.experimental import pallas as pl
from jax.experimental.pallas import tpu as pltpu
from jax.sharding import PartitionSpec as P

QH = 32
KVH = 4
HD = 128
WINDOW = 4
QUAD = 4
GROUP = QH // KVH
SCALE = HD**-0.5
LOG2_E = 1.4426950408889634
LANES = 128
ROW_STEP = 16


rope_base = 500000.0


def moved(block, axis, target):
    size = lax.axis_size(axis)
    return lax.ppermute(block, axis, [(i, target(i) % size) for i in range(size)])


def params(mib):
    return pltpu.CompilerParams(vmem_limit_bytes=mib * 1024 * 1024)


def cost(flops, bytes_accessed):
    return pl.CostEstimate(flops=flops, bytes_accessed=bytes_accessed, transcendentals=0)


def norm_kernel(starts_ref, x_ref, gain_ref, *outs):
    rows, width = x_ref.shape[1], x_ref.shape[2]
    pieces = starts_ref.shape[1]
    piece_width = outs[0].shape[1] // pieces
    for r in range(0, rows, ROW_STEP):
        x = x_ref[0, r : r + ROW_STEP, :].astype(jnp.float32)
        scale = lax.rsqrt(jnp.sum(x * x, axis=-1, keepdims=True) / width + 1e-05)
        for i, out in enumerate(outs):
            for j in range(pieces):
                start = pl.multiple_of(starts_ref[i, j], LANES)
                xs = x_ref[0, r : r + ROW_STEP, pl.ds(start, piece_width)].astype(jnp.float32)
                gain = gain_ref[:, pl.ds(start, piece_width)]
                out[r : r + ROW_STEP, j * piece_width : (j + 1) * piece_width] = (
                    xs * scale * gain
                ).astype(jnp.bfloat16)


def normed_cuts(activations, gain, starts):
    micro_count, tok_rows, width = activations.shape
    rows = micro_count * tok_rows
    cuts = starts.shape[0]
    part = width // cuts
    return pl.pallas_call(
        norm_kernel,
        grid=(micro_count,),
        in_specs=[
            pl.BlockSpec(memory_space=pltpu.SMEM),
            pl.BlockSpec((1, tok_rows, width), lambda m: (m, 0, 0)),
            pl.BlockSpec((1, width), lambda m: (0, 0)),
        ],
        out_specs=[pl.BlockSpec((tok_rows, part), lambda m: (m, 0))] * cuts,
        out_shape=[jax.ShapeDtypeStruct((rows, part), jnp.bfloat16)] * cuts,
        compiler_params=params(16),
        cost_estimate=cost(6 * rows * width, 4 * rows * width),
        name="norm_cuts",
    )(starts, activations, gain)


def product_kernel(blocks, *refs):
    xs, shards, out = refs[:blocks], refs[blocks:-1], refs[-1]
    shard_rows = shards[0].shape[0]
    first = 0
    for x in xs:
        total = 0.0
        for j, shard in enumerate(shards):
            total = total + jnp.dot(
                x[:, j * shard_rows : (j + 1) * shard_rows],
                shard[...],
                preferred_element_type=jnp.float32,
            )
        out[first : first + x.shape[0], :] = total.astype(out.dtype)
        first += x.shape[0]


def products(xs, shards, dtype):
    rows, part = sum(x.shape[0] for x in xs), xs[0].shape[1]
    width = shards[0].shape[1]
    size = 8 * rows * part
    return pl.pallas_call(
        lambda *refs: product_kernel(len(xs), *refs),
        out_shape=jax.ShapeDtypeStruct((rows, width), dtype),
        compiler_params=params(24),
        cost_estimate=cost(size * width, size),
        name="products",
    )(*xs, *shards)


def half_sum_kernel(held, arrived, own, onward):
    rows = own.shape[0]
    own[...] = held[:rows, :] + arrived[:rows, :].astype(jnp.float32)
    onward[...] = (held[rows:, :] + arrived[rows:, :].astype(jnp.float32)).astype(jnp.bfloat16)


def half_sum(held, arrived):
    rows, width = held.shape[0] // 2, held.shape[1]
    return pl.pallas_call(
        half_sum_kernel,
        out_shape=[
            jax.ShapeDtypeStruct((rows, width), jnp.float32),
            jax.ShapeDtypeStruct((rows, width), jnp.bfloat16),
        ],
        compiler_params=params(16),
        cost_estimate=cost(2 * held.size, 9 * held.size),
        name="half_sum",
    )(held, arrived)


def added(own, parts, cols):
    total = own[:, cols]
    for part in parts:
        total = total + part[:, cols].astype(jnp.float32)
    return total


def key_sum_kernel(cosine, sine_part, own, *refs):
    parts, out = refs[:-1], refs[-1]
    for h in range(out.shape[1] // HD):
        cols = slice(h * HD, (h + 1) * HD)
        total = added(own, parts, cols)
        turned = pltpu.roll(total, HD // 2, 1)
        out[:, cols] = (total * cosine[...] + turned * sine_part[...]).astype(jnp.bfloat16)


def value_sum_kernel(own, *refs):
    parts, out = refs[:-1], refs[-1]
    out[...] = added(own, parts, slice(None)).astype(jnp.bfloat16)


def block_sum(kernel, name, own, parts, *tables):
    return pl.pallas_call(
        kernel,
        out_shape=jax.ShapeDtypeStruct(own.shape, jnp.bfloat16),
        compiler_params=params(16),
        cost_estimate=cost(10 * own.size, 12 * own.size),
        name=name,
    )(*tables, own, *parts)


def score_kernel(odd_ref, q_ref, *refs):
    key_refs, (row_pos, col_pos, weights, sums, log_sums) = refs[:WINDOW], refs[WINDOW:]
    beside, two_back, before, own = [ref[...] for ref in key_refs]
    odd = odd_ref[0] == 1
    one_back, three_back = jnp.where(odd, before, beside), jnp.where(odd, beside, before)
    keys = jnp.concatenate([three_back, two_back, one_back, own], axis=0)
    tok_rows = q_ref.shape[2]
    visible = col_pos[0] <= row_pos[0]
    lane = lax.broadcasted_iota(jnp.int32, (tok_rows, LANES), 1)
    all_sums = jnp.ones((tok_rows, LANES), jnp.float32)
    all_max = jnp.zeros((tok_rows, LANES), jnp.float32)
    for h in range(GROUP):
        dots = lax.dot_general(
            q_ref[0, 0, :, h * HD : (h + 1) * HD],
            keys,
            (((1,), (1,)), ((), ())),
            preferred_element_type=jnp.float32,
        )
        dots = jnp.where(visible, dots, -jnp.inf)
        row_max = jnp.max(dots, axis=-1, keepdims=True)
        exps = jnp.exp2((dots - row_max) * (SCALE * LOG2_E))
        running = jnp.sum(exps, axis=-1, keepdims=True)
        weights[0, 0, h * tok_rows : (h + 1) * tok_rows, :] = exps.astype(jnp.bfloat16)
        all_sums = jnp.where(lane == h, running, all_sums)
        all_max = jnp.where(lane == h, row_max, all_max)
    sums[0, 0] = all_sums
    log_sums[0] = jnp.transpose(all_max * SCALE + jnp.log(all_sums))[:GROUP]


def window_specs(tok_rows):
    return [pl.BlockSpec((tok_rows, HD), lambda m, k: (m, k))] * WINDOW


def scored(odd, queries, window, row_pos, col_pos):
    _, micro_count, tok_rows, _ = queries.shape
    keys = WINDOW * tok_rows
    return pl.pallas_call(
        score_kernel,
        grid=(micro_count, KVH),
        in_specs=[
            pl.BlockSpec(memory_space=pltpu.SMEM),
            pl.BlockSpec((1, 1, tok_rows, GROUP * HD), lambda m, k: (0, m, 0, k)),
            *window_specs(tok_rows),
            pl.BlockSpec((1, tok_rows, 1), lambda m, k: (m, 0, 0)),
            pl.BlockSpec((1, 1, keys), lambda m, k: (m, 0, 0)),
        ],
        out_specs=[
            pl.BlockSpec((1, 1, GROUP * tok_rows, keys), lambda m, k: (m, k, 0, 0)),
            pl.BlockSpec((1, 1, tok_rows, LANES), lambda m, k: (m, k, 0, 0)),
            pl.BlockSpec((1, GROUP, tok_rows), lambda m, k: (m, k, 0)),
        ],
        out_shape=[
            jax.ShapeDtypeStruct((micro_count, KVH, GROUP * tok_rows, keys), jnp.bfloat16),
            jax.ShapeDtypeStruct((micro_count, KVH, tok_rows, LANES), jnp.float32),
            jax.ShapeDtypeStruct((micro_count, QH, tok_rows), jnp.float32),
        ],
        compiler_params=params(24),
        cost_estimate=cost(2 * micro_count * QH * tok_rows * keys * HD, 8 * 2**20),
        name="scores",
    )(odd, queries, *window, row_pos, col_pos)


def mix_kernel(weights, sums, *refs):
    values = jnp.concatenate([ref[...] for ref in refs[:WINDOW]], axis=0)
    out = refs[WINDOW]
    tok_rows = out.shape[2]
    for k in range(KVH):
        mixed = jnp.dot(
            weights[0, k], values[:, k * HD : (k + 1) * HD], preferred_element_type=jnp.float32
        )
        share = 1.0 / sums[0, k]
        for h in range(GROUP):
            head = k * GROUP + h
            out[0, 0, :, head * HD : (head + 1) * HD] = (
                mixed[h * tok_rows : (h + 1) * tok_rows] * share[:, h : h + 1]
            ).astype(jnp.bfloat16)


def mixed_values(weights, sums, window):
    micro_count, _, group_rows, keys = weights.shape
    tok_rows = group_rows // GROUP
    return pl.pallas_call(
        mix_kernel,
        grid=(micro_count,),
        in_specs=[
            pl.BlockSpec((1, KVH, group_rows, keys), lambda m: (m, 0, 0, 0)),
            pl.BlockSpec((1, KVH, tok_rows, LANES), lambda m: (m, 0, 0, 0)),
            *[pl.BlockSpec((tok_rows, KVH * HD), lambda m: (m, 0))] * WINDOW,
        ],
        out_specs=pl.BlockSpec((1, 1, tok_rows, QH * HD), lambda m: (0, m, 0, 0)),
        out_shape=jax.ShapeDtypeStruct((1, micro_count, tok_rows, QH * HD), jnp.bfloat16),
        compiler_params=params(32),
        cost_estimate=cost(2 * micro_count * QH * tok_rows * keys * HD, 8 * 2**20),
        name="mixed_values",
    )(weights, sums, *window)


def on_device(handoff, norm_gain, kv_weight, queries, span_order):
    sections = lax.axis_size("section")
    cycle_size = lax.axis_size("ctx")
    own_index = lax.axis_index("ctx")
    quads = cycle_size // QUAD
    own_quad, own_place = own_index // QUAD, own_index % QUAD
    weight = kv_weight[0]
    shard_rows, kv_width = weight.shape[0], weight.shape[1] // 2
    _, micro_count, tok_rows, _ = handoff.shape

    next_gain = moved(norm_gain, "section", lambda i: i - 1).astype(jnp.float32)
    odd = own_index % 2
    quad_order = (own_quad - jnp.arange(quads, dtype=jnp.int32)) % quads * QUAD
    flips = jnp.arange(QUAD, dtype=jnp.int32)
    cut_starts = (quad_order[None, :] + (own_place ^ flips)[:, None]) * shard_rows
    cuts = normed_cuts(handoff[0], next_gain, cut_starts)

    def to_next_section(part, flip):
        route = [
            (s * cycle_size + i, (s + 1) % sections * cycle_size + (i ^ flip))
            for s in range(sections)
            for i in range(cycle_size)
        ]
        return lax.ppermute(part, ("section", "ctx"), route)

    def same_place(part):
        return [part] + [
            moved(part, "ctx", lambda i, j=j: i + QUAD * j) for j in range(1, quads)
        ]

    key_shards = same_place(weight[:, :kv_width])
    late_part, _ = lax.optimization_barrier((weight[:, kv_width:], key_shards[-1]))
    value_shards = same_place(late_part)

    late_cut, _ = lax.optimization_barrier((cuts[2], key_shards[-1]))
    first_cuts = [to_next_section(cuts[flip], flip) for flip in (1, 3)]
    held_cuts = [
        to_next_section(cuts[0], 0),
        to_next_section(late_cut[:tok_rows], 2),
        to_next_section(late_cut[tok_rows:], 2),
    ]

    def over_y(part):
        return moved(part, "ctx", lambda i: i ^ 1)

    def over_z(part):
        return moved(part, "ctx", lambda i: i ^ 2)

    def for_others(shards):
        return products(first_cuts, shards, jnp.bfloat16)

    def held_here(shards):
        return products(held_cuts, shards, jnp.float32)

    def key_window_of(block, two_back):
        beside = over_y(two_back)
        onward = jnp.where(odd == 1, two_back, block)
        return [beside, two_back, moved(onward, "ctx", lambda i: i + 1), block]

    def value_window_of(block):
        one_back, two_back = [moved(block, "ctx", lambda i, d=d: i + d) for d in (1, 2)]
        return [moved(one_back, "ctx", lambda i: i + 2), two_back, one_back, block]

    span_len = tok_rows // 2
    places_of = span_order[:, :, None] * span_len + jnp.arange(span_len, dtype=jnp.int32)
    all_pos = places_of.reshape(micro_count, cycle_size * tok_rows)
    col_pos = lax.dynamic_slice_in_dim(
        jnp.concatenate([all_pos[:, -(WINDOW - 1) * tok_rows :], all_pos], axis=1),
        own_index * tok_rows,
        WINDOW * tok_rows,
        1,
    )
    own_pos = col_pos[:, -tok_rows:]
    half_dim = HD // 2
    frequency = rope_base ** (-2.0 * jnp.arange(half_dim, dtype=jnp.float32) / HD)
    angles = own_pos.reshape(-1, 1).astype(jnp.float32) * frequency
    cosine, sine_part = jnp.cos(angles), jnp.sin(angles)
    cosine = jnp.concatenate([cosine, cosine], axis=1)
    sine_part = jnp.concatenate([-sine_part, sine_part], axis=1)

    key_y = over_y(for_others(key_shards))
    own_keys, onward_keys = half_sum(held_here(key_shards), key_y)
    key_z = over_z(onward_keys)
    value_shards, _ = lax.optimization_barrier((value_shards, onward_keys))
    key_block = block_sum(key_sum_kernel, "key_sum", own_keys, [key_z], cosine, sine_part)
    key_two_back = moved(key_block, "ctx", lambda i: i + 2)
    value_y = over_y(for_others(value_shards))
    value_y, _ = lax.optimization_barrier((value_y, key_two_back))
    own_values, onward_values = half_sum(held_here(value_shards), value_y)
    value_z = over_z(onward_values)
    weights, sums, log_sums = scored(
        odd.astype(jnp.int32).reshape(1),
        queries,
        key_window_of(key_block, key_two_back),
        own_pos[:, :, None],
        col_pos[:, None, :],
    )
    value_block = block_sum(value_sum_kernel, "value_sum", own_values, [value_z])
    out = mixed_values(weights, sums, value_window_of(value_block))
    return (out, log_sums[None])


def solution(mesh):
    placed = (
        P("section", None, "ctx", None),
        P("section", None),
        P("section", "ctx", None),
        P("section", None, "ctx", None),
        P(),
    )
    return jax.shard_map(
        on_device,
        mesh=mesh,
        in_specs=placed,
        out_specs=(P("section", None, "ctx", None), P("section", None, None, "ctx")),
        check_vma=False,
    )
```

```python
import jax
import jax.numpy as jnp
from jax import lax
from jax.experimental import pallas as pl
from jax.experimental.pallas import tpu as pltpu
from jax.sharding import PartitionSpec as P

QH = 32
KVH = 4
HD = 128
WINDOW = 4
QUAD = 4
GROUP = QH // KVH
SCALE = HD**-0.5
LOG2_E = 1.4426950408889634
LANES = 128
ROW_STEP = 16


rope_base = 500000.0


def moved(block, axis, target):
    size = lax.axis_size(axis)
    return lax.ppermute(block, axis, [(i, target(i) % size) for i in range(size)])


def params(mib):
    return pltpu.CompilerParams(vmem_limit_bytes=mib * 1024 * 1024)


def cost(flops, bytes_accessed):
    return pl.CostEstimate(flops=flops, bytes_accessed=bytes_accessed, transcendentals=0)


def norm_kernel(starts_ref, x_ref, gain_ref, *outs):
    rows, width = x_ref.shape[1], x_ref.shape[2]
    pieces = starts_ref.shape[1]
    piece_width = outs[0].shape[1] // pieces
    for r in range(0, rows, ROW_STEP):
        x = x_ref[0, r : r + ROW_STEP, :].astype(jnp.float32)
        scale = lax.rsqrt(jnp.sum(x * x, axis=-1, keepdims=True) / width + 1e-05)
        for i, out in enumerate(outs):
            for j in range(pieces):
                start = pl.multiple_of(starts_ref[i, j], LANES)
                xs = x_ref[0, r : r + ROW_STEP, pl.ds(start, piece_width)].astype(jnp.float32)
                gain = gain_ref[:, pl.ds(start, piece_width)]
                out[r : r + ROW_STEP, j * piece_width : (j + 1) * piece_width] = (
                    xs * scale * gain
                ).astype(jnp.bfloat16)


def normed_cuts(activations, gain, starts):
    micro_count, tok_rows, width = activations.shape
    rows = micro_count * tok_rows
    cuts = starts.shape[0]
    part = width // cuts
    return pl.pallas_call(
        norm_kernel,
        grid=(micro_count,),
        in_specs=[
            pl.BlockSpec(memory_space=pltpu.SMEM),
            pl.BlockSpec((1, tok_rows, width), lambda m: (m, 0, 0)),
            pl.BlockSpec((1, width), lambda m: (0, 0)),
        ],
        out_specs=[pl.BlockSpec((tok_rows, part), lambda m: (m, 0))] * cuts,
        out_shape=[jax.ShapeDtypeStruct((rows, part), jnp.bfloat16)] * cuts,
        compiler_params=params(16),
        cost_estimate=cost(6 * rows * width, 4 * rows * width),
        name="norm_cuts",
    )(starts, activations, gain)


def product_kernel(counts, *refs):
    blocks = sum(counts)
    xs, shards, outs = list(refs[:blocks]), refs[blocks : -len(counts)], refs[-len(counts) :]
    shard_rows = shards[0].shape[0]
    for count, out in zip(counts, outs):
        first = 0
        for _ in range(count):
            x = xs.pop(0)
            total = 0.0
            for j, shard in enumerate(shards):
                total = total + jnp.dot(
                    x[:, j * shard_rows : (j + 1) * shard_rows],
                    shard[...],
                    preferred_element_type=jnp.float32,
                )
            out[first : first + x.shape[0], :] = total.astype(out.dtype)
            first += x.shape[0]


def products(groups, shards, dtype):
    counts = [len(group) for group in groups]
    heights = [sum(x.shape[0] for x in group) for group in groups]
    xs = [x for group in groups for x in group]
    width = shards[0].shape[1]
    size = 8 * sum(heights) * xs[0].shape[1]
    return pl.pallas_call(
        lambda *refs: product_kernel(counts, *refs),
        out_shape=[jax.ShapeDtypeStruct((height, width), dtype) for height in heights],
        compiler_params=params(24),
        cost_estimate=cost(size * width, size),
        name="products",
    )(*xs, *shards)


def half_sum_kernel(held, arrived, own, onward):
    rows = own.shape[0]
    own[...] = held[:rows, :] + arrived[:rows, :].astype(jnp.float32)
    onward[...] = (held[rows:, :] + arrived[rows:, :].astype(jnp.float32)).astype(jnp.bfloat16)


def half_sum(held, arrived):
    rows, width = held.shape[0] // 2, held.shape[1]
    return pl.pallas_call(
        half_sum_kernel,
        out_shape=[
            jax.ShapeDtypeStruct((rows, width), jnp.float32),
            jax.ShapeDtypeStruct((rows, width), jnp.bfloat16),
        ],
        compiler_params=params(16),
        cost_estimate=cost(2 * held.size, 9 * held.size),
        name="half_sum",
    )(held, arrived)


def added(own, parts, cols):
    total = own[:, cols]
    for part in parts:
        total = total + part[:, cols].astype(jnp.float32)
    return total


def key_sum_kernel(cosine, sine_part, own, *refs):
    parts, out = refs[:-1], refs[-1]
    for h in range(out.shape[1] // HD):
        cols = slice(h * HD, (h + 1) * HD)
        total = added(own, parts, cols)
        turned = pltpu.roll(total, HD // 2, 1)
        out[:, cols] = (total * cosine[...] + turned * sine_part[...]).astype(jnp.bfloat16)


def value_sum_kernel(own, *refs):
    parts, out = refs[:-1], refs[-1]
    out[...] = added(own, parts, slice(None)).astype(jnp.bfloat16)


def block_sum(kernel, name, own, parts, *tables):
    return pl.pallas_call(
        kernel,
        out_shape=jax.ShapeDtypeStruct(own.shape, jnp.bfloat16),
        compiler_params=params(16),
        cost_estimate=cost(10 * own.size, 12 * own.size),
        name=name,
    )(*tables, own, *parts)


def score_kernel(odd_ref, q_ref, *refs):
    key_refs, (row_pos, col_pos, weights, sums, log_sums) = refs[:WINDOW], refs[WINDOW:]
    beside, two_back, before, own = [ref[...] for ref in key_refs]
    odd = odd_ref[0] == 1
    one_back, three_back = jnp.where(odd, before, beside), jnp.where(odd, beside, before)
    keys = jnp.concatenate([three_back, two_back, one_back, own], axis=0)
    tok_rows = q_ref.shape[2]
    visible = col_pos[0] <= row_pos[0]
    lane = lax.broadcasted_iota(jnp.int32, (tok_rows, LANES), 1)
    all_sums = jnp.ones((tok_rows, LANES), jnp.float32)
    all_max = jnp.zeros((tok_rows, LANES), jnp.float32)
    for h in range(GROUP):
        dots = lax.dot_general(
            q_ref[0, 0, :, h * HD : (h + 1) * HD],
            keys,
            (((1,), (1,)), ((), ())),
            preferred_element_type=jnp.float32,
        )
        dots = jnp.where(visible, dots, -jnp.inf)
        row_max = jnp.max(dots, axis=-1, keepdims=True)
        exps = jnp.exp2((dots - row_max) * (SCALE * LOG2_E))
        running = jnp.sum(exps, axis=-1, keepdims=True)
        weights[0, 0, h * tok_rows : (h + 1) * tok_rows, :] = exps.astype(jnp.bfloat16)
        all_sums = jnp.where(lane == h, running, all_sums)
        all_max = jnp.where(lane == h, row_max, all_max)
    sums[0, 0] = all_sums
    log_sums[0] = jnp.transpose(all_max * SCALE + jnp.log(all_sums))[:GROUP]


def window_specs(tok_rows):
    return [pl.BlockSpec((tok_rows, HD), lambda m, k: (m, k))] * WINDOW


def scored(odd, queries, window, row_pos, col_pos):
    _, micro_count, tok_rows, _ = queries.shape
    keys = WINDOW * tok_rows
    return pl.pallas_call(
        score_kernel,
        grid=(micro_count, KVH),
        in_specs=[
            pl.BlockSpec(memory_space=pltpu.SMEM),
            pl.BlockSpec((1, 1, tok_rows, GROUP * HD), lambda m, k: (0, m, 0, k)),
            *window_specs(tok_rows),
            pl.BlockSpec((1, tok_rows, 1), lambda m, k: (m, 0, 0)),
            pl.BlockSpec((1, 1, keys), lambda m, k: (m, 0, 0)),
        ],
        out_specs=[
            pl.BlockSpec((1, 1, GROUP * tok_rows, keys), lambda m, k: (m, k, 0, 0)),
            pl.BlockSpec((1, 1, tok_rows, LANES), lambda m, k: (m, k, 0, 0)),
            pl.BlockSpec((1, GROUP, tok_rows), lambda m, k: (m, k, 0)),
        ],
        out_shape=[
            jax.ShapeDtypeStruct((micro_count, KVH, GROUP * tok_rows, keys), jnp.bfloat16),
            jax.ShapeDtypeStruct((micro_count, KVH, tok_rows, LANES), jnp.float32),
            jax.ShapeDtypeStruct((micro_count, QH, tok_rows), jnp.float32),
        ],
        compiler_params=params(24),
        cost_estimate=cost(2 * micro_count * QH * tok_rows * keys * HD, 8 * 2**20),
        name="scores",
    )(odd, queries, *window, row_pos, col_pos)


def mix_kernel(weights, sums, *refs):
    values = jnp.concatenate([ref[...] for ref in refs[:WINDOW]], axis=0)
    out = refs[WINDOW]
    tok_rows = out.shape[2]
    for k in range(KVH):
        mixed = jnp.dot(
            weights[0, k], values[:, k * HD : (k + 1) * HD], preferred_element_type=jnp.float32
        )
        share = 1.0 / sums[0, k]
        for h in range(GROUP):
            head = k * GROUP + h
            out[0, 0, :, head * HD : (head + 1) * HD] = (
                mixed[h * tok_rows : (h + 1) * tok_rows] * share[:, h : h + 1]
            ).astype(jnp.bfloat16)


def mixed_values(weights, sums, window):
    micro_count, _, group_rows, keys = weights.shape
    tok_rows = group_rows // GROUP
    return pl.pallas_call(
        mix_kernel,
        grid=(micro_count,),
        in_specs=[
            pl.BlockSpec((1, KVH, group_rows, keys), lambda m: (m, 0, 0, 0)),
            pl.BlockSpec((1, KVH, tok_rows, LANES), lambda m: (m, 0, 0, 0)),
            *[pl.BlockSpec((tok_rows, KVH * HD), lambda m: (m, 0))] * WINDOW,
        ],
        out_specs=pl.BlockSpec((1, 1, tok_rows, QH * HD), lambda m: (0, m, 0, 0)),
        out_shape=jax.ShapeDtypeStruct((1, micro_count, tok_rows, QH * HD), jnp.bfloat16),
        compiler_params=params(32),
        cost_estimate=cost(2 * micro_count * QH * tok_rows * keys * HD, 8 * 2**20),
        name="mixed_values",
    )(weights, sums, *window)


def on_device(handoff, norm_gain, kv_weight, queries, span_order):
    sections = lax.axis_size("section")
    cycle_size = lax.axis_size("ctx")
    own_index = lax.axis_index("ctx")
    quads = cycle_size // QUAD
    own_quad, own_place = own_index // QUAD, own_index % QUAD
    weight = kv_weight[0]
    shard_rows, kv_width = weight.shape[0], weight.shape[1] // 2
    _, micro_count, tok_rows, _ = handoff.shape

    next_gain = moved(norm_gain, "section", lambda i: i - 1).astype(jnp.float32)
    odd = own_index % 2
    quad_order = (own_quad - jnp.arange(quads, dtype=jnp.int32)) % quads * QUAD
    flips = jnp.arange(QUAD, dtype=jnp.int32)
    cut_starts = (quad_order[None, :] + (own_place ^ flips)[:, None]) * shard_rows
    cuts = normed_cuts(handoff[0], next_gain, cut_starts)

    def to_next_section(part, flip):
        route = [
            (s * cycle_size + i, (s + 1) % sections * cycle_size + (i ^ flip))
            for s in range(sections)
            for i in range(cycle_size)
        ]
        return lax.ppermute(part, ("section", "ctx"), route)

    def same_place(part):
        return [part] + [
            moved(part, "ctx", lambda i, j=j: i + QUAD * j) for j in range(1, quads)
        ]

    key_shards = same_place(weight[:, :kv_width])
    late_part, _ = lax.optimization_barrier((weight[:, kv_width:], key_shards[-1]))
    value_shards = same_place(late_part)

    late_cut, _ = lax.optimization_barrier((cuts[2], key_shards[-1]))
    first_cuts = [to_next_section(cuts[flip], flip) for flip in (1, 3)]
    held_cuts = [
        to_next_section(cuts[0], 0),
        to_next_section(late_cut[:tok_rows], 2),
        to_next_section(late_cut[tok_rows:], 2),
    ]

    def over_y(part):
        return moved(part, "ctx", lambda i: i ^ 1)

    def over_z(part):
        return moved(part, "ctx", lambda i: i ^ 2)

    def key_window_of(block, two_back):
        beside = over_y(two_back)
        onward = jnp.where(odd == 1, two_back, block)
        return [beside, two_back, moved(onward, "ctx", lambda i: i + 1), block]

    def value_window_of(block, weights):
        one_back, two_back = [moved(block, "ctx", lambda i, d=d: i + d) for d in (1, 2)]
        one_back, _ = lax.optimization_barrier((one_back, weights))
        return [moved(one_back, "ctx", lambda i: i + 2), two_back, one_back, block]

    span_len = tok_rows // 2
    places_of = span_order[:, :, None] * span_len + jnp.arange(span_len, dtype=jnp.int32)
    all_pos = places_of.reshape(micro_count, cycle_size * tok_rows)
    col_pos = lax.dynamic_slice_in_dim(
        jnp.concatenate([all_pos[:, -(WINDOW - 1) * tok_rows :], all_pos], axis=1),
        own_index * tok_rows,
        WINDOW * tok_rows,
        1,
    )
    own_pos = col_pos[:, -tok_rows:]
    half_dim = HD // 2
    frequency = rope_base ** (-2.0 * jnp.arange(half_dim, dtype=jnp.float32) / HD)
    angles = own_pos.reshape(-1, 1).astype(jnp.float32) * frequency
    cosine, sine_part = jnp.cos(angles), jnp.sin(angles)
    cosine = jnp.concatenate([cosine, cosine], axis=1)
    sine_part = jnp.concatenate([-sine_part, sine_part], axis=1)

    (key_products,) = products([first_cuts], key_shards, jnp.bfloat16)
    key_y = over_y(key_products)
    (key_held,) = products([held_cuts], key_shards, jnp.float32)
    own_keys, onward_keys = half_sum(key_held, key_y)
    key_z = over_z(onward_keys)
    value_shards, _ = lax.optimization_barrier((value_shards, onward_keys))
    value_products = products(
        [first_cuts[:1], held_cuts[1:], first_cuts[1:]], value_shards, jnp.bfloat16
    )
    key_z, value_products = lax.optimization_barrier((key_z, value_products))
    key_block = block_sum(key_sum_kernel, "key_sum", own_keys, [key_z], cosine, sine_part)
    key_two_back = moved(key_block, "ctx", lambda i: i + 2)
    value_parts = [
        moved(part, "ctx", lambda i, flip=flip: i ^ flip)
        for flip, part in enumerate(value_products, start=1)
    ]
    (own_values,) = products([held_cuts[:1]], value_shards, jnp.float32)
    value_parts, _ = lax.optimization_barrier((value_parts, key_two_back))
    weights, sums, log_sums = scored(
        odd.astype(jnp.int32).reshape(1),
        queries,
        key_window_of(key_block, key_two_back),
        own_pos[:, :, None],
        col_pos[:, None, :],
    )
    value_block = block_sum(value_sum_kernel, "value_sum", own_values, value_parts)
    out = mixed_values(weights, sums, value_window_of(value_block, weights))
    return (out, log_sums[None])


def solution(mesh):
    placed = (
        P("section", None, "ctx", None),
        P("section", None),
        P("section", "ctx", None),
        P("section", None, "ctx", None),
        P(),
    )
    return jax.shard_map(
        on_device,
        mesh=mesh,
        in_specs=placed,
        out_specs=(P("section", None, "ctx", None), P("section", None, None, "ctx")),
        check_vma=False,
    )
```

```python
import jax
import jax.numpy as jnp
from jax import lax
from jax.experimental import pallas as pl
from jax.experimental.pallas import tpu as pltpu
from jax.sharding import PartitionSpec as P

QH = 32
KVH = 4
HD = 128
WINDOW = 4
QUAD = 4
GROUP = QH // KVH
SCALE = HD**-0.5
LOG2_E = 1.4426950408889634
LANES = 128
ROW_STEP = 16


rope_base = 500000.0


def moved(block, axis, target):
    size = lax.axis_size(axis)
    return lax.ppermute(block, axis, [(i, target(i) % size) for i in range(size)])


def params(mib):
    return pltpu.CompilerParams(vmem_limit_bytes=mib * 1024 * 1024)


def cost(flops, bytes_accessed):
    return pl.CostEstimate(flops=flops, bytes_accessed=bytes_accessed, transcendentals=0)


def norm_kernel(starts_ref, x_ref, gain_ref, *outs):
    rows, width = x_ref.shape[1], x_ref.shape[2]
    pieces = starts_ref.shape[1]
    piece_width = outs[0].shape[1] // pieces
    for r in range(0, rows, ROW_STEP):
        x = x_ref[0, r : r + ROW_STEP, :].astype(jnp.float32)
        scale = lax.rsqrt(jnp.sum(x * x, axis=-1, keepdims=True) / width + 1e-05)
        for i, out in enumerate(outs):
            for j in range(pieces):
                start = pl.multiple_of(starts_ref[i, j], LANES)
                xs = x_ref[0, r : r + ROW_STEP, pl.ds(start, piece_width)].astype(jnp.float32)
                gain = gain_ref[:, pl.ds(start, piece_width)]
                out[r : r + ROW_STEP, j * piece_width : (j + 1) * piece_width] = (
                    xs * scale * gain
                ).astype(jnp.bfloat16)


def normed_cuts(activations, gain, starts):
    micro_count, tok_rows, width = activations.shape
    rows = micro_count * tok_rows
    cuts = starts.shape[0]
    part = width // cuts
    return pl.pallas_call(
        norm_kernel,
        grid=(micro_count,),
        in_specs=[
            pl.BlockSpec(memory_space=pltpu.SMEM),
            pl.BlockSpec((1, tok_rows, width), lambda m: (m, 0, 0)),
            pl.BlockSpec((1, width), lambda m: (0, 0)),
        ],
        out_specs=[pl.BlockSpec((tok_rows, part), lambda m: (m, 0))] * cuts,
        out_shape=[jax.ShapeDtypeStruct((rows, part), jnp.bfloat16)] * cuts,
        compiler_params=params(16),
        cost_estimate=cost(6 * rows * width, 4 * rows * width),
        name="norm_cuts",
    )(starts, activations, gain)


def product_kernel(counts, *refs):
    blocks = sum(counts)
    xs, shards, outs = list(refs[:blocks]), refs[blocks : -len(counts)], refs[-len(counts) :]
    shard_rows = shards[0].shape[0]
    for count, out in zip(counts, outs):
        first = 0
        for _ in range(count):
            x = xs.pop(0)
            total = 0.0
            for j, shard in enumerate(shards):
                total = total + jnp.dot(
                    x[:, j * shard_rows : (j + 1) * shard_rows],
                    shard[...],
                    preferred_element_type=jnp.float32,
                )
            out[first : first + x.shape[0], :] = total.astype(out.dtype)
            first += x.shape[0]


def products(groups, shards, dtype):
    counts = [len(group) for group in groups]
    heights = [sum(x.shape[0] for x in group) for group in groups]
    xs = [x for group in groups for x in group]
    width = shards[0].shape[1]
    size = 8 * sum(heights) * xs[0].shape[1]
    return pl.pallas_call(
        lambda *refs: product_kernel(counts, *refs),
        out_shape=[jax.ShapeDtypeStruct((height, width), dtype) for height in heights],
        compiler_params=params(24),
        cost_estimate=cost(size * width, size),
        name="products",
    )(*xs, *shards)


def half_sum_kernel(held, arrived, own, onward):
    rows = own.shape[0]
    own[...] = held[:rows, :] + arrived[:rows, :].astype(jnp.float32)
    onward[...] = (held[rows:, :] + arrived[rows:, :].astype(jnp.float32)).astype(jnp.bfloat16)


def half_sum(held, arrived):
    rows, width = held.shape[0] // 2, held.shape[1]
    return pl.pallas_call(
        half_sum_kernel,
        out_shape=[
            jax.ShapeDtypeStruct((rows, width), jnp.float32),
            jax.ShapeDtypeStruct((rows, width), jnp.bfloat16),
        ],
        compiler_params=params(16),
        cost_estimate=cost(2 * held.size, 9 * held.size),
        name="half_sum",
    )(held, arrived)


def added(own, parts, cols):
    total = own[:, cols]
    for part in parts:
        total = total + part[:, cols].astype(jnp.float32)
    return total


def key_sum_kernel(cosine, sine_part, own, *refs):
    parts, out = refs[:-1], refs[-1]
    for h in range(out.shape[1] // HD):
        cols = slice(h * HD, (h + 1) * HD)
        total = added(own, parts, cols)
        turned = pltpu.roll(total, HD // 2, 1)
        out[:, cols] = (total * cosine[...] + turned * sine_part[...]).astype(jnp.bfloat16)


def value_sum_kernel(own, *refs):
    parts, out = refs[:-1], refs[-1]
    out[...] = added(own, parts, slice(None)).astype(jnp.bfloat16)


def block_sum(kernel, name, own, parts, *tables):
    return pl.pallas_call(
        kernel,
        out_shape=jax.ShapeDtypeStruct(own.shape, jnp.bfloat16),
        compiler_params=params(16),
        cost_estimate=cost(10 * own.size, 12 * own.size),
        name=name,
    )(*tables, own, *parts)


def score_kernel(odd_ref, q_ref, *refs):
    key_refs, (row_pos, col_pos, weights, sums, log_sums) = refs[:WINDOW], refs[WINDOW:]
    beside, two_back, before, own = key_refs
    odd = odd_ref[0] == 1
    tok_rows = q_ref.shape[2]
    visible = col_pos[0] <= row_pos[0]
    lane = lax.broadcasted_iota(jnp.int32, (tok_rows, LANES), 1)
    for k in range(KVH):
        cols = slice(k * HD, (k + 1) * HD)
        one_back = jnp.where(odd, before[:, cols], beside[:, cols])
        three_back = jnp.where(odd, beside[:, cols], before[:, cols])
        keys = jnp.concatenate([three_back, two_back[:, cols], one_back, own[:, cols]], axis=0)
        all_sums = jnp.ones((tok_rows, LANES), jnp.float32)
        all_max = jnp.zeros((tok_rows, LANES), jnp.float32)
        for h in range(GROUP):
            head = k * GROUP + h
            dots = lax.dot_general(
                q_ref[0, 0, :, head * HD : (head + 1) * HD],
                keys,
                (((1,), (1,)), ((), ())),
                preferred_element_type=jnp.float32,
            )
            dots = jnp.where(visible, dots, -jnp.inf)
            row_max = jnp.max(dots, axis=-1, keepdims=True)
            exps = jnp.exp2((dots - row_max) * (SCALE * LOG2_E))
            running = jnp.sum(exps, axis=-1, keepdims=True)
            weights[0, k, h * tok_rows : (h + 1) * tok_rows, :] = exps.astype(jnp.bfloat16)
            all_sums = jnp.where(lane == h, running, all_sums)
            all_max = jnp.where(lane == h, row_max, all_max)
        sums[0, k] = all_sums
        log_sums[0, k * GROUP : (k + 1) * GROUP, :] = jnp.transpose(
            all_max * SCALE + jnp.log(all_sums)
        )[:GROUP]


def scored(odd, queries, window, row_pos, col_pos):
    _, micro_count, tok_rows, width = queries.shape
    keys = WINDOW * tok_rows
    return pl.pallas_call(
        score_kernel,
        grid=(micro_count,),
        in_specs=[
            pl.BlockSpec(memory_space=pltpu.SMEM),
            pl.BlockSpec((1, 1, tok_rows, width), lambda m: (0, m, 0, 0)),
            *[pl.BlockSpec((tok_rows, KVH * HD), lambda m: (m, 0))] * WINDOW,
            pl.BlockSpec((1, tok_rows, 1), lambda m: (m, 0, 0)),
            pl.BlockSpec((1, 1, keys), lambda m: (m, 0, 0)),
        ],
        out_specs=[
            pl.BlockSpec((1, KVH, GROUP * tok_rows, keys), lambda m: (m, 0, 0, 0)),
            pl.BlockSpec((1, KVH, tok_rows, LANES), lambda m: (m, 0, 0, 0)),
            pl.BlockSpec((1, QH, tok_rows), lambda m: (m, 0, 0)),
        ],
        out_shape=[
            jax.ShapeDtypeStruct((micro_count, KVH, GROUP * tok_rows, keys), jnp.bfloat16),
            jax.ShapeDtypeStruct((micro_count, KVH, tok_rows, LANES), jnp.float32),
            jax.ShapeDtypeStruct((micro_count, QH, tok_rows), jnp.float32),
        ],
        compiler_params=params(32),
        cost_estimate=cost(2 * micro_count * QH * tok_rows * keys * HD, 8 * 2**20),
        name="scores",
    )(odd, queries, *window, row_pos, col_pos)


def mix_kernel(weights, sums, *refs):
    values = jnp.concatenate([ref[...] for ref in refs[:WINDOW]], axis=0)
    out = refs[WINDOW]
    tok_rows = out.shape[2]
    for k in range(KVH):
        mixed = jnp.dot(
            weights[0, k], values[:, k * HD : (k + 1) * HD], preferred_element_type=jnp.float32
        )
        share = 1.0 / sums[0, k]
        for h in range(GROUP):
            head = k * GROUP + h
            out[0, 0, :, head * HD : (head + 1) * HD] = (
                mixed[h * tok_rows : (h + 1) * tok_rows] * share[:, h : h + 1]
            ).astype(jnp.bfloat16)


def mixed_values(weights, sums, window):
    micro_count, _, group_rows, keys = weights.shape
    tok_rows = group_rows // GROUP
    return pl.pallas_call(
        mix_kernel,
        grid=(micro_count,),
        in_specs=[
            pl.BlockSpec((1, KVH, group_rows, keys), lambda m: (m, 0, 0, 0)),
            pl.BlockSpec((1, KVH, tok_rows, LANES), lambda m: (m, 0, 0, 0)),
            *[pl.BlockSpec((tok_rows, KVH * HD), lambda m: (m, 0))] * WINDOW,
        ],
        out_specs=pl.BlockSpec((1, 1, tok_rows, QH * HD), lambda m: (0, m, 0, 0)),
        out_shape=jax.ShapeDtypeStruct((1, micro_count, tok_rows, QH * HD), jnp.bfloat16),
        compiler_params=params(32),
        cost_estimate=cost(2 * micro_count * QH * tok_rows * keys * HD, 8 * 2**20),
        name="mixed_values",
    )(weights, sums, *window)


def on_device(handoff, norm_gain, kv_weight, queries, span_order):
    sections = lax.axis_size("section")
    cycle_size = lax.axis_size("ctx")
    own_index = lax.axis_index("ctx")
    quads = cycle_size // QUAD
    own_quad, own_place = own_index // QUAD, own_index % QUAD
    weight = kv_weight[0]
    shard_rows, kv_width = weight.shape[0], weight.shape[1] // 2
    _, micro_count, tok_rows, _ = handoff.shape

    next_gain = moved(norm_gain, "section", lambda i: i - 1).astype(jnp.float32)
    odd = own_index % 2
    quad_order = (own_quad - jnp.arange(quads, dtype=jnp.int32)) % quads * QUAD
    flips = jnp.arange(QUAD, dtype=jnp.int32)
    cut_starts = (quad_order[None, :] + (own_place ^ flips)[:, None]) * shard_rows
    cuts = normed_cuts(handoff[0], next_gain, cut_starts)

    def to_next_section(part, flip):
        route = [
            (s * cycle_size + i, (s + 1) % sections * cycle_size + (i ^ flip))
            for s in range(sections)
            for i in range(cycle_size)
        ]
        return lax.ppermute(part, ("section", "ctx"), route)

    def same_place(part):
        return [part] + [
            moved(part, "ctx", lambda i, j=j: i + QUAD * j) for j in range(1, quads)
        ]

    key_shards = same_place(weight[:, :kv_width])
    late_part, _ = lax.optimization_barrier((weight[:, kv_width:], key_shards[-1]))
    value_shards = same_place(late_part)

    late_cut, _ = lax.optimization_barrier((cuts[2], key_shards[-1]))
    first_cuts = [to_next_section(cuts[flip], flip) for flip in (1, 3)]
    held_cuts = [
        to_next_section(cuts[0], 0),
        to_next_section(late_cut[:tok_rows], 2),
        to_next_section(late_cut[tok_rows:], 2),
    ]

    def over_y(part):
        return moved(part, "ctx", lambda i: i ^ 1)

    def over_z(part):
        return moved(part, "ctx", lambda i: i ^ 2)

    def key_window_of(block, two_back):
        beside = over_y(two_back)
        onward = jnp.where(odd == 1, two_back, block)
        return [beside, two_back, moved(onward, "ctx", lambda i: i + 1), block]

    def value_window_of(block):
        one_back, two_back = [moved(block, "ctx", lambda i, d=d: i + d) for d in (1, 2)]
        return [moved(one_back, "ctx", lambda i: i + 2), two_back, one_back, block]

    span_len = tok_rows // 2
    places_of = span_order[:, :, None] * span_len + jnp.arange(span_len, dtype=jnp.int32)
    all_pos = places_of.reshape(micro_count, cycle_size * tok_rows)
    col_pos = lax.dynamic_slice_in_dim(
        jnp.concatenate([all_pos[:, -(WINDOW - 1) * tok_rows :], all_pos], axis=1),
        own_index * tok_rows,
        WINDOW * tok_rows,
        1,
    )
    own_pos = col_pos[:, -tok_rows:]
    half_dim = HD // 2
    frequency = rope_base ** (-2.0 * jnp.arange(half_dim, dtype=jnp.float32) / HD)
    angles = own_pos.reshape(-1, 1).astype(jnp.float32) * frequency
    cosine, sine_part = jnp.cos(angles), jnp.sin(angles)
    cosine = jnp.concatenate([cosine, cosine], axis=1)
    sine_part = jnp.concatenate([-sine_part, sine_part], axis=1)

    (key_products,) = products([first_cuts], key_shards, jnp.bfloat16)
    key_y = over_y(key_products)
    (key_held,) = products([held_cuts], key_shards, jnp.float32)
    own_keys, onward_keys = half_sum(key_held, key_y)
    key_z = over_z(onward_keys)
    value_shards, _ = lax.optimization_barrier((value_shards, onward_keys))
    value_products = products(
        [first_cuts[:1], held_cuts[1:], first_cuts[1:]], value_shards, jnp.bfloat16
    )
    key_z, value_products = lax.optimization_barrier((key_z, value_products))
    key_block = block_sum(key_sum_kernel, "key_sum", own_keys, [key_z], cosine, sine_part)
    key_two_back = moved(key_block, "ctx", lambda i: i + 2)
    value_parts = [
        moved(part, "ctx", lambda i, flip=flip: i ^ flip)
        for flip, part in enumerate(value_products, start=1)
    ]
    (own_values,) = products([held_cuts[:1]], value_shards, jnp.float32)
    value_parts, _ = lax.optimization_barrier((value_parts, key_two_back))
    weights, sums, log_sums = scored(
        odd.astype(jnp.int32).reshape(1),
        queries,
        key_window_of(key_block, key_two_back),
        own_pos[:, :, None],
        col_pos[:, None, :],
    )
    value_block = block_sum(value_sum_kernel, "value_sum", own_values, value_parts)
    out = mixed_values(weights, sums, value_window_of(value_block))
    return (out, log_sums[None])


def solution(mesh):
    placed = (
        P("section", None, "ctx", None),
        P("section", None),
        P("section", "ctx", None),
        P("section", None, "ctx", None),
        P(),
    )
    return jax.shard_map(
        on_device,
        mesh=mesh,
        in_specs=placed,
        out_specs=(P("section", None, "ctx", None), P("section", None, None, "ctx")),
        check_vma=False,
    )
```

```python
import jax
import jax.numpy as jnp
from jax import lax
from jax.experimental import pallas as pl
from jax.experimental.pallas import tpu as pltpu
from jax.sharding import PartitionSpec as P

QH = 32
KVH = 4
HD = 128
WINDOW = 4
QUAD = 4
GROUP = QH // KVH
SCALE = HD**-0.5
LOG2_E = 1.4426950408889634
LANES = 128
ROW_STEP = 16


rope_base = 500000.0


def moved(block, axis, target):
    size = lax.axis_size(axis)
    return lax.ppermute(block, axis, [(i, target(i) % size) for i in range(size)])


def params(mib):
    return pltpu.CompilerParams(vmem_limit_bytes=mib * 1024 * 1024)


def cost(flops, bytes_accessed):
    return pl.CostEstimate(flops=flops, bytes_accessed=bytes_accessed, transcendentals=0)


def norm_kernel(starts_ref, x_ref, gain_ref, *outs):
    rows, width = x_ref.shape[1], x_ref.shape[2]
    pieces = starts_ref.shape[1]
    piece_width = outs[0].shape[1] // pieces
    for r in range(0, rows, ROW_STEP):
        x = x_ref[0, r : r + ROW_STEP, :].astype(jnp.float32)
        scale = lax.rsqrt(jnp.sum(x * x, axis=-1, keepdims=True) / width + 1e-05)
        for i, out in enumerate(outs):
            for j in range(pieces):
                start = pl.multiple_of(starts_ref[i, j], LANES)
                xs = x_ref[0, r : r + ROW_STEP, pl.ds(start, piece_width)].astype(jnp.float32)
                gain = gain_ref[:, pl.ds(start, piece_width)]
                out[r : r + ROW_STEP, j * piece_width : (j + 1) * piece_width] = (
                    xs * scale * gain
                ).astype(jnp.bfloat16)


def normed_cuts(activations, gain, starts):
    micro_count, tok_rows, width = activations.shape
    rows = micro_count * tok_rows
    cuts = starts.shape[0]
    part = width // cuts
    return pl.pallas_call(
        norm_kernel,
        grid=(micro_count,),
        in_specs=[
            pl.BlockSpec(memory_space=pltpu.SMEM),
            pl.BlockSpec((1, tok_rows, width), lambda m: (m, 0, 0)),
            pl.BlockSpec((1, width), lambda m: (0, 0)),
        ],
        out_specs=[pl.BlockSpec((tok_rows, part), lambda m: (m, 0))] * cuts,
        out_shape=[jax.ShapeDtypeStruct((rows, part), jnp.bfloat16)] * cuts,
        compiler_params=params(16),
        cost_estimate=cost(6 * rows * width, 4 * rows * width),
        name="norm_cuts",
    )(starts, activations, gain)


def product_kernel(counts, *refs):
    blocks = sum(counts)
    xs, shards, outs = list(refs[:blocks]), refs[blocks : -len(counts)], refs[-len(counts) :]
    shard_rows = shards[0].shape[0]
    for count, out in zip(counts, outs):
        first = 0
        for _ in range(count):
            x = xs.pop(0)
            total = 0.0
            for j, shard in enumerate(shards):
                total = total + jnp.dot(
                    x[:, j * shard_rows : (j + 1) * shard_rows],
                    shard[...],
                    preferred_element_type=jnp.float32,
                )
            out[first : first + x.shape[0], :] = total.astype(out.dtype)
            first += x.shape[0]


def products(groups, shards, dtype):
    counts = [len(group) for group in groups]
    heights = [sum(x.shape[0] for x in group) for group in groups]
    xs = [x for group in groups for x in group]
    width = shards[0].shape[1]
    size = 8 * sum(heights) * xs[0].shape[1]
    return pl.pallas_call(
        lambda *refs: product_kernel(counts, *refs),
        out_shape=[jax.ShapeDtypeStruct((height, width), dtype) for height in heights],
        compiler_params=params(24),
        cost_estimate=cost(size * width, size),
        name="products",
    )(*xs, *shards)


def half_sum_kernel(held, arrived, own, onward):
    rows = own.shape[0]
    own[...] = held[:rows, :] + arrived[:rows, :].astype(jnp.float32)
    onward[...] = (held[rows:, :] + arrived[rows:, :].astype(jnp.float32)).astype(jnp.bfloat16)


def half_sum(held, arrived):
    rows, width = held.shape[0] // 2, held.shape[1]
    return pl.pallas_call(
        half_sum_kernel,
        out_shape=[
            jax.ShapeDtypeStruct((rows, width), jnp.float32),
            jax.ShapeDtypeStruct((rows, width), jnp.bfloat16),
        ],
        compiler_params=params(16),
        cost_estimate=cost(2 * held.size, 9 * held.size),
        name="half_sum",
    )(held, arrived)


def added(own, parts, cols):
    total = own[:, cols]
    for part in parts:
        total = total + part[:, cols].astype(jnp.float32)
    return total


def key_sum_kernel(cosine, sine_part, own, *refs):
    parts, out = refs[:-1], refs[-1]
    for h in range(out.shape[1] // HD):
        cols = slice(h * HD, (h + 1) * HD)
        total = added(own, parts, cols)
        turned = pltpu.roll(total, HD // 2, 1)
        out[:, cols] = (total * cosine[...] + turned * sine_part[...]).astype(jnp.bfloat16)


def value_sum_kernel(own, *refs):
    parts, out = refs[:-1], refs[-1]
    out[...] = added(own, parts, slice(None)).astype(jnp.bfloat16)


def block_sum(kernel, name, own, parts, *tables):
    return pl.pallas_call(
        kernel,
        out_shape=jax.ShapeDtypeStruct(own.shape, jnp.bfloat16),
        compiler_params=params(16),
        cost_estimate=cost(10 * own.size, 12 * own.size),
        name=name,
    )(*tables, own, *parts)


def score_kernel(odd_ref, q_ref, *refs):
    key_refs, (row_pos, col_pos, weights, sums, log_sums) = refs[:WINDOW], refs[WINDOW:]
    beside, two_back, before, own = key_refs
    odd = odd_ref[0] == 1
    tok_rows = q_ref.shape[2]
    visible = col_pos[0] <= row_pos[0]
    lane = lax.broadcasted_iota(jnp.int32, (tok_rows, LANES), 1)
    for k in range(KVH):
        cols = slice(k * HD, (k + 1) * HD)
        one_back = jnp.where(odd, before[:, cols], beside[:, cols])
        three_back = jnp.where(odd, beside[:, cols], before[:, cols])
        keys = jnp.concatenate([three_back, two_back[:, cols], one_back, own[:, cols]], axis=0)
        all_sums = jnp.ones((tok_rows, LANES), jnp.float32)
        all_max = jnp.zeros((tok_rows, LANES), jnp.float32)
        for h in range(GROUP):
            head = k * GROUP + h
            dots = lax.dot_general(
                q_ref[0, 0, :, head * HD : (head + 1) * HD],
                keys,
                (((1,), (1,)), ((), ())),
                preferred_element_type=jnp.float32,
            )
            dots = jnp.where(visible, dots, -jnp.inf)
            row_max = jnp.max(dots, axis=-1, keepdims=True)
            exps = jnp.exp2((dots - row_max) * (SCALE * LOG2_E))
            running = jnp.sum(exps, axis=-1, keepdims=True)
            weights[0, k, h * tok_rows : (h + 1) * tok_rows, :] = exps.astype(jnp.bfloat16)
            all_sums = jnp.where(lane == h, running, all_sums)
            all_max = jnp.where(lane == h, row_max, all_max)
        sums[0, k] = all_sums
        log_sums[0, k * GROUP : (k + 1) * GROUP, :] = jnp.transpose(
            all_max * SCALE + jnp.log(all_sums)
        )[:GROUP]


def scored(odd, queries, window, row_pos, col_pos):
    _, micro_count, tok_rows, width = queries.shape
    keys = WINDOW * tok_rows
    return pl.pallas_call(
        score_kernel,
        grid=(micro_count,),
        in_specs=[
            pl.BlockSpec(memory_space=pltpu.SMEM),
            pl.BlockSpec((1, 1, tok_rows, width), lambda m: (0, m, 0, 0)),
            *[pl.BlockSpec((tok_rows, KVH * HD), lambda m: (m, 0))] * WINDOW,
            pl.BlockSpec((1, tok_rows, 1), lambda m: (m, 0, 0)),
            pl.BlockSpec((1, 1, keys), lambda m: (m, 0, 0)),
        ],
        out_specs=[
            pl.BlockSpec((1, KVH, GROUP * tok_rows, keys), lambda m: (m, 0, 0, 0)),
            pl.BlockSpec((1, KVH, tok_rows, LANES), lambda m: (m, 0, 0, 0)),
            pl.BlockSpec((1, QH, tok_rows), lambda m: (m, 0, 0)),
        ],
        out_shape=[
            jax.ShapeDtypeStruct((micro_count, KVH, GROUP * tok_rows, keys), jnp.bfloat16),
            jax.ShapeDtypeStruct((micro_count, KVH, tok_rows, LANES), jnp.float32),
            jax.ShapeDtypeStruct((micro_count, QH, tok_rows), jnp.float32),
        ],
        compiler_params=params(32),
        cost_estimate=cost(2 * micro_count * QH * tok_rows * keys * HD, 8 * 2**20),
        name="scores",
    )(odd, queries, *window, row_pos, col_pos)


def mix_kernel(weights, sums, *refs):
    values = jnp.concatenate([ref[...] for ref in refs[:WINDOW]], axis=0)
    out = refs[WINDOW]
    tok_rows = out.shape[2]
    for k in range(KVH):
        mixed = jnp.dot(
            weights[0, k], values[:, k * HD : (k + 1) * HD], preferred_element_type=jnp.float32
        )
        share = 1.0 / sums[0, k]
        for h in range(GROUP):
            head = k * GROUP + h
            out[0, 0, :, head * HD : (head + 1) * HD] = (
                mixed[h * tok_rows : (h + 1) * tok_rows] * share[:, h : h + 1]
            ).astype(jnp.bfloat16)


def mixed_values(weights, sums, window):
    micro_count, _, group_rows, keys = weights.shape
    tok_rows = group_rows // GROUP
    return pl.pallas_call(
        mix_kernel,
        grid=(micro_count,),
        in_specs=[
            pl.BlockSpec((1, KVH, group_rows, keys), lambda m: (m, 0, 0, 0)),
            pl.BlockSpec((1, KVH, tok_rows, LANES), lambda m: (m, 0, 0, 0)),
            *[pl.BlockSpec((tok_rows, KVH * HD), lambda m: (m, 0))] * WINDOW,
        ],
        out_specs=pl.BlockSpec((1, 1, tok_rows, QH * HD), lambda m: (0, m, 0, 0)),
        out_shape=jax.ShapeDtypeStruct((1, micro_count, tok_rows, QH * HD), jnp.bfloat16),
        compiler_params=params(32),
        cost_estimate=cost(2 * micro_count * QH * tok_rows * keys * HD, 8 * 2**20),
        name="mixed_values",
    )(weights, sums, *window)


def on_device(handoff, norm_gain, kv_weight, queries, span_order):
    sections = lax.axis_size("section")
    cycle_size = lax.axis_size("ctx")
    own_index = lax.axis_index("ctx")
    quads = cycle_size // QUAD
    own_quad, own_place = own_index // QUAD, own_index % QUAD
    weight = kv_weight[0]
    shard_rows, kv_width = weight.shape[0], weight.shape[1] // 2
    _, micro_count, tok_rows, _ = handoff.shape

    next_gain = moved(norm_gain, "section", lambda i: i - 1).astype(jnp.float32)
    odd = own_index % 2
    quad_order = (own_quad - jnp.arange(quads, dtype=jnp.int32)) % quads * QUAD
    flips = jnp.arange(QUAD, dtype=jnp.int32)
    cut_starts = (quad_order[None, :] + (own_place ^ flips)[:, None]) * shard_rows
    cuts = normed_cuts(handoff[0], next_gain, cut_starts)

    def to_next_section(part, flip):
        route = [
            (s * cycle_size + i, (s + 1) % sections * cycle_size + (i ^ flip))
            for s in range(sections)
            for i in range(cycle_size)
        ]
        return lax.ppermute(part, ("section", "ctx"), route)

    def same_place(part):
        return [part] + [
            moved(part, "ctx", lambda i, j=j: i + QUAD * j) for j in range(1, quads)
        ]

    key_shards = same_place(weight[:, :kv_width])
    late_part, _ = lax.optimization_barrier((weight[:, kv_width:], key_shards[-1]))
    value_shards = same_place(late_part)

    late_cut, _ = lax.optimization_barrier((cuts[2], key_shards[-1]))
    first_cuts = [to_next_section(cuts[flip], flip) for flip in (1, 3)]
    held_cuts = [
        to_next_section(cuts[0], 0),
        to_next_section(late_cut[:tok_rows], 2),
        to_next_section(late_cut[tok_rows:], 2),
    ]

    def over_y(part):
        return moved(part, "ctx", lambda i: i ^ 1)

    def over_z(part):
        return moved(part, "ctx", lambda i: i ^ 2)

    def key_window_of(block, two_back):
        beside = over_y(two_back)
        onward = jnp.where(odd == 1, two_back, block)
        return [beside, two_back, moved(onward, "ctx", lambda i: i + 1), block]

    def value_window_of(block):
        one_back, two_back = [moved(block, "ctx", lambda i, d=d: i + d) for d in (1, 2)]
        return [moved(one_back, "ctx", lambda i: i + 2), two_back, one_back, block]

    span_len = tok_rows // 2
    places_of = span_order[:, :, None] * span_len + jnp.arange(span_len, dtype=jnp.int32)
    all_pos = places_of.reshape(micro_count, cycle_size * tok_rows)
    col_pos = lax.dynamic_slice_in_dim(
        jnp.concatenate([all_pos[:, -(WINDOW - 1) * tok_rows :], all_pos], axis=1),
        own_index * tok_rows,
        WINDOW * tok_rows,
        1,
    )
    own_pos = col_pos[:, -tok_rows:]
    half_dim = HD // 2
    frequency = rope_base ** (-2.0 * jnp.arange(half_dim, dtype=jnp.float32) / HD)
    angles = own_pos.reshape(-1, 1).astype(jnp.float32) * frequency
    cosine, sine_part = jnp.cos(angles), jnp.sin(angles)
    cosine = jnp.concatenate([cosine, cosine], axis=1)
    sine_part = jnp.concatenate([-sine_part, sine_part], axis=1)

    (key_products,) = products([first_cuts], key_shards, jnp.bfloat16)
    key_y = over_y(key_products)
    (key_held,) = products([held_cuts], key_shards, jnp.float32)
    own_keys, onward_keys = half_sum(key_held, key_y)
    key_z = over_z(onward_keys)
    value_shards, _ = lax.optimization_barrier((value_shards, onward_keys))
    value_products = products(
        [first_cuts[:1], held_cuts[1:], first_cuts[1:]], value_shards, jnp.bfloat16
    )
    key_block = block_sum(key_sum_kernel, "key_sum", own_keys, [key_z], cosine, sine_part)
    key_two_back = moved(key_block, "ctx", lambda i: i + 2)
    value_parts = [
        moved(part, "ctx", lambda i, flip=flip: i ^ flip)
        for flip, part in enumerate(value_products, start=1)
    ]
    (own_values,) = products([held_cuts[:1]], value_shards, jnp.float32)
    value_parts, _ = lax.optimization_barrier((value_parts, key_two_back))
    weights, sums, log_sums = scored(
        odd.astype(jnp.int32).reshape(1),
        queries,
        key_window_of(key_block, key_two_back),
        own_pos[:, :, None],
        col_pos[:, None, :],
    )
    value_block = block_sum(value_sum_kernel, "value_sum", own_values, value_parts)
    out = mixed_values(weights, sums, value_window_of(value_block))
    return (out, log_sums[None])


def solution(mesh):
    placed = (
        P("section", None, "ctx", None),
        P("section", None),
        P("section", "ctx", None),
        P("section", None, "ctx", None),
        P(),
    )
    return jax.shard_map(
        on_device,
        mesh=mesh,
        in_specs=placed,
        out_specs=(P("section", None, "ctx", None), P("section", None, None, "ctx")),
        check_vma=False,
    )
```

```python
import jax
import jax.numpy as jnp
from jax import lax
from jax.experimental import pallas as pl
from jax.experimental.pallas import tpu as pltpu
from jax.sharding import PartitionSpec as P

QH = 32
KVH = 4
HD = 128
WINDOW = 4
QUAD = 4
GROUP = QH // KVH
SCALE = HD**-0.5
LOG2_E = 1.4426950408889634
LANES = 128
ROW_STEP = 16


rope_base = 500000.0


def moved(block, axis, target):
    size = lax.axis_size(axis)
    return lax.ppermute(block, axis, [(i, target(i) % size) for i in range(size)])


def params(mib):
    return pltpu.CompilerParams(vmem_limit_bytes=mib * 1024 * 1024)


def cost(flops, bytes_accessed):
    return pl.CostEstimate(flops=flops, bytes_accessed=bytes_accessed, transcendentals=0)


def norm_kernel(starts_ref, x_ref, gain_ref, *outs):
    rows, width = x_ref.shape[1], x_ref.shape[2]
    pieces = starts_ref.shape[1]
    piece_width = outs[0].shape[1] // pieces
    for r in range(0, rows, ROW_STEP):
        x = x_ref[0, r : r + ROW_STEP, :].astype(jnp.float32)
        scale = lax.rsqrt(jnp.sum(x * x, axis=-1, keepdims=True) / width + 1e-05)
        for i, out in enumerate(outs):
            for j in range(pieces):
                start = pl.multiple_of(starts_ref[i, j], LANES)
                xs = x_ref[0, r : r + ROW_STEP, pl.ds(start, piece_width)].astype(jnp.float32)
                gain = gain_ref[:, pl.ds(start, piece_width)]
                out[r : r + ROW_STEP, j * piece_width : (j + 1) * piece_width] = (
                    xs * scale * gain
                ).astype(jnp.bfloat16)


def normed_cuts(activations, gain, starts):
    micro_count, tok_rows, width = activations.shape
    rows = micro_count * tok_rows
    cuts = starts.shape[0]
    part = width // cuts
    return pl.pallas_call(
        norm_kernel,
        grid=(micro_count,),
        in_specs=[
            pl.BlockSpec(memory_space=pltpu.SMEM),
            pl.BlockSpec((1, tok_rows, width), lambda m: (m, 0, 0)),
            pl.BlockSpec((1, width), lambda m: (0, 0)),
        ],
        out_specs=[pl.BlockSpec((tok_rows, part), lambda m: (m, 0))] * cuts,
        out_shape=[jax.ShapeDtypeStruct((rows, part), jnp.bfloat16)] * cuts,
        compiler_params=params(16),
        cost_estimate=cost(6 * rows * width, 4 * rows * width),
        name="norm_cuts",
    )(starts, activations, gain)


def product_kernel(counts, *refs):
    blocks = sum(counts)
    xs, shards, outs = list(refs[:blocks]), refs[blocks : -len(counts)], refs[-len(counts) :]
    shard_rows = shards[0].shape[0]
    for count, out in zip(counts, outs):
        first = 0
        for _ in range(count):
            x = xs.pop(0)
            total = 0.0
            for j, shard in enumerate(shards):
                total = total + jnp.dot(
                    x[:, j * shard_rows : (j + 1) * shard_rows],
                    shard[...],
                    preferred_element_type=jnp.float32,
                )
            out[first : first + x.shape[0], :] = total.astype(out.dtype)
            first += x.shape[0]


def products(groups, shards, dtype):
    counts = [len(group) for group in groups]
    heights = [sum(x.shape[0] for x in group) for group in groups]
    xs = [x for group in groups for x in group]
    width = shards[0].shape[1]
    size = 8 * sum(heights) * xs[0].shape[1]
    return pl.pallas_call(
        lambda *refs: product_kernel(counts, *refs),
        out_shape=[jax.ShapeDtypeStruct((height, width), dtype) for height in heights],
        compiler_params=params(24),
        cost_estimate=cost(size * width, size),
        name="products",
    )(*xs, *shards)


def half_sum_kernel(held, arrived, own, onward):
    rows = own.shape[0]
    own[...] = held[:rows, :] + arrived[:rows, :].astype(jnp.float32)
    onward[...] = (held[rows:, :] + arrived[rows:, :].astype(jnp.float32)).astype(jnp.bfloat16)


def half_sum(held, arrived):
    rows, width = held.shape[0] // 2, held.shape[1]
    return pl.pallas_call(
        half_sum_kernel,
        out_shape=[
            jax.ShapeDtypeStruct((rows, width), jnp.float32),
            jax.ShapeDtypeStruct((rows, width), jnp.bfloat16),
        ],
        compiler_params=params(16),
        cost_estimate=cost(2 * held.size, 9 * held.size),
        name="half_sum",
    )(held, arrived)


def added(own, parts, cols):
    total = own[:, cols]
    for part in parts:
        total = total + part[:, cols].astype(jnp.float32)
    return total


def key_sum_kernel(cosine, sine_part, own, *refs):
    parts, out = refs[:-1], refs[-1]
    for h in range(out.shape[1] // HD):
        cols = slice(h * HD, (h + 1) * HD)
        total = added(own, parts, cols)
        turned = pltpu.roll(total, HD // 2, 1)
        out[:, cols] = (total * cosine[...] + turned * sine_part[...]).astype(jnp.bfloat16)


def value_sum_kernel(own, *refs):
    parts, out = refs[:-1], refs[-1]
    out[...] = added(own, parts, slice(None)).astype(jnp.bfloat16)


def block_sum(kernel, name, own, parts, *tables):
    return pl.pallas_call(
        kernel,
        out_shape=jax.ShapeDtypeStruct(own.shape, jnp.bfloat16),
        compiler_params=params(16),
        cost_estimate=cost(10 * own.size, 12 * own.size),
        name=name,
    )(*tables, own, *parts)


def score_kernel(odd_ref, q_ref, *refs):
    key_refs, (row_pos, col_pos, weights, sums, log_sums) = refs[:WINDOW], refs[WINDOW:]
    beside, two_back, before, own = key_refs
    odd = odd_ref[0] == 1
    tok_rows = q_ref.shape[2]
    visible = col_pos[0] <= row_pos[0]
    lane = lax.broadcasted_iota(jnp.int32, (tok_rows, LANES), 1)
    for k in range(KVH):
        cols = slice(k * HD, (k + 1) * HD)
        one_back = jnp.where(odd, before[:, cols], beside[:, cols])
        three_back = jnp.where(odd, beside[:, cols], before[:, cols])
        keys = jnp.concatenate([three_back, two_back[:, cols], one_back, own[:, cols]], axis=0)
        all_sums = jnp.ones((tok_rows, LANES), jnp.float32)
        all_max = jnp.zeros((tok_rows, LANES), jnp.float32)
        for h in range(GROUP):
            head = k * GROUP + h
            dots = lax.dot_general(
                q_ref[0, 0, :, head * HD : (head + 1) * HD],
                keys,
                (((1,), (1,)), ((), ())),
                preferred_element_type=jnp.float32,
            )
            dots = jnp.where(visible, dots, -jnp.inf)
            row_max = jnp.max(dots, axis=-1, keepdims=True)
            exps = jnp.exp2((dots - row_max) * (SCALE * LOG2_E))
            running = jnp.sum(exps, axis=-1, keepdims=True)
            weights[0, k, h * tok_rows : (h + 1) * tok_rows, :] = exps.astype(jnp.bfloat16)
            all_sums = jnp.where(lane == h, running, all_sums)
            all_max = jnp.where(lane == h, row_max, all_max)
        sums[0, k] = all_sums
        log_sums[0, k * GROUP : (k + 1) * GROUP, :] = jnp.transpose(
            all_max * SCALE + jnp.log(all_sums)
        )[:GROUP]


def scored(odd, queries, window, row_pos, col_pos):
    _, micro_count, tok_rows, width = queries.shape
    keys = WINDOW * tok_rows
    return pl.pallas_call(
        score_kernel,
        grid=(micro_count,),
        in_specs=[
            pl.BlockSpec(memory_space=pltpu.SMEM),
            pl.BlockSpec((1, 1, tok_rows, width), lambda m: (0, m, 0, 0)),
            *[pl.BlockSpec((tok_rows, KVH * HD), lambda m: (m, 0))] * WINDOW,
            pl.BlockSpec((1, tok_rows, 1), lambda m: (m, 0, 0)),
            pl.BlockSpec((1, 1, keys), lambda m: (m, 0, 0)),
        ],
        out_specs=[
            pl.BlockSpec((1, KVH, GROUP * tok_rows, keys), lambda m: (m, 0, 0, 0)),
            pl.BlockSpec((1, KVH, tok_rows, LANES), lambda m: (m, 0, 0, 0)),
            pl.BlockSpec((1, QH, tok_rows), lambda m: (m, 0, 0)),
        ],
        out_shape=[
            jax.ShapeDtypeStruct((micro_count, KVH, GROUP * tok_rows, keys), jnp.bfloat16),
            jax.ShapeDtypeStruct((micro_count, KVH, tok_rows, LANES), jnp.float32),
            jax.ShapeDtypeStruct((micro_count, QH, tok_rows), jnp.float32),
        ],
        compiler_params=params(32),
        cost_estimate=cost(2 * micro_count * QH * tok_rows * keys * HD, 8 * 2**20),
        name="scores",
    )(odd, queries, *window, row_pos, col_pos)


def mix_kernel(weights, sums, *refs):
    values = jnp.concatenate([ref[...] for ref in refs[:WINDOW]], axis=0)
    out = refs[WINDOW]
    tok_rows = out.shape[2]
    for k in range(KVH):
        mixed = jnp.dot(
            weights[0, k], values[:, k * HD : (k + 1) * HD], preferred_element_type=jnp.float32
        )
        share = 1.0 / sums[0, k]
        for h in range(GROUP):
            head = k * GROUP + h
            out[0, 0, :, head * HD : (head + 1) * HD] = (
                mixed[h * tok_rows : (h + 1) * tok_rows] * share[:, h : h + 1]
            ).astype(jnp.bfloat16)


def mixed_values(weights, sums, window):
    micro_count, _, group_rows, keys = weights.shape
    tok_rows = group_rows // GROUP
    return pl.pallas_call(
        mix_kernel,
        grid=(micro_count,),
        in_specs=[
            pl.BlockSpec((1, KVH, group_rows, keys), lambda m: (m, 0, 0, 0)),
            pl.BlockSpec((1, KVH, tok_rows, LANES), lambda m: (m, 0, 0, 0)),
            *[pl.BlockSpec((tok_rows, KVH * HD), lambda m: (m, 0))] * WINDOW,
        ],
        out_specs=pl.BlockSpec((1, 1, tok_rows, QH * HD), lambda m: (0, m, 0, 0)),
        out_shape=jax.ShapeDtypeStruct((1, micro_count, tok_rows, QH * HD), jnp.bfloat16),
        compiler_params=params(32),
        cost_estimate=cost(2 * micro_count * QH * tok_rows * keys * HD, 8 * 2**20),
        name="mixed_values",
    )(weights, sums, *window)


def on_device(handoff, norm_gain, kv_weight, queries, span_order):
    sections = lax.axis_size("section")
    cycle_size = lax.axis_size("ctx")
    own_index = lax.axis_index("ctx")
    quads = cycle_size // QUAD
    own_quad, own_place = own_index // QUAD, own_index % QUAD
    weight = kv_weight[0]
    shard_rows, kv_width = weight.shape[0], weight.shape[1] // 2
    _, micro_count, tok_rows, _ = handoff.shape

    next_gain = moved(norm_gain, "section", lambda i: i - 1).astype(jnp.float32)
    odd = own_index % 2
    quad_order = (own_quad - jnp.arange(quads, dtype=jnp.int32)) % quads * QUAD
    flips = jnp.arange(QUAD, dtype=jnp.int32)
    cut_starts = (quad_order[None, :] + (own_place ^ flips)[:, None]) * shard_rows
    cuts = normed_cuts(handoff[0], next_gain, cut_starts)

    def to_next_section(part, flip):
        route = [
            (s * cycle_size + i, (s + 1) % sections * cycle_size + (i ^ flip))
            for s in range(sections)
            for i in range(cycle_size)
        ]
        return lax.ppermute(part, ("section", "ctx"), route)

    def same_place(part):
        return [part] + [
            moved(part, "ctx", lambda i, j=j: i + QUAD * j) for j in range(1, quads)
        ]

    key_shards = same_place(weight[:, :kv_width])
    late_part, _ = lax.optimization_barrier((weight[:, kv_width:], key_shards[-1]))
    value_shards = same_place(late_part)

    late_cut, _ = lax.optimization_barrier((cuts[2], key_shards[-1]))
    first_cuts = [to_next_section(cuts[flip], flip) for flip in (1, 3)]
    held_cuts = [
        to_next_section(cuts[0], 0),
        to_next_section(late_cut[:tok_rows], 2),
        to_next_section(late_cut[tok_rows:], 2),
    ]

    def over_y(part):
        return moved(part, "ctx", lambda i: i ^ 1)

    def over_z(part):
        return moved(part, "ctx", lambda i: i ^ 2)

    def key_window_of(block, two_back):
        beside = over_y(two_back)
        onward = jnp.where(odd == 1, two_back, block)
        return [beside, two_back, moved(onward, "ctx", lambda i: i + 1), block]

    def value_window_of(block):
        one_back, two_back = [moved(block, "ctx", lambda i, d=d: i + d) for d in (1, 2)]
        return [moved(one_back, "ctx", lambda i: i + 2), two_back, one_back, block]

    span_len = tok_rows // 2
    places_of = span_order[:, :, None] * span_len + jnp.arange(span_len, dtype=jnp.int32)
    all_pos = places_of.reshape(micro_count, cycle_size * tok_rows)
    col_pos = lax.dynamic_slice_in_dim(
        jnp.concatenate([all_pos[:, -(WINDOW - 1) * tok_rows :], all_pos], axis=1),
        own_index * tok_rows,
        WINDOW * tok_rows,
        1,
    )
    own_pos = col_pos[:, -tok_rows:]
    half_dim = HD // 2
    frequency = rope_base ** (-2.0 * jnp.arange(half_dim, dtype=jnp.float32) / HD)
    angles = own_pos.reshape(-1, 1).astype(jnp.float32) * frequency
    cosine, sine_part = jnp.cos(angles), jnp.sin(angles)
    cosine = jnp.concatenate([cosine, cosine], axis=1)
    sine_part = jnp.concatenate([-sine_part, sine_part], axis=1)

    (key_products,) = products([first_cuts], key_shards, jnp.bfloat16)
    key_y = over_y(key_products)
    (key_held,) = products([held_cuts], key_shards, jnp.float32)
    own_keys, onward_keys = half_sum(key_held, key_y)
    key_z = over_z(onward_keys)
    value_shards, _ = lax.optimization_barrier((value_shards, onward_keys))
    value_products = products(
        [first_cuts[:1], held_cuts[1:], first_cuts[1:]], value_shards, jnp.bfloat16
    )
    key_block = block_sum(key_sum_kernel, "key_sum", own_keys, [key_z], cosine, sine_part)
    key_two_back = moved(key_block, "ctx", lambda i: i + 2)
    value_parts = [
        moved(part, "ctx", lambda i, flip=flip: i ^ flip)
        for flip, part in enumerate(value_products, start=1)
    ]
    (own_values,) = products([held_cuts[:1]], value_shards, jnp.float32)
    weights, sums, log_sums = scored(
        odd.astype(jnp.int32).reshape(1),
        queries,
        key_window_of(key_block, key_two_back),
        own_pos[:, :, None],
        col_pos[:, None, :],
    )
    value_block = block_sum(value_sum_kernel, "value_sum", own_values, value_parts)
    out = mixed_values(weights, sums, value_window_of(value_block))
    return (out, log_sums[None])


def solution(mesh):
    placed = (
        P("section", None, "ctx", None),
        P("section", None),
        P("section", "ctx", None),
        P("section", None, "ctx", None),
        P(),
    )
    return jax.shard_map(
        on_device,
        mesh=mesh,
        in_specs=placed,
        out_specs=(P("section", None, "ctx", None), P("section", None, None, "ctx")),
        check_vma=False,
    )
```

```python
import jax
import jax.numpy as jnp
from jax import lax
from jax.experimental import pallas as pl
from jax.experimental.pallas import tpu as pltpu
from jax.sharding import PartitionSpec as P

QH = 32
KVH = 4
HD = 128
WINDOW = 4
QUAD = 4
GROUP = QH // KVH
SCALE = HD**-0.5
LOG2_E = 1.4426950408889634
LANES = 128
ROW_STEP = 16


rope_base = 500000.0


def moved(block, axis, target):
    size = lax.axis_size(axis)
    return lax.ppermute(block, axis, [(i, target(i) % size) for i in range(size)])


def params(mib):
    return pltpu.CompilerParams(vmem_limit_bytes=mib * 1024 * 1024)


def cost(flops, bytes_accessed):
    return pl.CostEstimate(flops=flops, bytes_accessed=bytes_accessed, transcendentals=0)


def norm_kernel(starts_ref, x_ref, gain_ref, *outs):
    rows, width = x_ref.shape[1], x_ref.shape[2]
    pieces = starts_ref.shape[1]
    piece_width = outs[0].shape[1] // pieces
    for r in range(0, rows, ROW_STEP):
        x = x_ref[0, r : r + ROW_STEP, :].astype(jnp.float32)
        scale = lax.rsqrt(jnp.sum(x * x, axis=-1, keepdims=True) / width + 1e-05)
        for i, out in enumerate(outs):
            for j in range(pieces):
                start = pl.multiple_of(starts_ref[i, j], LANES)
                xs = x_ref[0, r : r + ROW_STEP, pl.ds(start, piece_width)].astype(jnp.float32)
                gain = gain_ref[:, pl.ds(start, piece_width)]
                out[r : r + ROW_STEP, j * piece_width : (j + 1) * piece_width] = (
                    xs * scale * gain
                ).astype(jnp.bfloat16)


def normed_cuts(activations, gain, starts):
    micro_count, tok_rows, width = activations.shape
    rows = micro_count * tok_rows
    cuts = starts.shape[0]
    part = width // cuts
    return pl.pallas_call(
        norm_kernel,
        grid=(micro_count,),
        in_specs=[
            pl.BlockSpec(memory_space=pltpu.SMEM),
            pl.BlockSpec((1, tok_rows, width), lambda m: (m, 0, 0)),
            pl.BlockSpec((1, width), lambda m: (0, 0)),
        ],
        out_specs=[pl.BlockSpec((tok_rows, part), lambda m: (m, 0))] * cuts,
        out_shape=[jax.ShapeDtypeStruct((rows, part), jnp.bfloat16)] * cuts,
        compiler_params=params(16),
        cost_estimate=cost(6 * rows * width, 4 * rows * width),
        name="norm_cuts",
    )(starts, activations, gain)


def product_kernel(counts, *refs):
    blocks = sum(counts)
    xs, shards, outs = list(refs[:blocks]), refs[blocks : -len(counts)], refs[-len(counts) :]
    shard_rows = shards[0].shape[0]
    for count, out in zip(counts, outs):
        first = 0
        for _ in range(count):
            x = xs.pop(0)
            total = 0.0
            for j, shard in enumerate(shards):
                total = total + jnp.dot(
                    x[:, j * shard_rows : (j + 1) * shard_rows],
                    shard[...],
                    preferred_element_type=jnp.float32,
                )
            out[first : first + x.shape[0], :] = total.astype(out.dtype)
            first += x.shape[0]


def products(groups, shards, dtype):
    counts = [len(group) for group in groups]
    heights = [sum(x.shape[0] for x in group) for group in groups]
    xs = [x for group in groups for x in group]
    width = shards[0].shape[1]
    size = 8 * sum(heights) * xs[0].shape[1]
    return pl.pallas_call(
        lambda *refs: product_kernel(counts, *refs),
        out_shape=[jax.ShapeDtypeStruct((height, width), dtype) for height in heights],
        compiler_params=params(24),
        cost_estimate=cost(size * width, size),
        name="products",
    )(*xs, *shards)


def half_sum_kernel(held, arrived, own, onward):
    rows = own.shape[0]
    own[...] = held[:rows, :] + arrived[:rows, :].astype(jnp.float32)
    onward[...] = (held[rows:, :] + arrived[rows:, :].astype(jnp.float32)).astype(jnp.bfloat16)


def half_sum(held, arrived):
    rows, width = held.shape[0] // 2, held.shape[1]
    return pl.pallas_call(
        half_sum_kernel,
        out_shape=[
            jax.ShapeDtypeStruct((rows, width), jnp.float32),
            jax.ShapeDtypeStruct((rows, width), jnp.bfloat16),
        ],
        compiler_params=params(16),
        cost_estimate=cost(2 * held.size, 9 * held.size),
        name="half_sum",
    )(held, arrived)


def added(own, parts, cols):
    total = own[:, cols]
    for part in parts:
        total = total + part[:, cols].astype(jnp.float32)
    return total


def key_sum_kernel(cosine, sine_part, own, *refs):
    parts, out = refs[:-1], refs[-1]
    for h in range(out.shape[1] // HD):
        cols = slice(h * HD, (h + 1) * HD)
        total = added(own, parts, cols)
        turned = pltpu.roll(total, HD // 2, 1)
        out[:, cols] = (total * cosine[...] + turned * sine_part[...]).astype(jnp.bfloat16)


def value_sum_kernel(own, *refs):
    parts, out = refs[:-1], refs[-1]
    out[...] = added(own, parts, slice(None)).astype(jnp.bfloat16)


def block_sum(kernel, name, own, parts, *tables):
    return pl.pallas_call(
        kernel,
        out_shape=jax.ShapeDtypeStruct(own.shape, jnp.bfloat16),
        compiler_params=params(16),
        cost_estimate=cost(10 * own.size, 12 * own.size),
        name=name,
    )(*tables, own, *parts)


def score_kernel(odd_ref, q_ref, *refs):
    key_refs, (row_pos, col_pos, weights, sums, log_sums) = refs[:WINDOW], refs[WINDOW:]
    beside, two_back, before, own = key_refs
    odd = odd_ref[0] == 1
    tok_rows = q_ref.shape[2]
    visible = col_pos[0] <= row_pos[0]
    lane = lax.broadcasted_iota(jnp.int32, (tok_rows, LANES), 1)
    for k in range(KVH):
        cols = slice(k * HD, (k + 1) * HD)
        one_back = jnp.where(odd, before[:, cols], beside[:, cols])
        three_back = jnp.where(odd, beside[:, cols], before[:, cols])
        keys = jnp.concatenate([three_back, two_back[:, cols], one_back, own[:, cols]], axis=0)
        all_sums = jnp.ones((tok_rows, LANES), jnp.float32)
        all_max = jnp.zeros((tok_rows, LANES), jnp.float32)
        for h in range(GROUP):
            head = k * GROUP + h
            dots = lax.dot_general(
                q_ref[0, 0, :, head * HD : (head + 1) * HD],
                keys,
                (((1,), (1,)), ((), ())),
                preferred_element_type=jnp.float32,
            )
            dots = jnp.where(visible, dots, -jnp.inf)
            row_max = jnp.max(dots, axis=-1, keepdims=True)
            exps = jnp.exp2((dots - row_max) * (SCALE * LOG2_E))
            running = jnp.sum(exps, axis=-1, keepdims=True)
            weights[0, k, h * tok_rows : (h + 1) * tok_rows, :] = exps.astype(jnp.bfloat16)
            all_sums = jnp.where(lane == h, running, all_sums)
            all_max = jnp.where(lane == h, row_max, all_max)
        sums[0, k] = all_sums
        log_sums[0, k * GROUP : (k + 1) * GROUP, :] = jnp.transpose(
            all_max * SCALE + jnp.log(all_sums)
        )[:GROUP]


def scored(odd, queries, window, row_pos, col_pos):
    _, micro_count, tok_rows, width = queries.shape
    keys = WINDOW * tok_rows
    return pl.pallas_call(
        score_kernel,
        grid=(micro_count,),
        in_specs=[
            pl.BlockSpec(memory_space=pltpu.SMEM),
            pl.BlockSpec((1, 1, tok_rows, width), lambda m: (0, m, 0, 0)),
            *[pl.BlockSpec((tok_rows, KVH * HD), lambda m: (m, 0))] * WINDOW,
            pl.BlockSpec((1, tok_rows, 1), lambda m: (m, 0, 0)),
            pl.BlockSpec((1, 1, keys), lambda m: (m, 0, 0)),
        ],
        out_specs=[
            pl.BlockSpec((1, KVH, GROUP * tok_rows, keys), lambda m: (m, 0, 0, 0)),
            pl.BlockSpec((1, KVH, tok_rows, LANES), lambda m: (m, 0, 0, 0)),
            pl.BlockSpec((1, QH, tok_rows), lambda m: (m, 0, 0)),
        ],
        out_shape=[
            jax.ShapeDtypeStruct((micro_count, KVH, GROUP * tok_rows, keys), jnp.bfloat16),
            jax.ShapeDtypeStruct((micro_count, KVH, tok_rows, LANES), jnp.float32),
            jax.ShapeDtypeStruct((micro_count, QH, tok_rows), jnp.float32),
        ],
        compiler_params=params(32),
        cost_estimate=cost(2 * micro_count * QH * tok_rows * keys * HD, 8 * 2**20),
        name="scores",
    )(odd, queries, *window, row_pos, col_pos)


def mix_kernel(weights, sums, *refs):
    values = jnp.concatenate([ref[...] for ref in refs[:WINDOW]], axis=0)
    out = refs[WINDOW]
    tok_rows = out.shape[2]
    for k in range(KVH):
        mixed = jnp.dot(
            weights[0, k], values[:, k * HD : (k + 1) * HD], preferred_element_type=jnp.float32
        )
        share = 1.0 / sums[0, k]
        for h in range(GROUP):
            head = k * GROUP + h
            out[0, 0, :, head * HD : (head + 1) * HD] = (
                mixed[h * tok_rows : (h + 1) * tok_rows] * share[:, h : h + 1]
            ).astype(jnp.bfloat16)


def mixed_values(weights, sums, window):
    micro_count, _, group_rows, keys = weights.shape
    tok_rows = group_rows // GROUP
    return pl.pallas_call(
        mix_kernel,
        grid=(micro_count,),
        in_specs=[
            pl.BlockSpec((1, KVH, group_rows, keys), lambda m: (m, 0, 0, 0)),
            pl.BlockSpec((1, KVH, tok_rows, LANES), lambda m: (m, 0, 0, 0)),
            *[pl.BlockSpec((tok_rows, KVH * HD), lambda m: (m, 0))] * WINDOW,
        ],
        out_specs=pl.BlockSpec((1, 1, tok_rows, QH * HD), lambda m: (0, m, 0, 0)),
        out_shape=jax.ShapeDtypeStruct((1, micro_count, tok_rows, QH * HD), jnp.bfloat16),
        compiler_params=params(32),
        cost_estimate=cost(2 * micro_count * QH * tok_rows * keys * HD, 8 * 2**20),
        name="mixed_values",
    )(weights, sums, *window)


def on_device(handoff, norm_gain, kv_weight, queries, span_order):
    sections = lax.axis_size("section")
    cycle_size = lax.axis_size("ctx")
    own_index = lax.axis_index("ctx")
    quads = cycle_size // QUAD
    own_quad, own_place = own_index // QUAD, own_index % QUAD
    weight = kv_weight[0]
    shard_rows, kv_width = weight.shape[0], weight.shape[1] // 2
    _, micro_count, tok_rows, _ = handoff.shape

    next_gain = moved(norm_gain, "section", lambda i: i - 1).astype(jnp.float32)
    odd = own_index % 2
    quad_order = (own_quad - jnp.arange(quads, dtype=jnp.int32)) % quads * QUAD
    flips = jnp.arange(QUAD, dtype=jnp.int32)
    cut_starts = (quad_order[None, :] + (own_place ^ flips)[:, None]) * shard_rows
    cuts = normed_cuts(handoff[0], next_gain, cut_starts)

    def to_next_section(part, flip):
        route = [
            (s * cycle_size + i, (s + 1) % sections * cycle_size + (i ^ flip))
            for s in range(sections)
            for i in range(cycle_size)
        ]
        return lax.ppermute(part, ("section", "ctx"), route)

    def same_place(part):
        return [part] + [
            moved(part, "ctx", lambda i, j=j: i + QUAD * j) for j in range(1, quads)
        ]

    key_shards = same_place(weight[:, :kv_width])
    late_part, _ = lax.optimization_barrier((weight[:, kv_width:], key_shards[-1]))
    value_shards = same_place(late_part)

    late_cut, _ = lax.optimization_barrier((cuts[2], key_shards[-1]))
    first_cuts = [to_next_section(cuts[flip], flip) for flip in (1, 3)]
    held_cuts = [
        to_next_section(cuts[0], 0),
        to_next_section(late_cut[:tok_rows], 2),
        to_next_section(late_cut[tok_rows:], 2),
    ]

    def over_y(part):
        return moved(part, "ctx", lambda i: i ^ 1)

    def over_z(part):
        return moved(part, "ctx", lambda i: i ^ 2)

    def key_window_of(block, two_back):
        beside = over_y(two_back)
        onward = jnp.where(odd == 1, two_back, block)
        return [beside, two_back, moved(onward, "ctx", lambda i: i + 1), block]

    def value_window_of(block):
        one_back, two_back = [moved(block, "ctx", lambda i, d=d: i + d) for d in (1, 2)]
        return [moved(one_back, "ctx", lambda i: i + 2), two_back, one_back, block]

    span_len = tok_rows // 2
    places_of = span_order[:, :, None] * span_len + jnp.arange(span_len, dtype=jnp.int32)
    all_pos = places_of.reshape(micro_count, cycle_size * tok_rows)
    col_pos = lax.dynamic_slice_in_dim(
        jnp.concatenate([all_pos[:, -(WINDOW - 1) * tok_rows :], all_pos], axis=1),
        own_index * tok_rows,
        WINDOW * tok_rows,
        1,
    )
    own_pos = col_pos[:, -tok_rows:]
    half_dim = HD // 2
    frequency = rope_base ** (-2.0 * jnp.arange(half_dim, dtype=jnp.float32) / HD)
    angles = own_pos.reshape(-1, 1).astype(jnp.float32) * frequency
    cosine, sine_part = jnp.cos(angles), jnp.sin(angles)
    cosine = jnp.concatenate([cosine, cosine], axis=1)
    sine_part = jnp.concatenate([-sine_part, sine_part], axis=1)

    (key_products,) = products([first_cuts], key_shards, jnp.bfloat16)
    key_y = over_y(key_products)
    (key_held,) = products([held_cuts], key_shards, jnp.float32)
    own_keys, onward_keys = half_sum(key_held, key_y)
    key_z = over_z(onward_keys)
    value_shards, _ = lax.optimization_barrier((value_shards, onward_keys))
    value_products = products(
        [held_cuts[1:], first_cuts[1:], first_cuts[:1]], value_shards, jnp.bfloat16
    )
    key_block = block_sum(key_sum_kernel, "key_sum", own_keys, [key_z], cosine, sine_part)
    key_two_back = moved(key_block, "ctx", lambda i: i + 2)
    value_parts = [
        moved(part, "ctx", lambda i, flip=flip: i ^ flip)
        for flip, part in zip((2, 3, 1), value_products)
    ]
    (own_values,) = products([held_cuts[:1]], value_shards, jnp.float32)
    weights, sums, log_sums = scored(
        odd.astype(jnp.int32).reshape(1),
        queries,
        key_window_of(key_block, key_two_back),
        own_pos[:, :, None],
        col_pos[:, None, :],
    )
    value_block = block_sum(value_sum_kernel, "value_sum", own_values, value_parts)
    out = mixed_values(weights, sums, value_window_of(value_block))
    return (out, log_sums[None])


def solution(mesh):
    placed = (
        P("section", None, "ctx", None),
        P("section", None),
        P("section", "ctx", None),
        P("section", None, "ctx", None),
        P(),
    )
    return jax.shard_map(
        on_device,
        mesh=mesh,
        in_specs=placed,
        out_specs=(P("section", None, "ctx", None), P("section", None, None, "ctx")),
        check_vma=False,
    )
```

```python
import jax
import jax.numpy as jnp
from jax import lax
from jax.experimental import pallas as pl
from jax.experimental.pallas import tpu as pltpu
from jax.sharding import PartitionSpec as P

QH = 32
KVH = 4
HD = 128
WINDOW = 4
QUAD = 4
GROUP = QH // KVH
SCALE = HD**-0.5
LOG2_E = 1.4426950408889634
LANES = 128
ROW_STEP = 16


rope_base = 500000.0


def moved(block, axis, target):
    size = lax.axis_size(axis)
    return lax.ppermute(block, axis, [(i, target(i) % size) for i in range(size)])


def params(mib):
    return pltpu.CompilerParams(vmem_limit_bytes=mib * 1024 * 1024)


def cost(flops, bytes_accessed):
    return pl.CostEstimate(flops=flops, bytes_accessed=bytes_accessed, transcendentals=0)


def norm_kernel(starts_ref, x_ref, gain_ref, *outs):
    rows, width = x_ref.shape[1], x_ref.shape[2]
    pieces = starts_ref.shape[1]
    piece_width = outs[0].shape[1] // pieces
    for r in range(0, rows, ROW_STEP):
        x = x_ref[0, r : r + ROW_STEP, :].astype(jnp.float32)
        scale = lax.rsqrt(jnp.sum(x * x, axis=-1, keepdims=True) / width + 1e-05)
        for i, out in enumerate(outs):
            for j in range(pieces):
                start = pl.multiple_of(starts_ref[i, j], LANES)
                xs = x_ref[0, r : r + ROW_STEP, pl.ds(start, piece_width)].astype(jnp.float32)
                gain = gain_ref[:, pl.ds(start, piece_width)]
                out[r : r + ROW_STEP, j * piece_width : (j + 1) * piece_width] = (
                    xs * scale * gain
                ).astype(jnp.bfloat16)


def normed_cuts(activations, gain, starts):
    micro_count, tok_rows, width = activations.shape
    rows = micro_count * tok_rows
    cuts = starts.shape[0]
    part = width // cuts
    return pl.pallas_call(
        norm_kernel,
        grid=(micro_count,),
        in_specs=[
            pl.BlockSpec(memory_space=pltpu.SMEM),
            pl.BlockSpec((1, tok_rows, width), lambda m: (m, 0, 0)),
            pl.BlockSpec((1, width), lambda m: (0, 0)),
        ],
        out_specs=[pl.BlockSpec((tok_rows, part), lambda m: (m, 0))] * cuts,
        out_shape=[jax.ShapeDtypeStruct((rows, part), jnp.bfloat16)] * cuts,
        compiler_params=params(16),
        cost_estimate=cost(6 * rows * width, 4 * rows * width),
        name="norm_cuts",
    )(starts, activations, gain)


def product_kernel(counts, *refs):
    blocks = sum(counts)
    xs, shards, outs = list(refs[:blocks]), refs[blocks : -len(counts)], refs[-len(counts) :]
    shard_rows = shards[0].shape[0]
    for count, out in zip(counts, outs):
        first = 0
        for _ in range(count):
            x = xs.pop(0)
            total = 0.0
            for j, shard in enumerate(shards):
                total = total + jnp.dot(
                    x[:, j * shard_rows : (j + 1) * shard_rows],
                    shard[...],
                    preferred_element_type=jnp.float32,
                )
            out[first : first + x.shape[0], :] = total.astype(out.dtype)
            first += x.shape[0]


def products(groups, shards, dtype):
    counts = [len(group) for group in groups]
    heights = [sum(x.shape[0] for x in group) for group in groups]
    xs = [x for group in groups for x in group]
    width = shards[0].shape[1]
    size = 8 * sum(heights) * xs[0].shape[1]
    return pl.pallas_call(
        lambda *refs: product_kernel(counts, *refs),
        out_shape=[jax.ShapeDtypeStruct((height, width), dtype) for height in heights],
        compiler_params=params(24),
        cost_estimate=cost(size * width, size),
        name="products",
    )(*xs, *shards)


def half_sum_kernel(held, arrived, own, onward):
    rows = own.shape[0]
    own[...] = held[:rows, :] + arrived[:rows, :].astype(jnp.float32)
    onward[...] = (held[rows:, :] + arrived[rows:, :].astype(jnp.float32)).astype(jnp.bfloat16)


def half_sum(held, arrived):
    rows, width = held.shape[0] // 2, held.shape[1]
    return pl.pallas_call(
        half_sum_kernel,
        out_shape=[
            jax.ShapeDtypeStruct((rows, width), jnp.float32),
            jax.ShapeDtypeStruct((rows, width), jnp.bfloat16),
        ],
        compiler_params=params(16),
        cost_estimate=cost(2 * held.size, 9 * held.size),
        name="half_sum",
    )(held, arrived)


def added(own, parts, cols):
    total = own[:, cols]
    for part in parts:
        total = total + part[:, cols].astype(jnp.float32)
    return total


def key_sum_kernel(cosine, sine_part, own, *refs):
    parts, out = refs[:-1], refs[-1]
    for h in range(out.shape[1] // HD):
        cols = slice(h * HD, (h + 1) * HD)
        total = added(own, parts, cols)
        turned = pltpu.roll(total, HD // 2, 1)
        out[:, cols] = (total * cosine[...] + turned * sine_part[...]).astype(jnp.bfloat16)


def value_sum_kernel(own, *refs):
    parts, out = refs[:-1], refs[-1]
    out[...] = added(own, parts, slice(None)).astype(jnp.bfloat16)


def block_sum(kernel, name, own, parts, *tables):
    return pl.pallas_call(
        kernel,
        out_shape=jax.ShapeDtypeStruct(own.shape, jnp.bfloat16),
        compiler_params=params(16),
        cost_estimate=cost(10 * own.size, 12 * own.size),
        name=name,
    )(*tables, own, *parts)


def score_kernel(odd_ref, q_ref, *refs):
    key_refs, (row_pos, col_pos, weights, sums, log_sums) = refs[:WINDOW], refs[WINDOW:]
    beside, two_back, before, own = key_refs
    odd = odd_ref[0] == 1
    tok_rows = q_ref.shape[2]
    visible = col_pos[0] <= row_pos[0]
    lane = lax.broadcasted_iota(jnp.int32, (tok_rows, LANES), 1)
    for k in range(KVH):
        cols = slice(k * HD, (k + 1) * HD)
        one_back = jnp.where(odd, before[:, cols], beside[:, cols])
        three_back = jnp.where(odd, beside[:, cols], before[:, cols])
        keys = jnp.concatenate([three_back, two_back[:, cols], one_back, own[:, cols]], axis=0)
        all_sums = jnp.ones((tok_rows, LANES), jnp.float32)
        all_max = jnp.zeros((tok_rows, LANES), jnp.float32)
        for h in range(GROUP):
            head = k * GROUP + h
            dots = lax.dot_general(
                q_ref[0, 0, :, head * HD : (head + 1) * HD],
                keys,
                (((1,), (1,)), ((), ())),
                preferred_element_type=jnp.float32,
            )
            dots = jnp.where(visible, dots, -jnp.inf)
            row_max = jnp.max(dots, axis=-1, keepdims=True)
            exps = jnp.exp2((dots - row_max) * (SCALE * LOG2_E))
            running = jnp.sum(exps, axis=-1, keepdims=True)
            weights[0, k, h * tok_rows : (h + 1) * tok_rows, :] = exps.astype(jnp.bfloat16)
            all_sums = jnp.where(lane == h, running, all_sums)
            all_max = jnp.where(lane == h, row_max, all_max)
        sums[0, k] = all_sums
        log_sums[0, k * GROUP : (k + 1) * GROUP, :] = jnp.transpose(
            all_max * SCALE + jnp.log(all_sums)
        )[:GROUP]


def scored(odd, queries, window, row_pos, col_pos):
    _, micro_count, tok_rows, width = queries.shape
    keys = WINDOW * tok_rows
    return pl.pallas_call(
        score_kernel,
        grid=(micro_count,),
        in_specs=[
            pl.BlockSpec(memory_space=pltpu.SMEM),
            pl.BlockSpec((1, 1, tok_rows, width), lambda m: (0, m, 0, 0)),
            *[pl.BlockSpec((tok_rows, KVH * HD), lambda m: (m, 0))] * WINDOW,
            pl.BlockSpec((1, tok_rows, 1), lambda m: (m, 0, 0)),
            pl.BlockSpec((1, 1, keys), lambda m: (m, 0, 0)),
        ],
        out_specs=[
            pl.BlockSpec((1, KVH, GROUP * tok_rows, keys), lambda m: (m, 0, 0, 0)),
            pl.BlockSpec((1, KVH, tok_rows, LANES), lambda m: (m, 0, 0, 0)),
            pl.BlockSpec((1, QH, tok_rows), lambda m: (m, 0, 0)),
        ],
        out_shape=[
            jax.ShapeDtypeStruct((micro_count, KVH, GROUP * tok_rows, keys), jnp.bfloat16),
            jax.ShapeDtypeStruct((micro_count, KVH, tok_rows, LANES), jnp.float32),
            jax.ShapeDtypeStruct((micro_count, QH, tok_rows), jnp.float32),
        ],
        compiler_params=params(32),
        cost_estimate=cost(2 * micro_count * QH * tok_rows * keys * HD, 8 * 2**20),
        name="scores",
    )(odd, queries, *window, row_pos, col_pos)


def mix_kernel(weights, sums, *refs):
    values = jnp.concatenate([ref[...] for ref in refs[:WINDOW]], axis=0)
    out = refs[WINDOW]
    tok_rows = out.shape[2]
    for k in range(KVH):
        mixed = jnp.dot(
            weights[0, k], values[:, k * HD : (k + 1) * HD], preferred_element_type=jnp.float32
        )
        share = 1.0 / sums[0, k]
        for h in range(GROUP):
            head = k * GROUP + h
            out[0, 0, :, head * HD : (head + 1) * HD] = (
                mixed[h * tok_rows : (h + 1) * tok_rows] * share[:, h : h + 1]
            ).astype(jnp.bfloat16)


def mixed_values(weights, sums, window):
    micro_count, _, group_rows, keys = weights.shape
    tok_rows = group_rows // GROUP
    return pl.pallas_call(
        mix_kernel,
        grid=(micro_count,),
        in_specs=[
            pl.BlockSpec((1, KVH, group_rows, keys), lambda m: (m, 0, 0, 0)),
            pl.BlockSpec((1, KVH, tok_rows, LANES), lambda m: (m, 0, 0, 0)),
            *[pl.BlockSpec((tok_rows, KVH * HD), lambda m: (m, 0))] * WINDOW,
        ],
        out_specs=pl.BlockSpec((1, 1, tok_rows, QH * HD), lambda m: (0, m, 0, 0)),
        out_shape=jax.ShapeDtypeStruct((1, micro_count, tok_rows, QH * HD), jnp.bfloat16),
        compiler_params=params(32),
        cost_estimate=cost(2 * micro_count * QH * tok_rows * keys * HD, 8 * 2**20),
        name="mixed_values",
    )(weights, sums, *window)


def on_device(handoff, norm_gain, kv_weight, queries, span_order):
    sections = lax.axis_size("section")
    cycle_size = lax.axis_size("ctx")
    own_index = lax.axis_index("ctx")
    quads = cycle_size // QUAD
    own_quad, own_place = own_index // QUAD, own_index % QUAD
    weight = kv_weight[0]
    shard_rows, kv_width = weight.shape[0], weight.shape[1] // 2
    _, micro_count, tok_rows, _ = handoff.shape

    next_gain = moved(norm_gain, "section", lambda i: i - 1).astype(jnp.float32)
    odd = own_index % 2
    quad_order = (own_quad - jnp.arange(quads, dtype=jnp.int32)) % quads * QUAD
    flips = jnp.arange(QUAD, dtype=jnp.int32)
    cut_starts = (quad_order[None, :] + (own_place ^ flips)[:, None]) * shard_rows
    cuts = normed_cuts(handoff[0], next_gain, cut_starts)

    def to_next_section(part, flip):
        route = [
            (s * cycle_size + i, (s + 1) % sections * cycle_size + (i ^ flip))
            for s in range(sections)
            for i in range(cycle_size)
        ]
        return lax.ppermute(part, ("section", "ctx"), route)

    def same_place(part):
        return [part] + [
            moved(part, "ctx", lambda i, j=j: i + QUAD * j) for j in range(1, quads)
        ]

    key_shards = same_place(weight[:, :kv_width])
    late_part, _ = lax.optimization_barrier((weight[:, kv_width:], key_shards[-1]))
    value_shards = same_place(late_part)

    late_cut, _ = lax.optimization_barrier((cuts[2], key_shards[-1]))
    first_cuts = [to_next_section(cuts[flip], flip) for flip in (1, 3)]
    held_cuts = [
        to_next_section(cuts[0], 0),
        to_next_section(late_cut[:tok_rows], 2),
        to_next_section(late_cut[tok_rows:], 2),
    ]

    def over_y(part):
        return moved(part, "ctx", lambda i: i ^ 1)

    def over_z(part):
        return moved(part, "ctx", lambda i: i ^ 2)

    def key_window_of(block, two_back):
        beside = over_y(two_back)
        onward = jnp.where(odd == 1, two_back, block)
        return [beside, two_back, moved(onward, "ctx", lambda i: i + 1), block]

    def value_window_of(block):
        one_back, two_back = [moved(block, "ctx", lambda i, d=d: i + d) for d in (1, 2)]
        return [moved(one_back, "ctx", lambda i: i + 2), two_back, one_back, block]

    span_len = tok_rows // 2
    places_of = span_order[:, :, None] * span_len + jnp.arange(span_len, dtype=jnp.int32)
    all_pos = places_of.reshape(micro_count, cycle_size * tok_rows)
    col_pos = lax.dynamic_slice_in_dim(
        jnp.concatenate([all_pos[:, -(WINDOW - 1) * tok_rows :], all_pos], axis=1),
        own_index * tok_rows,
        WINDOW * tok_rows,
        1,
    )
    own_pos = col_pos[:, -tok_rows:]
    half_dim = HD // 2
    frequency = rope_base ** (-2.0 * jnp.arange(half_dim, dtype=jnp.float32) / HD)
    angles = own_pos.reshape(-1, 1).astype(jnp.float32) * frequency
    cosine, sine_part = jnp.cos(angles), jnp.sin(angles)
    cosine = jnp.concatenate([cosine, cosine], axis=1)
    sine_part = jnp.concatenate([-sine_part, sine_part], axis=1)

    (key_products,) = products([first_cuts], key_shards, jnp.bfloat16)
    key_y = over_y(key_products)
    (key_held,) = products([held_cuts], key_shards, jnp.float32)
    own_keys, onward_keys = half_sum(key_held, key_y)
    key_z = over_z(onward_keys)
    value_shards, _ = lax.optimization_barrier((value_shards, onward_keys))
    value_products = products([held_cuts[1:], first_cuts[1:]], value_shards, jnp.bfloat16)
    key_block = block_sum(key_sum_kernel, "key_sum", own_keys, [key_z], cosine, sine_part)
    key_two_back = moved(key_block, "ctx", lambda i: i + 2)
    value_products += products([first_cuts[:1]], value_shards, jnp.bfloat16)
    value_parts = [
        moved(part, "ctx", lambda i, flip=flip: i ^ flip)
        for flip, part in zip((2, 3, 1), value_products)
    ]
    (own_values,) = products([held_cuts[:1]], value_shards, jnp.float32)
    weights, sums, log_sums = scored(
        odd.astype(jnp.int32).reshape(1),
        queries,
        key_window_of(key_block, key_two_back),
        own_pos[:, :, None],
        col_pos[:, None, :],
    )
    value_block = block_sum(value_sum_kernel, "value_sum", own_values, value_parts)
    out = mixed_values(weights, sums, value_window_of(value_block))
    return (out, log_sums[None])


def solution(mesh):
    placed = (
        P("section", None, "ctx", None),
        P("section", None),
        P("section", "ctx", None),
        P("section", None, "ctx", None),
        P(),
    )
    return jax.shard_map(
        on_device,
        mesh=mesh,
        in_specs=placed,
        out_specs=(P("section", None, "ctx", None), P("section", None, None, "ctx")),
        check_vma=False,
    )
```

```python
import jax
import jax.numpy as jnp
from jax import lax
from jax.experimental import pallas as pl
from jax.experimental.pallas import tpu as pltpu
from jax.sharding import PartitionSpec as P

QH = 32
KVH = 4
HD = 128
WINDOW = 4
QUAD = 4
GROUP = QH // KVH
SCALE = HD**-0.5
LOG2_E = 1.4426950408889634
LANES = 128
ROW_STEP = 16


rope_base = 500000.0


def moved(block, axis, target):
    size = lax.axis_size(axis)
    return lax.ppermute(block, axis, [(i, target(i) % size) for i in range(size)])


def params(mib):
    return pltpu.CompilerParams(vmem_limit_bytes=mib * 1024 * 1024)


def cost(flops, bytes_accessed):
    return pl.CostEstimate(flops=flops, bytes_accessed=bytes_accessed, transcendentals=0)


def norm_kernel(starts_ref, x_ref, gain_ref, *outs):
    rows, width = x_ref.shape[1], x_ref.shape[2]
    pieces = starts_ref.shape[1]
    piece_width = outs[0].shape[1] // pieces
    for r in range(0, rows, ROW_STEP):
        x = x_ref[0, r : r + ROW_STEP, :].astype(jnp.float32)
        scale = lax.rsqrt(jnp.sum(x * x, axis=-1, keepdims=True) / width + 1e-05)
        for i, out in enumerate(outs):
            for j in range(pieces):
                start = pl.multiple_of(starts_ref[i, j], LANES)
                xs = x_ref[0, r : r + ROW_STEP, pl.ds(start, piece_width)].astype(jnp.float32)
                gain = gain_ref[:, pl.ds(start, piece_width)]
                out[r : r + ROW_STEP, j * piece_width : (j + 1) * piece_width] = (
                    xs * scale * gain
                ).astype(jnp.bfloat16)


def normed_cuts(activations, gain, starts):
    micro_count, tok_rows, width = activations.shape
    rows = micro_count * tok_rows
    cuts = starts.shape[0]
    part = width // cuts
    return pl.pallas_call(
        norm_kernel,
        grid=(micro_count,),
        in_specs=[
            pl.BlockSpec(memory_space=pltpu.SMEM),
            pl.BlockSpec((1, tok_rows, width), lambda m: (m, 0, 0)),
            pl.BlockSpec((1, width), lambda m: (0, 0)),
        ],
        out_specs=[pl.BlockSpec((tok_rows, part), lambda m: (m, 0))] * cuts,
        out_shape=[jax.ShapeDtypeStruct((rows, part), jnp.bfloat16)] * cuts,
        compiler_params=params(16),
        cost_estimate=cost(6 * rows * width, 4 * rows * width),
        name="norm_cuts",
    )(starts, activations, gain)


def product_kernel(counts, *refs):
    blocks = sum(counts)
    xs, shards, outs = list(refs[:blocks]), refs[blocks : -len(counts)], refs[-len(counts) :]
    shard_rows = shards[0].shape[0]
    for count, out in zip(counts, outs):
        first = 0
        for _ in range(count):
            x = xs.pop(0)
            total = 0.0
            for j, shard in enumerate(shards):
                total = total + jnp.dot(
                    x[:, j * shard_rows : (j + 1) * shard_rows],
                    shard[...],
                    preferred_element_type=jnp.float32,
                )
            out[first : first + x.shape[0], :] = total.astype(out.dtype)
            first += x.shape[0]


def products(groups, shards, dtype):
    counts = [len(group) for group in groups]
    heights = [sum(x.shape[0] for x in group) for group in groups]
    xs = [x for group in groups for x in group]
    width = shards[0].shape[1]
    size = 8 * sum(heights) * xs[0].shape[1]
    return pl.pallas_call(
        lambda *refs: product_kernel(counts, *refs),
        out_shape=[jax.ShapeDtypeStruct((height, width), dtype) for height in heights],
        compiler_params=params(24),
        cost_estimate=cost(size * width, size),
        name="products",
    )(*xs, *shards)


def half_sum_kernel(held, arrived, own, onward):
    rows = own.shape[0]
    own[...] = held[:rows, :] + arrived[:rows, :].astype(jnp.float32)
    onward[...] = (held[rows:, :] + arrived[rows:, :].astype(jnp.float32)).astype(jnp.bfloat16)


def half_sum(held, arrived):
    rows, width = held.shape[0] // 2, held.shape[1]
    return pl.pallas_call(
        half_sum_kernel,
        out_shape=[
            jax.ShapeDtypeStruct((rows, width), jnp.float32),
            jax.ShapeDtypeStruct((rows, width), jnp.bfloat16),
        ],
        compiler_params=params(16),
        cost_estimate=cost(2 * held.size, 9 * held.size),
        name="half_sum",
    )(held, arrived)


def added(own, parts, cols):
    total = own[:, cols]
    for part in parts:
        total = total + part[:, cols].astype(jnp.float32)
    return total


def key_sum_kernel(cosine, sine_part, own, *refs):
    parts, out = refs[:-1], refs[-1]
    for h in range(out.shape[1] // HD):
        cols = slice(h * HD, (h + 1) * HD)
        total = added(own, parts, cols)
        turned = pltpu.roll(total, HD // 2, 1)
        out[:, cols] = (total * cosine[...] + turned * sine_part[...]).astype(jnp.bfloat16)


def value_sum_kernel(own, *refs):
    parts, out = refs[:-1], refs[-1]
    out[...] = added(own, parts, slice(None)).astype(jnp.bfloat16)


def block_sum(kernel, name, own, parts, *tables):
    return pl.pallas_call(
        kernel,
        out_shape=jax.ShapeDtypeStruct(own.shape, jnp.bfloat16),
        compiler_params=params(16),
        cost_estimate=cost(10 * own.size, 12 * own.size),
        name=name,
    )(*tables, own, *parts)


def score_kernel(odd_ref, q_ref, *refs):
    key_refs, (row_pos, col_pos, weights, sums, log_sums) = refs[:WINDOW], refs[WINDOW:]
    beside, two_back, before, own = key_refs
    odd = odd_ref[0] == 1
    tok_rows = q_ref.shape[2]
    visible = col_pos[0] <= row_pos[0]
    lane = lax.broadcasted_iota(jnp.int32, (tok_rows, LANES), 1)
    for k in range(KVH):
        cols = slice(k * HD, (k + 1) * HD)
        one_back = jnp.where(odd, before[:, cols], beside[:, cols])
        three_back = jnp.where(odd, beside[:, cols], before[:, cols])
        keys = jnp.concatenate([three_back, two_back[:, cols], one_back, own[:, cols]], axis=0)
        all_sums = jnp.ones((tok_rows, LANES), jnp.float32)
        all_max = jnp.zeros((tok_rows, LANES), jnp.float32)
        for h in range(GROUP):
            head = k * GROUP + h
            dots = lax.dot_general(
                q_ref[0, 0, :, head * HD : (head + 1) * HD],
                keys,
                (((1,), (1,)), ((), ())),
                preferred_element_type=jnp.float32,
            )
            dots = jnp.where(visible, dots, -jnp.inf)
            row_max = jnp.max(dots, axis=-1, keepdims=True)
            exps = jnp.exp2((dots - row_max) * (SCALE * LOG2_E))
            running = jnp.sum(exps, axis=-1, keepdims=True)
            weights[0, k, h * tok_rows : (h + 1) * tok_rows, :] = exps.astype(jnp.bfloat16)
            all_sums = jnp.where(lane == h, running, all_sums)
            all_max = jnp.where(lane == h, row_max, all_max)
        sums[0, k] = all_sums
        log_sums[0, k * GROUP : (k + 1) * GROUP, :] = jnp.transpose(
            all_max * SCALE + jnp.log(all_sums)
        )[:GROUP]


def scored(odd, queries, window, row_pos, col_pos):
    _, micro_count, tok_rows, width = queries.shape
    keys = WINDOW * tok_rows
    return pl.pallas_call(
        score_kernel,
        grid=(micro_count,),
        in_specs=[
            pl.BlockSpec(memory_space=pltpu.SMEM),
            pl.BlockSpec((1, 1, tok_rows, width), lambda m: (0, m, 0, 0)),
            *[pl.BlockSpec((tok_rows, KVH * HD), lambda m: (m, 0))] * WINDOW,
            pl.BlockSpec((1, tok_rows, 1), lambda m: (m, 0, 0)),
            pl.BlockSpec((1, 1, keys), lambda m: (m, 0, 0)),
        ],
        out_specs=[
            pl.BlockSpec((1, KVH, GROUP * tok_rows, keys), lambda m: (m, 0, 0, 0)),
            pl.BlockSpec((1, KVH, tok_rows, LANES), lambda m: (m, 0, 0, 0)),
            pl.BlockSpec((1, QH, tok_rows), lambda m: (m, 0, 0)),
        ],
        out_shape=[
            jax.ShapeDtypeStruct((micro_count, KVH, GROUP * tok_rows, keys), jnp.bfloat16),
            jax.ShapeDtypeStruct((micro_count, KVH, tok_rows, LANES), jnp.float32),
            jax.ShapeDtypeStruct((micro_count, QH, tok_rows), jnp.float32),
        ],
        compiler_params=params(32),
        cost_estimate=cost(2 * micro_count * QH * tok_rows * keys * HD, 8 * 2**20),
        name="scores",
    )(odd, queries, *window, row_pos, col_pos)


def mix_kernel(weights, sums, *refs):
    values = jnp.concatenate([ref[...] for ref in refs[:WINDOW]], axis=0)
    out = refs[WINDOW]
    tok_rows = out.shape[2]
    for k in range(KVH):
        mixed = jnp.dot(
            weights[0, k], values[:, k * HD : (k + 1) * HD], preferred_element_type=jnp.float32
        )
        share = 1.0 / sums[0, k]
        for h in range(GROUP):
            head = k * GROUP + h
            out[0, 0, :, head * HD : (head + 1) * HD] = (
                mixed[h * tok_rows : (h + 1) * tok_rows] * share[:, h : h + 1]
            ).astype(jnp.bfloat16)


def mixed_values(weights, sums, window):
    micro_count, _, group_rows, keys = weights.shape
    tok_rows = group_rows // GROUP
    return pl.pallas_call(
        mix_kernel,
        grid=(micro_count,),
        in_specs=[
            pl.BlockSpec((1, KVH, group_rows, keys), lambda m: (m, 0, 0, 0)),
            pl.BlockSpec((1, KVH, tok_rows, LANES), lambda m: (m, 0, 0, 0)),
            *[pl.BlockSpec((tok_rows, KVH * HD), lambda m: (m, 0))] * WINDOW,
        ],
        out_specs=pl.BlockSpec((1, 1, tok_rows, QH * HD), lambda m: (0, m, 0, 0)),
        out_shape=jax.ShapeDtypeStruct((1, micro_count, tok_rows, QH * HD), jnp.bfloat16),
        compiler_params=params(32),
        cost_estimate=cost(2 * micro_count * QH * tok_rows * keys * HD, 8 * 2**20),
        name="mixed_values",
    )(weights, sums, *window)


def on_device(handoff, norm_gain, kv_weight, queries, span_order):
    sections = lax.axis_size("section")
    cycle_size = lax.axis_size("ctx")
    own_index = lax.axis_index("ctx")
    quads = cycle_size // QUAD
    own_quad, own_place = own_index // QUAD, own_index % QUAD
    weight = kv_weight[0]
    shard_rows, kv_width = weight.shape[0], weight.shape[1] // 2
    _, micro_count, tok_rows, _ = handoff.shape

    next_gain = moved(norm_gain, "section", lambda i: i - 1).astype(jnp.float32)
    odd = own_index % 2
    quad_order = (own_quad - jnp.arange(quads, dtype=jnp.int32)) % quads * QUAD
    flips = jnp.arange(QUAD, dtype=jnp.int32)
    cut_starts = (quad_order[None, :] + (own_place ^ flips)[:, None]) * shard_rows
    cuts = normed_cuts(handoff[0], next_gain, cut_starts)

    def to_next_section(part, flip):
        route = [
            (s * cycle_size + i, (s + 1) % sections * cycle_size + (i ^ flip))
            for s in range(sections)
            for i in range(cycle_size)
        ]
        return lax.ppermute(part, ("section", "ctx"), route)

    def same_place(part):
        return [part] + [
            moved(part, "ctx", lambda i, j=j: i + QUAD * j) for j in range(1, quads)
        ]

    key_shards = same_place(weight[:, :kv_width])
    late_part, _ = lax.optimization_barrier((weight[:, kv_width:], key_shards[-1]))
    value_shards = same_place(late_part)

    late_cut, _ = lax.optimization_barrier((cuts[2], key_shards[-1]))
    first_cuts = [to_next_section(cuts[flip], flip) for flip in (1, 3)]
    held_cuts = [
        to_next_section(cuts[0], 0),
        to_next_section(late_cut[:tok_rows], 2),
        to_next_section(late_cut[tok_rows:], 2),
    ]

    def over_y(part):
        return moved(part, "ctx", lambda i: i ^ 1)

    def over_z(part):
        return moved(part, "ctx", lambda i: i ^ 2)

    def key_window_of(block, two_back):
        beside = over_y(two_back)
        onward = jnp.where(odd == 1, two_back, block)
        return [beside, two_back, moved(onward, "ctx", lambda i: i + 1), block]

    def value_window_of(block):
        one_back, two_back = [moved(block, "ctx", lambda i, d=d: i + d) for d in (1, 2)]
        return [moved(one_back, "ctx", lambda i: i + 2), two_back, one_back, block]

    span_len = tok_rows // 2
    places_of = span_order[:, :, None] * span_len + jnp.arange(span_len, dtype=jnp.int32)
    all_pos = places_of.reshape(micro_count, cycle_size * tok_rows)
    col_pos = lax.dynamic_slice_in_dim(
        jnp.concatenate([all_pos[:, -(WINDOW - 1) * tok_rows :], all_pos], axis=1),
        own_index * tok_rows,
        WINDOW * tok_rows,
        1,
    )
    own_pos = col_pos[:, -tok_rows:]
    half_dim = HD // 2
    frequency = rope_base ** (-2.0 * jnp.arange(half_dim, dtype=jnp.float32) / HD)
    angles = own_pos.reshape(-1, 1).astype(jnp.float32) * frequency
    cosine, sine_part = jnp.cos(angles), jnp.sin(angles)
    cosine = jnp.concatenate([cosine, cosine], axis=1)
    sine_part = jnp.concatenate([-sine_part, sine_part], axis=1)

    (key_products,) = products([first_cuts], key_shards, jnp.bfloat16)
    key_y = over_y(key_products)
    (key_held,) = products([held_cuts], key_shards, jnp.float32)
    own_keys, onward_keys = half_sum(key_held, key_y)
    key_z = over_z(onward_keys)
    value_shards, _ = lax.optimization_barrier((value_shards, onward_keys))
    value_products = products([held_cuts[1:], first_cuts[1:]], value_shards, jnp.bfloat16)
    key_block = block_sum(key_sum_kernel, "key_sum", own_keys, [key_z], cosine, sine_part)
    key_two_back = moved(key_block, "ctx", lambda i: i + 2)
    last_shards, _ = lax.optimization_barrier((value_shards, key_block))
    value_products += products([first_cuts[:1]], last_shards, jnp.bfloat16)
    value_parts = [
        moved(part, "ctx", lambda i, flip=flip: i ^ flip)
        for flip, part in zip((2, 3, 1), value_products)
    ]
    (own_values,) = products([held_cuts[:1]], value_shards, jnp.float32)
    weights, sums, log_sums = scored(
        odd.astype(jnp.int32).reshape(1),
        queries,
        key_window_of(key_block, key_two_back),
        own_pos[:, :, None],
        col_pos[:, None, :],
    )
    value_block = block_sum(value_sum_kernel, "value_sum", own_values, value_parts)
    out = mixed_values(weights, sums, value_window_of(value_block))
    return (out, log_sums[None])


def solution(mesh):
    placed = (
        P("section", None, "ctx", None),
        P("section", None),
        P("section", "ctx", None),
        P("section", None, "ctx", None),
        P(),
    )
    return jax.shard_map(
        on_device,
        mesh=mesh,
        in_specs=placed,
        out_specs=(P("section", None, "ctx", None), P("section", None, None, "ctx")),
        check_vma=False,
    )
```
